32 devices in a mesh: groups: 2 (over y), batch: 4 (over z), tensor: 4 (over x, core).
Axes of the slice: x: 2, y: 2, z: 4, core: 2. Of those that a mesh axis runs over, the one named last changes fastest.
Arguments:
- tokens: bfloat16 [6144, 8192], P(('groups', 'batch'), 'tensor'), parts along dimension 0, may hold values from -6 to 6
- request_adapter: int32 [6144], P(('groups', 'batch')), parts along dimension 0, may hold values from 0 to 31, as said below
- adapter_entry: int32 [32], replicated, may hold values from 0 to 31, each once
- key_value_weight: bfloat16 [8192, 1024], P('tensor'), may hold values from -0.0625 to 0.0625
- adapter_down: bfloat16 [32, 8192, 128], P('batch', 'tensor'), may hold values from -0.0625 to 0.0625
- adapter_up: bfloat16 [32, 64, 1024], P('batch', None, 'tensor'), may hold values from -0.75 to 0.75
Outputs:
- projected: bfloat16 [6144, 1024], P(('groups', 'batch'), 'tensor'), parts along dimension 0
The draws below stay inside these ranges and needn't reach their ends.
There are 2 independent parts, one for each index of `groups`. The reference program is written for one: setup_inputs(seed, part) draws one part's arguments, and reference() takes and returns one part's arrays. A program takes and returns all parts, laid end to end along the dimension named above; an argument that names none is the same for every part. Nothing has to cross between parts.
Inputs may be any that keep to these rules, and one draw needn't show every extreme that they name: `request_adapter`: on the rows of one device (aligned blocks of 768), one adapter appears exactly 48 times and every other at most 24 times; the adapter that appears 48 times is the same on every device of a group, and so is another one that appears exactly 24 times. `adapter_entry`: every entry once.
All inputs are finite; a program needn't handle non-finite values.
Results may differ from the reference program's by a relative error of at most 0.001.
Values may be sent and summed in bfloat16 or wider, within the bound.
No kernel may reach another device: no remote copies, remote signals or barrier semaphores. Data moves between devices by JAX's collectives and lax.ppermute only.
A program may use at most 64 MiB of HBM per device.

```python
import jax
import jax.numpy as jnp
from jax import lax

MODEL_WIDTH = 8192
ADAPTER_RANK = 64
KEY_VALUE_WIDTH = 1024
ADAPTER_COUNT = 32
TOK_DEV = 768
TOKENS = 3072
LIGHT = 24
HEAVY = 48
N_BATCH = 4


def draw_request_adapter(key, part):
    key = jax.random.fold_in(key, 11)
    blocks = TOKENS // TOK_DEV
    rest_rows = TOK_DEV - HEAVY
    places = (ADAPTER_COUNT - 1) * LIGHT
    pick_key, block_base = jax.random.split(key)
    pick_pair = jax.random.permutation(pick_key, ADAPTER_COUNT).astype(jnp.int32)
    hot_adapter = pick_pair[0]
    full_adapter = pick_pair[1]
    full_index = full_adapter - (full_adapter > hot_adapter).astype(jnp.int32)
    owner_index = jnp.arange(places, dtype=jnp.int32) // LIGHT

    def one_block(block_key):
        perm_key, shuffle_key = jax.random.split(block_key)
        scores = jax.random.permutation(perm_key, places).astype(jnp.int32)
        scores = jnp.where(owner_index == full_index, scores - places, scores)
        picked_rows = jnp.argsort(scores, stable=True)[:rest_rows]
        other_ids = owner_index[picked_rows]
        other_ids = other_ids + (other_ids >= hot_adapter).astype(jnp.int32)
        block_ids = jnp.concatenate([jnp.full((HEAVY,), hot_adapter, jnp.int32), other_ids.astype(jnp.int32)])
        return block_ids[jax.random.permutation(shuffle_key, TOK_DEV)]
    block_keys = jax.random.split(block_base, blocks)
    return jax.vmap(one_block)(block_keys).reshape(-1).astype(jnp.int32)


def shard_levels(rng, extent, pieces, smallest, high):
    def one(dim, blocks):
        draws = jax.random.uniform(jax.random.fold_in(jax.random.fold_in(rng, 6), dim), (blocks,), jnp.float32, smallest / len(pieces), high / len(pieces))
        return jnp.repeat(jnp.exp(draws), extent[dim] // blocks).reshape((-1,) + (1,) * (len(extent) - dim - 1))

    level = one(*pieces[0])
    for cut in pieces[1:]:
        level = level * one(*cut)
    return level


def centred(stream_key, shape, spread, most, cuts=(), kind=jnp.bfloat16):
    factor_of = shard_levels(stream_key, shape, cuts, -0.22, 0.18) if cuts else 1.0
    array = jax.random.normal(stream_key, shape, jnp.float32) * spread * factor_of
    return jnp.minimum(jnp.maximum(array, -most), most).astype(kind)


def setup_inputs(seed: int = 0, part: int = 0) -> dict:
    arg_keys = jax.random.split(jax.random.key(seed), 7)
    part_keys = jax.random.split(jax.random.fold_in(arg_keys[6], part), 7)
    tokens = centred(part_keys[0], (TOKENS, MODEL_WIDTH), 1.0, 6.0, ((0, 4), (1, 4)))
    request_adapter = draw_request_adapter(jax.random.fold_in(jax.random.fold_in(arg_keys[6], part), 71), part)
    adapter_entry = jax.random.permutation(arg_keys[2], ADAPTER_COUNT).astype(jnp.int32)
    key_value_weight = centred(arg_keys[3], (MODEL_WIDTH, KEY_VALUE_WIDTH), MODEL_WIDTH ** -0.5, 0.0625, ((0, 4),))
    adapter_down = centred(arg_keys[4], (ADAPTER_COUNT, MODEL_WIDTH, 2 * ADAPTER_RANK), MODEL_WIDTH ** -0.5, 0.0625, ((0, 4), (1, 4)))
    adapter_up = centred(arg_keys[5], (ADAPTER_COUNT, ADAPTER_RANK, KEY_VALUE_WIDTH), ADAPTER_RANK ** -0.5, 0.75, ((0, 4), (2, 4)))
    return dict(tokens=tokens, request_adapter=request_adapter, adapter_entry=adapter_entry, key_value_weight=key_value_weight, adapter_down=adapter_down, adapter_up=adapter_up)


adapter_scale = 0.5


def reference(tokens, request_adapter, adapter_entry, key_value_weight, adapter_down, adapter_up):
    row_total, feat_width = tokens.shape
    entry_count = adapter_down.shape[0]
    rank_columns = adapter_up.shape[1]
    value_start = key_value_weight.shape[1] // 2
    slot_span = N_BATCH * HEAVY
    base_product = jnp.dot(tokens, key_value_weight, preferred_element_type=jnp.float32)
    row_slot = jnp.take(adapter_entry, request_adapter).astype(jnp.int32)
    sorted_order = jnp.argsort(row_slot, stable=True).astype(jnp.int32)
    ordered = jnp.concatenate([jnp.take(tokens, sorted_order, axis=0), jnp.zeros((slot_span, feat_width), tokens.dtype)], axis=0)
    slot_range = jnp.arange(entry_count, dtype=jnp.int32)
    counts = jnp.sum((row_slot[None, :] == slot_range[:, None]).astype(jnp.int32), axis=1)
    starts = (jnp.cumsum(counts) - counts).astype(jnp.int32)
    start_positions = jnp.arange(slot_span, dtype=jnp.int32)

    def accumulate(running_total, entry_number):
        start_offset = starts[entry_number]
        entry_rows = lax.dynamic_slice_in_dim(ordered, start_offset, slot_span, 0)
        down_product = jnp.dot(entry_rows, adapter_down[entry_number], preferred_element_type=jnp.float32)
        second_factor = adapter_up[entry_number].astype(jnp.float32)
        key_projection = jnp.dot(down_product[:, :rank_columns], second_factor[:, :value_start], precision=lax.Precision.HIGHEST)
        value_projection = jnp.dot(down_product[:, rank_columns:], second_factor[:, value_start:], precision=lax.Precision.HIGHEST)
        adapter_delta = jnp.concatenate([key_projection, value_projection], axis=1)
        valid_mask = (start_positions < counts[entry_number])[:, None]
        running_total = running_total.at[start_offset + start_positions].add(jnp.where(valid_mask, adapter_delta, jnp.zeros_like(adapter_delta)))
        return running_total, None

    initial = jnp.zeros((row_total + slot_span, 2 * value_start), jnp.float32)
    combined_output, _ = lax.scan(accumulate, initial, slot_range)
    adapter_delta = jnp.zeros((row_total, 2 * value_start), jnp.float32).at[sorted_order].set(combined_output[:row_total])
    return (base_product + adapter_scale * adapter_delta).astype(jnp.bfloat16)
```

```python
import functools

import jax
import jax.numpy as jnp
from jax import lax
from jax.experimental import pallas as pl
from jax.experimental.pallas import tpu as pltpu
from jax.sharding import PartitionSpec as P

adapter_scale = 0.5
VMEM_BYTES = 48 * 1024 * 1024


def pack_kernel(homes, held, light, place_ref, request_ref, entry_ref, tokens_ref, *out_refs):
    index_ref, heavy_ref, block_refs = out_refs[0], out_refs[1], out_refs[2:]
    rows = tokens_ref.shape[0]
    adapters = entry_ref.shape[0]
    span = (held + 1) * light
    request = request_ref[...]
    onehot = lax.broadcasted_iota(jnp.int32, (adapters, rows), 0) == request
    earlier = lax.broadcasted_iota(jnp.int32, (rows, rows), 0) < lax.broadcasted_iota(
        jnp.int32, (rows, rows), 1
    )
    before = jnp.dot(
        onehot.astype(jnp.bfloat16), earlier.astype(jnp.bfloat16), preferred_element_type=jnp.float32
    )
    position = jnp.sum(jnp.where(onehot, before, 0.0), axis=0, keepdims=True).astype(jnp.int32)
    slot = jnp.sum(jnp.where(onehot, entry_ref[...], 0), axis=0, keepdims=True)
    home = slot // held
    relative = lax.rem(home - place_ref[0] + homes, homes)
    inside = jnp.where(
        position < light, (slot - home * held) * light + position, held * light + position - light
    )
    index = relative * span + inside
    index_ref[...] = index
    heavy = jnp.max(jnp.where(position >= light, slot, 0), axis=1, keepdims=True)
    heavy_ref[...] = jnp.broadcast_to(heavy, heavy_ref.shape)
    local = lax.broadcasted_iota(jnp.int32, (span, rows), 0)
    for r in range(homes):
        choose = (local + r * span == index).astype(jnp.bfloat16)
        block_refs[r][...] = jnp.dot(
            choose, tokens_ref[...], preferred_element_type=jnp.float32
        ).astype(jnp.bfloat16)


def pack(tokens, request_adapter, adapter_entry, place, homes, held, light):
    rows, width = tokens.shape
    span = (held + 1) * light
    vmem = pl.BlockSpec(memory_space=pltpu.VMEM)
    out = pl.pallas_call(
        functools.partial(pack_kernel, homes, held, light),
        out_shape=[
            jax.ShapeDtypeStruct((1, rows), jnp.int32),
            jax.ShapeDtypeStruct((8, 128), jnp.int32),
        ]
        + [jax.ShapeDtypeStruct((span, width), jnp.bfloat16)] * homes,
        in_specs=[pl.BlockSpec(memory_space=pltpu.SMEM), vmem, vmem, vmem],
        out_specs=[vmem] * (homes + 2),
        compiler_params=pltpu.CompilerParams(vmem_limit_bytes=VMEM_BYTES),
        name="pack",
    )(place.reshape(1), request_adapter.reshape(1, rows), adapter_entry.reshape(-1, 1), tokens)
    return out[0], out[1][0, 0], out[2:]


def split_pair(value):
    high = value.astype(jnp.bfloat16)
    low = (value - high.astype(jnp.float32)).astype(jnp.bfloat16)
    return high, low


def finish_kernel(homes, held, light, place_ref, index_ref, base_ref, up_ref, *refs):
    shrink_refs, out_ref, high_ref, low_ref = refs[:homes], refs[homes], refs[homes + 1], refs[homes + 2]
    span = (held + 1) * light
    rows = base_ref.shape[0]

    def expand(shrink, entry, start):
        high, low = split_pair(shrink)
        factor = up_ref[entry]
        delta = jnp.dot(high, factor, preferred_element_type=jnp.float32) + jnp.dot(
            low, factor, preferred_element_type=jnp.float32
        )
        high, low = split_pair(delta)
        high_ref[pl.ds(start, light), :] = high
        low_ref[pl.ds(start, light), :] = low

    heavy = place_ref[1]
    for r in range(homes):
        home = lax.rem(place_ref[0] + r, homes)
        for k in range(held):
            expand(shrink_refs[r][k * light : (k + 1) * light, :], home * held + k, r * span + k * light)
        expand(shrink_refs[r][held * light :, :], heavy, r * span + held * light)
    choose = (
        lax.broadcasted_iota(jnp.int32, (rows, homes * span), 1) == index_ref[...]
    ).astype(jnp.bfloat16)
    delta = jnp.dot(choose, high_ref[...], preferred_element_type=jnp.float32) + jnp.dot(
        choose, low_ref[...], preferred_element_type=jnp.float32
    )
    out_ref[...] = (base_ref[...] + adapter_scale * delta).astype(jnp.bfloat16)


def finish(place, heavy, index, base, up, shrinks, homes, held, light):
    rows, columns = base.shape
    span = (held + 1) * light
    vmem = pl.BlockSpec(memory_space=pltpu.VMEM)
    return pl.pallas_call(
        functools.partial(finish_kernel, homes, held, light),
        out_shape=jax.ShapeDtypeStruct((rows, columns), jnp.bfloat16),
        in_specs=[pl.BlockSpec(memory_space=pltpu.SMEM)] + [vmem] * (3 + homes),
        out_specs=vmem,
        scratch_shapes=[pltpu.VMEM((homes * span, columns), jnp.bfloat16)] * 2,
        compiler_params=pltpu.CompilerParams(vmem_limit_bytes=VMEM_BYTES),
        name="finish",
    )(jnp.stack([place, heavy]), index.reshape(rows, 1), base, up, *shrinks)


def on_device(tokens, request_adapter, adapter_entry, key_value_weight, adapter_down, adapter_up):
    rows, width = tokens.shape
    adapters = adapter_entry.shape[0]
    held, rank, columns = adapter_up.shape
    value_start = key_value_weight.shape[1] // 2
    homes = lax.axis_size("batch")
    pieces = lax.axis_size("tensor")
    place = lax.axis_index("batch").astype(jnp.int32)
    piece = lax.axis_index("tensor").astype(jnp.int32)
    light = rows // adapters

    index, heavy, blocks = pack(tokens, request_adapter, adapter_entry, place, homes, held, light)
    arrived = [blocks[0]] + [
        lax.ppermute(blocks[r], "batch", [(i, (i + r) % homes) for i in range(homes)])
        for r in range(1, homes)
    ]
    up = lax.all_gather(adapter_up, "batch", axis=0, tiled=True)
    partial = jnp.dot(tokens, key_value_weight, preferred_element_type=jnp.float32)
    base = lax.psum_scatter(partial, "tensor", scatter_dimension=1, tiled=True)

    heavy_here = heavy // held == place
    heavy_factor = lax.dynamic_index_in_dim(
        adapter_down, lax.rem(heavy, held), axis=0, keepdims=False
    )

    def half_of(value, other):
        return jnp.where(other * columns >= value_start, value[:, rank:], value[:, :rank])

    shrinks = []
    for r in range(homes):
        block = arrived[r]
        ordinary = jnp.einsum(
            "jcd,jdr->jcr",
            block[: held * light].reshape(held, light, width),
            adapter_down,
            preferred_element_type=jnp.float32,
        ).reshape(held * light, 2 * rank)
        extra = jnp.dot(block[held * light :], heavy_factor, preferred_element_type=jnp.float32)
        value = jnp.concatenate([ordinary, jnp.where(heavy_here, extra, 0.0)], axis=0)
        total = half_of(value, piece)
        for o in range(1, pieces):
            total = total + lax.ppermute(
                half_of(value, piece ^ o), "tensor", [(i, i ^ o) for i in range(pieces)]
            )
        if r:
            total = lax.ppermute(total, "batch", [(i, (i - r) % homes) for i in range(homes)])
        shrinks.append(total)
    return finish(place, heavy, index, base, up, shrinks, homes, held, light)


def solution(mesh):
    in_specs = (
        P(("groups", "batch"), "tensor"),
        P(("groups", "batch")),
        P(),
        P("tensor", None),
        P("batch", "tensor", None),
        P("batch", None, "tensor"),
    )
    out_specs = P(("groups", "batch"), "tensor")
    return jax.shard_map(
        on_device, mesh=mesh, in_specs=in_specs, out_specs=out_specs, check_vma=False
    )
```

```python
import functools

import jax
import jax.numpy as jnp
from jax import lax
from jax.experimental import pallas as pl
from jax.experimental.pallas import tpu as pltpu
from jax.sharding import PartitionSpec as P

adapter_scale = 0.5
VMEM_BYTES = 24 * 1024 * 1024
VMEM = pl.BlockSpec(memory_space=pltpu.VMEM)
SMEM = pl.BlockSpec(memory_space=pltpu.SMEM)
PARAMS = pltpu.CompilerParams(vmem_limit_bytes=VMEM_BYTES)


def place_rows(index, start, tokens_ref, block_ref):
    local = lax.broadcasted_iota(jnp.int32, (block_ref.shape[0], index.shape[1]), 0)
    choose = (local + start == index).astype(jnp.bfloat16)
    block_ref[...] = jnp.dot(
        choose, tokens_ref[...], preferred_element_type=jnp.float32
    ).astype(jnp.bfloat16)


def route_kernel(
    homes, held, light, shift, place_ref, request_ref, entry_ref, tokens_ref, index_ref, heavy_ref, block_ref
):
    rows = tokens_ref.shape[0]
    adapters = entry_ref.shape[0]
    span = (held + 1) * light
    onehot = lax.broadcasted_iota(jnp.int32, (adapters, rows), 0) == request_ref[...]
    earlier = lax.broadcasted_iota(jnp.int32, (rows, rows), 0) < lax.broadcasted_iota(
        jnp.int32, (rows, rows), 1
    )
    before = jnp.dot(
        onehot.astype(jnp.bfloat16), earlier.astype(jnp.bfloat16), preferred_element_type=jnp.float32
    )
    position = jnp.sum(jnp.where(onehot, before, 0.0), axis=0, keepdims=True).astype(jnp.int32)
    slot = jnp.sum(jnp.where(onehot, entry_ref[...], 0), axis=0, keepdims=True)
    home = slot // held
    relative = lax.rem(home - place_ref[0] + homes, homes)
    inside = jnp.where(
        position < light, (slot - home * held) * light + position, held * light + position - light
    )
    index = relative * span + inside
    index_ref[...] = index
    heavy = jnp.max(jnp.where(position >= light, slot, 0), axis=1, keepdims=True)
    heavy_ref[...] = jnp.broadcast_to(heavy, heavy_ref.shape)
    place_rows(index, shift * span, tokens_ref, block_ref)


def pack_kernel(span, shifts, index_ref, tokens_ref, *block_refs):
    for shift, block_ref in zip(shifts, block_refs):
        place_rows(index_ref[...], shift * span, tokens_ref, block_ref)


def entry_places(held):
    return (held + 2) // 2


def shrink_kernel(held, light, rank, pieces, value_side, scalar_ref, block_ref, down_ref, *out_refs):
    groups = entry_places(held)

    def product(e):
        if e > held:
            return jnp.zeros((light, 2 * rank), jnp.float32)
        factor = down_ref[e] if e < held else down_ref[scalar_ref[1]]
        value = jnp.dot(
            block_ref[e * light : (e + 1) * light, :], factor, preferred_element_type=jnp.float32
        )
        return value if e < held else jnp.where(scalar_ref[2] == 1, value, 0.0)

    piece = scalar_ref[0]
    for g in range(groups):
        first, second = product(g), product(g + groups)
        key = jnp.concatenate([first[:, :rank], second[:, :rank]], axis=1)
        value = jnp.concatenate([first[:, rank:], second[:, rank:]], axis=1)
        for o in range(pieces):
            out_refs[o][g * light : (g + 1) * light, :] = jnp.where(
                (piece ^ o) >= value_side, value, key
            )


def split_pair(value):
    high = value.astype(jnp.bfloat16)
    low = (value - high.astype(jnp.float32)).astype(jnp.bfloat16)
    return high, low


def finish_kernel(homes, held, light, rank, shifts, place_ref, index_ref, base_ref, up_ref, *refs):
    count = len(shifts)
    shrink_refs, out_ref, high_ref, low_ref = refs[:count], refs[count], refs[count + 1], refs[count + 2]
    span = (held + 1) * light
    rows = base_ref.shape[0]
    groups = entry_places(held)
    local = []
    for n, r in enumerate(shifts):
        home = lax.rem(place_ref[0] + r, homes)
        for e in range(held + 1):
            entry = home * held + e if e < held else place_ref[1]
            g, side = e % groups, e // groups
            high, low = split_pair(
                shrink_refs[n][g * light : (g + 1) * light, side * rank : (side + 1) * rank]
            )
            factor = up_ref[entry]
            delta = jnp.dot(high, factor, preferred_element_type=jnp.float32) + jnp.dot(
                low, factor, preferred_element_type=jnp.float32
            )
            high, low = split_pair(delta)
            start = n * span + e * light
            high_ref[start : start + light, :] = high
            low_ref[start : start + light, :] = low
        local.append(lax.broadcasted_iota(jnp.int32, (rows, span), 1) + r * span == index_ref[...])
    delta = base_ref[...]
    for n in range(count):
        choose = local[n].astype(jnp.bfloat16)
        delta = delta + adapter_scale * (
            jnp.dot(choose, high_ref[n * span : (n + 1) * span, :], preferred_element_type=jnp.float32)
            + jnp.dot(choose, low_ref[n * span : (n + 1) * span, :], preferred_element_type=jnp.float32)
        )
    out_ref[...] = delta.astype(out_ref.dtype)


def finish(scalars, index, base, up, shrinks, shifts, dtype, homes, held, light):
    rows, columns = base.shape
    span = (held + 1) * light
    return pl.pallas_call(
        functools.partial(finish_kernel, homes, held, light, up.shape[1], shifts),
        out_shape=jax.ShapeDtypeStruct((rows, columns), dtype),
        in_specs=[SMEM] + [VMEM] * (3 + len(shifts)),
        out_specs=VMEM,
        scratch_shapes=[pltpu.VMEM((len(shifts) * span, columns), jnp.bfloat16)] * 2,
        compiler_params=PARAMS,
        name="finish",
    )(scalars, index, base, up, *shrinks)


def line_gather(value, axis):
    size = lax.axis_size(axis)
    found = {0: value}
    for step in (1, -1):
        moving = value
        for hop in range(1, size):
            pairs = [(i, i + step) for i in range(size) if 0 <= i + step < size and 0 <= i - step * (hop - 1) < size]
            moving = lax.ppermute(moving, axis, pairs)
            found[-step * hop] = moving
    return found


def gather_up(adapter_up, place, homes):
    teams = lax.axis_size("groups")
    held, rank, columns = adapter_up.shape
    share = rank // teams
    team = lax.axis_index("groups")
    found = line_gather(lax.dynamic_slice_in_dim(adapter_up, team * share, share, 1), "batch")
    ordered = jnp.concatenate(
        [
            functools.reduce(
                lambda kept, hop: jnp.where(place + hop == home, found[hop], kept),
                sorted(found),
                jnp.zeros_like(found[0]),
            )
            for home in range(homes)
        ],
        axis=0,
    )
    shares = [ordered] + [
        lax.ppermute(ordered, "groups", [(i, (i + s) % teams) for i in range(teams)])
        for s in range(1, teams)
    ]
    return jnp.concatenate(
        [
            functools.reduce(
                lambda kept, s: jnp.where(lax.rem(team + teams - s, teams) == part, shares[s], kept),
                range(1, teams),
                shares[0],
            )
            for part in range(teams)
        ],
        axis=1,
    )


def reduce_base(tokens, weight, piece, pieces, columns):
    rows, width = tokens.shape
    bit = 1
    blocks = weight.reshape(width, pieces // 2, 2, columns)
    own = piece & 1

    def part(side):
        chosen = lax.dynamic_index_in_dim(blocks, side, axis=2, keepdims=False)
        return jnp.dot(
            tokens, chosen.reshape(width, pieces // 2 * columns), preferred_element_type=jnp.float32
        )

    sent = part(1 - own)
    kept = part(own) + lax.ppermute(sent, "tensor", [(i, i ^ 1) for i in range(pieces)])
    while 2 * bit < pieces:
        bit *= 2
        own = (piece // bit) & 1
        view = kept.reshape(rows, -1, 2, columns)
        sent = lax.dynamic_index_in_dim(view, 1 - own, axis=2, keepdims=False).reshape(rows, -1)
        kept = lax.dynamic_index_in_dim(view, own, axis=2, keepdims=False).reshape(rows, -1)
        kept = kept + lax.ppermute(sent, "tensor", [(i, i ^ bit) for i in range(pieces)])
    return kept


def on_device(tokens, request_adapter, adapter_entry, key_value_weight, adapter_down, adapter_up):
    rows, width = tokens.shape
    adapters = adapter_entry.shape[0]
    held, rank, columns = adapter_up.shape
    value_side = key_value_weight.shape[1] // 2 // columns
    homes = lax.axis_size("batch")
    pieces = lax.axis_size("tensor")
    place = lax.axis_index("batch").astype(jnp.int32)
    piece = lax.axis_index("tensor").astype(jnp.int32)
    light = rows // adapters
    span = (held + 1) * light
    order = sorted(range(1, homes), key=lambda r: (-min(r, homes - r), r))
    block_shape = jax.ShapeDtypeStruct((span, width), jnp.bfloat16)

    index, heavy, first = pl.pallas_call(
        functools.partial(route_kernel, homes, held, light, order[0]),
        out_shape=[
            jax.ShapeDtypeStruct((1, rows), jnp.int32),
            jax.ShapeDtypeStruct((8, 128), jnp.int32),
            block_shape,
        ],
        in_specs=[SMEM, VMEM, VMEM, VMEM],
        out_specs=[VMEM] * 3,
        compiler_params=PARAMS,
        name="route",
    )(place.reshape(1), request_adapter.reshape(1, rows), adapter_entry.reshape(-1, 1), tokens)
    later = order[1:] + [0]
    rest = pl.pallas_call(
        functools.partial(pack_kernel, span, later),
        out_shape=[block_shape] * len(later),
        in_specs=[VMEM] * 2,
        out_specs=[VMEM] * len(later),
        compiler_params=PARAMS,
        name="pack",
    )(index, tokens)
    blocks = {order[0]: first, **dict(zip(later, rest))}

    arrived = {0: blocks[0]}
    for r in order:
        arrived[r] = lax.ppermute(blocks[r], "batch", [(i, (i + r) % homes) for i in range(homes)])
    up = gather_up(adapter_up, place, homes)
    held_tokens, _ = lax.optimization_barrier((tokens, rest))
    base = reduce_base(held_tokens, key_value_weight, piece, pieces, columns)

    heavy = heavy[0, 0]
    heavy_here = (heavy // held == place).astype(jnp.int32)
    scalars = jnp.stack([piece, lax.rem(heavy, held), heavy_here])
    shrinks = {}
    for r in [0] + order:
        parts = pl.pallas_call(
            functools.partial(shrink_kernel, held, light, rank, pieces, value_side),
            out_shape=[jax.ShapeDtypeStruct((entry_places(held) * light, 2 * rank), jnp.float32)] * pieces,
            in_specs=[SMEM, VMEM, VMEM],
            out_specs=[VMEM] * pieces,
            compiler_params=PARAMS,
            name="shrink",
        )(scalars, arrived[r], adapter_down)
        total = parts[0]
        for o in range(1, pieces):
            total = total + lax.ppermute(parts[o], "tensor", [(i, i ^ o) for i in range(pieces)])
        if r:
            total = lax.ppermute(total, "batch", [(i, (i - r) % homes) for i in range(homes)])
        shrinks[r] = total

    places = jnp.stack([place, heavy])
    column = index.reshape(rows, 1)
    early = [0] + order[:-1]
    running = finish(
        places, column, base, up, [shrinks[r] for r in early], early, jnp.float32, homes, held, light
    )
    return finish(
        places, column, running, up, [shrinks[order[-1]]], order[-1:], jnp.bfloat16, homes, held, light
    )


def solution(mesh):
    in_specs = (
        P(("groups", "batch"), "tensor"),
        P(("groups", "batch")),
        P(),
        P("tensor", None),
        P("batch", "tensor", None),
        P("batch", None, "tensor"),
    )
    out_specs = P(("groups", "batch"), "tensor")
    return jax.shard_map(
        on_device, mesh=mesh, in_specs=in_specs, out_specs=out_specs, check_vma=False
    )
```

```python
import functools

import jax
import jax.numpy as jnp
from jax import lax
from jax.experimental import pallas as pl
from jax.experimental.pallas import tpu as pltpu
from jax.sharding import PartitionSpec as P

adapter_scale = 0.5
VMEM_BYTES = 24 * 1024 * 1024
VMEM = pl.BlockSpec(memory_space=pltpu.VMEM)
ANY = pl.BlockSpec(memory_space=pl.ANY)
SMEM = pl.BlockSpec(memory_space=pltpu.SMEM)
PARAMS = pltpu.CompilerParams(vmem_limit_bytes=VMEM_BYTES)


def place_rows(index, start, tokens_ref, block_ref):
    local = lax.broadcasted_iota(jnp.int32, (block_ref.shape[0], index.shape[1]), 0)
    choose = (local + start == index).astype(jnp.bfloat16)
    block_ref[...] = jnp.dot(
        choose, tokens_ref[...], preferred_element_type=jnp.float32
    ).astype(jnp.bfloat16)


def route_kernel(
    homes, held, light, shift, place_ref, entry_ref, request_ref, tokens_ref, index_ref, heavy_ref, block_ref
):
    rows = tokens_ref.shape[0]
    adapters = entry_ref.shape[0]
    span = (held + 1) * light
    onehot = lax.broadcasted_iota(jnp.int32, (adapters, rows), 0) == request_ref[...]
    earlier = lax.broadcasted_iota(jnp.int32, (rows, rows), 0) < lax.broadcasted_iota(
        jnp.int32, (rows, rows), 1
    )
    before = jnp.dot(
        onehot.astype(jnp.bfloat16), earlier.astype(jnp.bfloat16), preferred_element_type=jnp.float32
    )
    position = jnp.sum(jnp.where(onehot, before, 0.0), axis=0, keepdims=True).astype(jnp.int32)
    slot = jnp.zeros_like(position)
    for a in range(adapters):
        slot = jnp.where(request_ref[...] == a, entry_ref[a], slot)
    home = slot // held
    relative = lax.rem(home - place_ref[0] + homes, homes)
    inside = jnp.where(
        position < light, (slot - home * held) * light + position, held * light + position - light
    )
    index = relative * span + inside
    index_ref[...] = index
    heavy = jnp.max(jnp.where(position >= light, slot, 0), axis=1, keepdims=True)
    heavy_ref[...] = jnp.broadcast_to(heavy, heavy_ref.shape)
    place_rows(index, shift * span, tokens_ref, block_ref)


def pack_kernel(span, shifts, waited, index_ref, tokens_ref, *refs):
    block_refs = refs[waited:]
    for shift, block_ref in zip(shifts, block_refs):
        place_rows(index_ref[...], shift * span, tokens_ref, block_ref)


def entry_places(held):
    return (held + 2) // 2


def shrink_kernel(held, light, rank, pieces, value_side, waited, scalar_ref, block_ref, down_ref, *refs):
    out_refs = refs[waited:]
    groups = entry_places(held)

    def product(e):
        if e > held:
            return jnp.zeros((light, 2 * rank), jnp.float32)
        factor = down_ref[e] if e < held else down_ref[scalar_ref[1]]
        value = jnp.dot(
            block_ref[e * light : (e + 1) * light, :], factor, preferred_element_type=jnp.float32
        )
        return value if e < held else jnp.where(scalar_ref[2] == 1, value, 0.0)

    piece = scalar_ref[0]
    for g in range(groups):
        first, second = product(g), product(g + groups)
        key = jnp.concatenate([first[:, :rank], second[:, :rank]], axis=1)
        value = jnp.concatenate([first[:, rank:], second[:, rank:]], axis=1)
        for o in range(pieces):
            out_refs[o][g * light : (g + 1) * light, :] = jnp.where(
                (piece ^ o) >= value_side, value, key
            )


def split_pair(value):
    high = value.astype(jnp.bfloat16)
    low = (value - high.astype(jnp.float32)).astype(jnp.bfloat16)
    return high, low


def finish_kernel(homes, held, light, rank, shifts, waited, place_ref, index_ref, base_ref, up_ref, *refs):
    count = len(shifts)
    refs = refs[:count] + refs[count + waited :]
    shrink_refs, out_ref, high_ref, low_ref = refs[:count], refs[count], refs[count + 1], refs[count + 2]
    span = (held + 1) * light
    rows = base_ref.shape[0]
    groups = entry_places(held)
    local = []
    for n, r in enumerate(shifts):
        home = lax.rem(place_ref[0] + r, homes)
        for e in range(held + 1):
            entry = home * held + e if e < held else place_ref[1]
            g, side = e % groups, e // groups
            high, low = split_pair(
                shrink_refs[n][g * light : (g + 1) * light, side * rank : (side + 1) * rank]
            )
            factor = up_ref[entry]
            delta = jnp.dot(high, factor, preferred_element_type=jnp.float32) + jnp.dot(
                low, factor, preferred_element_type=jnp.float32
            )
            high, low = split_pair(delta)
            start = n * span + e * light
            high_ref[start : start + light, :] = high
            low_ref[start : start + light, :] = low
        local.append(lax.broadcasted_iota(jnp.int32, (rows, span), 1) + r * span == index_ref[...])
    delta = base_ref[...]
    for n in range(count):
        choose = local[n].astype(jnp.bfloat16)
        delta = delta + adapter_scale * (
            jnp.dot(choose, high_ref[n * span : (n + 1) * span, :], preferred_element_type=jnp.float32)
            + jnp.dot(choose, low_ref[n * span : (n + 1) * span, :], preferred_element_type=jnp.float32)
        )
    out_ref[...] = delta.astype(out_ref.dtype)


def finish(scalars, index, base, up, shrinks, after, shifts, dtype, homes, held, light):
    rows, columns = base.shape
    span = (held + 1) * light
    return pl.pallas_call(
        functools.partial(finish_kernel, homes, held, light, up.shape[1], shifts, len(after)),
        out_shape=jax.ShapeDtypeStruct((rows, columns), dtype),
        in_specs=[SMEM] + [VMEM] * (3 + len(shifts)) + [ANY] * len(after),
        out_specs=VMEM,
        scratch_shapes=[pltpu.VMEM((len(shifts) * span, columns), jnp.bfloat16)] * 2,
        compiler_params=PARAMS,
        name="finish",
    )(scalars, index, base, up, *shrinks, *after)


def gate_kernel(value_ref, *refs):
    pass


def gate(value, after):
    return pl.pallas_call(
        gate_kernel,
        out_shape=jax.ShapeDtypeStruct(value.shape, value.dtype),
        in_specs=[ANY] * (1 + len(after)),
        out_specs=ANY,
        input_output_aliases={0: 0},
        name="gate",
    )(value, *after)


def line_step(moving, hop, size):
    return [
        lax.ppermute(
            value,
            "batch",
            [(i, i + step) for i in range(size) if 0 <= i + step < size and 0 <= i - step * (hop - 1) < size],
        )
        for value, step in zip(moving, (1, -1))
    ]


def join_up(found, place, homes):
    teams = lax.axis_size("groups")
    team = lax.axis_index("groups")
    ordered = jnp.concatenate(
        [
            functools.reduce(
                lambda kept, hop: jnp.where(place + hop == home, found[hop], kept),
                sorted(found),
                jnp.zeros_like(found[0]),
            )
            for home in range(homes)
        ],
        axis=0,
    )
    shares = [ordered] + [
        lax.ppermute(ordered, "groups", [(i, (i + s) % teams) for i in range(teams)])
        for s in range(1, teams)
    ]
    return jnp.concatenate(
        [
            functools.reduce(
                lambda kept, s: jnp.where(lax.rem(team + teams - s, teams) == part, shares[s], kept),
                range(1, teams),
                shares[0],
            )
            for part in range(teams)
        ],
        axis=1,
    )


def base_kernel(waited, block_ref, tokens_ref, weight_ref, *refs):
    refs[waited][...] = jnp.dot(tokens_ref[...], weight_ref[...], preferred_element_type=jnp.float32)


def base_part(tokens, weight, blocks, columns, after):
    rows, width = tokens.shape
    count = blocks.shape[0]
    return pl.pallas_call(
        functools.partial(base_kernel, len(after)),
        out_shape=jax.ShapeDtypeStruct((rows, count * columns), jnp.float32),
        grid_spec=pltpu.PrefetchScalarGridSpec(
            num_scalar_prefetch=1,
            grid=(count,),
            in_specs=[
                pl.BlockSpec((rows, width), lambda j, chosen: (0, 0)),
                pl.BlockSpec((width, columns), lambda j, chosen: (0, chosen[j])),
            ]
            + [ANY] * len(after),
            out_specs=pl.BlockSpec((rows, columns), lambda j, chosen: (0, j)),
        ),
        compiler_params=PARAMS,
        name="base",
    )(blocks, tokens, weight, *after)


def reduce_base(tokens, weight, piece, pieces, columns, after):
    keep = [0]
    bit = pieces // 2
    while bit > 1:
        keep = keep + [p + bit for p in keep]
        bit //= 2
    keep = jnp.array(keep, jnp.int32)
    sent = base_part(tokens, weight, piece ^ keep ^ 1, columns, after)
    kept = base_part(tokens, weight, piece ^ keep, columns, [sent])
    bit = 1
    while True:
        kept = kept + lax.ppermute(sent, "tensor", [(i, i ^ bit) for i in range(pieces)])
        bit *= 2
        if bit >= pieces:
            return kept
        half = kept.shape[1] // 2
        kept, sent = kept[:, :half], kept[:, half:]


def on_device(tokens, request_adapter, adapter_entry, key_value_weight, adapter_down, adapter_up):
    rows, width = tokens.shape
    adapters = adapter_entry.shape[0]
    held, rank, columns = adapter_up.shape
    value_side = key_value_weight.shape[1] // 2 // columns
    homes = lax.axis_size("batch")
    pieces = lax.axis_size("tensor")
    place = lax.axis_index("batch").astype(jnp.int32)
    piece = lax.axis_index("tensor").astype(jnp.int32)
    light = rows // adapters
    span = (held + 1) * light
    order = sorted(range(1, homes), key=lambda r: (-min(r, homes - r), r))
    block_shape = jax.ShapeDtypeStruct((span, width), jnp.bfloat16)

    teams = lax.axis_size("groups")
    share = rank // teams
    own_up = lax.dynamic_slice_in_dim(adapter_up, lax.axis_index("groups") * share, share, 1)
    found = {0: own_up}
    moving = line_step([own_up] * 2, 1, homes)
    found[-1], found[1] = moving

    index, heavy, first = pl.pallas_call(
        functools.partial(route_kernel, homes, held, light, order[0]),
        out_shape=[
            jax.ShapeDtypeStruct((1, rows), jnp.int32),
            jax.ShapeDtypeStruct((8, 128), jnp.int32),
            block_shape,
        ],
        in_specs=[SMEM, SMEM, VMEM, VMEM],
        out_specs=[VMEM] * 3,
        compiler_params=PARAMS,
        name="route",
    )(place.reshape(1), adapter_entry, request_adapter.reshape(1, rows), tokens)
    later = order[1:] + [0]
    rest = pl.pallas_call(
        functools.partial(pack_kernel, span, later, len(moving)),
        out_shape=[block_shape] * len(later),
        in_specs=[VMEM] * 2 + [ANY] * len(moving),
        out_specs=[VMEM] * len(later),
        compiler_params=PARAMS,
        name="pack",
    )(index, tokens, *moving)
    blocks = {order[0]: first, **dict(zip(later, rest))}

    arrived = {0: blocks[0]}
    for r in order:
        arrived[r] = lax.ppermute(blocks[r], "batch", [(i, (i + r) % homes) for i in range(homes)])
    base = reduce_base(tokens, key_value_weight, piece, pieces, columns, [blocks[0]])
    for hop in range(2, homes):
        if hop > 2:
            moving = [gate(value, [base]) for value in moving]
        moving = line_step(moving, hop, homes)
        found[-hop], found[hop] = moving
    up = join_up(found, place, homes)

    heavy = heavy[0, 0]
    heavy_here = (heavy // held == place).astype(jnp.int32)
    scalars = jnp.stack([piece, lax.rem(heavy, held), heavy_here])
    shrinks = {}
    after = [base]
    for r in [0] + order:
        parts = pl.pallas_call(
            functools.partial(shrink_kernel, held, light, rank, pieces, value_side, len(after)),
            out_shape=[jax.ShapeDtypeStruct((entry_places(held) * light, 2 * rank), jnp.float32)] * pieces,
            in_specs=[SMEM, VMEM, VMEM] + [ANY] * len(after),
            out_specs=[VMEM] * pieces,
            compiler_params=PARAMS,
            name="shrink",
        )(scalars, arrived[r], adapter_down, *after)
        total = parts[0]
        for o in range(1, pieces):
            total = total + lax.ppermute(parts[o], "tensor", [(i, i ^ o) for i in range(pieces)])
        after = [total]
        if r:
            shrinks[r] = lax.ppermute(total, "batch", [(i, (i - r) % homes) for i in range(homes)])
        else:
            shrinks[r] = total

    places = jnp.stack([place, heavy])
    column = index.reshape(rows, 1)
    early = [0] + order[:-1]
    running = finish(
        places, column, base, up, [shrinks[r] for r in early], after, early, jnp.float32, homes, held, light
    )
    return finish(
        places, column, running, up, [shrinks[order[-1]]], [], order[-1:], jnp.bfloat16, homes, held, light
    )


def solution(mesh):
    in_specs = (
        P(("groups", "batch"), "tensor"),
        P(("groups", "batch")),
        P(),
        P("tensor", None),
        P("batch", "tensor", None),
        P("batch", None, "tensor"),
    )
    out_specs = P(("groups", "batch"), "tensor")
    return jax.shard_map(
        on_device, mesh=mesh, in_specs=in_specs, out_specs=out_specs, check_vma=False
    )
```

```python
import functools

import jax
import jax.numpy as jnp
from jax import lax
from jax.experimental import pallas as pl
from jax.experimental.pallas import tpu as pltpu
from jax.sharding import PartitionSpec as P

adapter_scale = 0.5
VMEM_BYTES = 24 * 1024 * 1024
VMEM = pl.BlockSpec(memory_space=pltpu.VMEM)
ANY = pl.BlockSpec(memory_space=pl.ANY)
SMEM = pl.BlockSpec(memory_space=pltpu.SMEM)
COST = pl.CostEstimate(flops=1, bytes_accessed=1, transcendentals=0)
PARAMS = pltpu.CompilerParams(vmem_limit_bytes=VMEM_BYTES)


def place_rows(index, start, tokens_ref, block_ref):
    local = lax.broadcasted_iota(jnp.int32, (block_ref.shape[0], index.shape[1]), 0)
    choose = (local + start == index).astype(jnp.bfloat16)
    block_ref[...] = jnp.dot(
        choose, tokens_ref[...], preferred_element_type=jnp.float32
    ).astype(jnp.bfloat16)


def route_kernel(
    homes, held, light, shift, place_ref, entry_hbm, request_hbm, tokens_hbm,
    index_ref, heavy_ref, block_ref, entry_ref, request_ref, tokens_ref, sems,
):
    loads = [
        pltpu.make_async_copy(source, target, sems.at[n])
        for n, (source, target) in enumerate(
            [(request_hbm, request_ref), (entry_hbm, entry_ref), (tokens_hbm, tokens_ref)]
        )
    ]
    for load in loads:
        load.start()
    rows = tokens_ref.shape[0]
    adapters = entry_ref.shape[0]
    span = (held + 1) * light
    earlier = (
        lax.broadcasted_iota(jnp.int32, (rows, rows), 0) < lax.broadcasted_iota(jnp.int32, (rows, rows), 1)
    ).astype(jnp.bfloat16)
    loads[0].wait()
    request = request_ref[...].reshape(1, rows)
    onehot = lax.broadcasted_iota(jnp.int32, (adapters, rows), 0) == request
    before = jnp.dot(onehot.astype(jnp.bfloat16), earlier, preferred_element_type=jnp.float32)
    position = jnp.sum(jnp.where(onehot, before, 0.0), axis=0, keepdims=True).astype(jnp.int32)
    loads[1].wait()
    slot = jnp.zeros_like(position)
    for a in range(adapters):
        slot = jnp.where(request == a, entry_ref[a], slot)
    home = slot // held
    relative = lax.rem(home - place_ref[0] + homes, homes)
    inside = jnp.where(
        position < light, (slot - home * held) * light + position, held * light + position - light
    )
    index = relative * span + inside
    index_ref[...] = index
    heavy = jnp.max(jnp.where(position >= light, slot, 0), axis=1, keepdims=True)
    heavy_ref[...] = jnp.broadcast_to(heavy, heavy_ref.shape)
    loads[2].wait()
    place_rows(index, shift * span, tokens_ref, block_ref)


def pack_kernel(span, shifts, index_ref, tokens_ref, mark_ref, *block_refs):
    mark_ref[...] = jnp.zeros_like(mark_ref)
    for shift, block_ref in zip(shifts, block_refs):
        place_rows(index_ref[...], shift * span, tokens_ref, block_ref)


def entry_places(held):
    return (held + 2) // 2


def shrink_kernel(held, light, rank, value_side, waited, passed, scalar_ref, block_ref, down_ref, *refs):
    passed_refs, out_ref, left_refs = refs[waited : waited + passed], refs[waited + passed], refs[waited + passed + 1 :]
    groups = entry_places(held)

    def product(e):
        if e > held:
            return jnp.zeros((light, 2 * rank), jnp.float32)
        factor = down_ref[e] if e < held else down_ref[scalar_ref[1]]
        value = jnp.dot(
            block_ref[e * light : (e + 1) * light, :], factor, preferred_element_type=jnp.float32
        )
        return value if e < held else jnp.where(scalar_ref[2] == 1, value, 0.0)

    on_value_side = scalar_ref[0] >= value_side
    for g in range(groups):
        first, second = product(g), product(g + groups)
        key = jnp.concatenate([first[:, :rank], second[:, :rank]], axis=1)
        value = jnp.concatenate([first[:, rank:], second[:, rank:]], axis=1)
        out_ref[g * light : (g + 1) * light, :] = jnp.where(on_value_side, value, key)
        out_ref[(groups + g) * light : (groups + g + 1) * light, :] = jnp.where(on_value_side, key, value)
    for source, target in zip(passed_refs, left_refs):
        target[...] = source[...]


def split_pair(value):
    high = value.astype(jnp.bfloat16)
    low = (value - high.astype(jnp.float32)).astype(jnp.bfloat16)
    return high, low


def finish_kernel(homes, held, light, rank, shifts, waited, place_ref, index_ref, base_ref, up_ref, *refs):
    count = len(shifts)
    refs = refs[:count] + refs[count + waited :]
    shrink_refs, out_ref, high_ref, low_ref = refs[:count], refs[count], refs[count + 1], refs[count + 2]
    span = (held + 1) * light
    rows = base_ref.shape[0]
    groups = entry_places(held)
    local = []
    for n, r in enumerate(shifts):
        home = lax.rem(place_ref[0] + r, homes)
        for e in range(held + 1):
            entry = home * held + e if e < held else place_ref[1]
            g, side = e % groups, e // groups
            high, low = split_pair(
                shrink_refs[n][g * light : (g + 1) * light, side * rank : (side + 1) * rank]
            )
            factor = up_ref[entry]
            delta = jnp.dot(high, factor, preferred_element_type=jnp.float32) + jnp.dot(
                low, factor, preferred_element_type=jnp.float32
            )
            high, low = split_pair(delta)
            start = n * span + e * light
            high_ref[start : start + light, :] = high
            low_ref[start : start + light, :] = low
        local.append(lax.broadcasted_iota(jnp.int32, (rows, span), 1) + r * span == index_ref[...])
    delta = base_ref[...]
    for n in range(count):
        choose = local[n].astype(jnp.bfloat16)
        delta = delta + adapter_scale * (
            jnp.dot(choose, high_ref[n * span : (n + 1) * span, :], preferred_element_type=jnp.float32)
            + jnp.dot(choose, low_ref[n * span : (n + 1) * span, :], preferred_element_type=jnp.float32)
        )
    out_ref[...] = delta.astype(out_ref.dtype)


def finish(scalars, index, base, up, shrinks, after, shifts, dtype, homes, held, light):
    rows, columns = base.shape
    span = (held + 1) * light
    return pl.pallas_call(
        functools.partial(finish_kernel, homes, held, light, up.shape[1], shifts, len(after)),
        out_shape=jax.ShapeDtypeStruct((rows, columns), dtype),
        in_specs=[SMEM] + [VMEM] * (3 + len(shifts)) + [ANY] * len(after),
        out_specs=VMEM,
        scratch_shapes=[pltpu.VMEM((len(shifts) * span, columns), jnp.bfloat16)] * 2,
        compiler_params=PARAMS,
        cost_estimate=COST,
        name="finish",
    )(scalars, index, base, up, *shrinks, *after)


def join_kernel(first_ref, second_ref, after_ref, out_ref):
    count = first_ref.shape[0]
    out_ref[:count] = first_ref[...]
    out_ref[count:] = second_ref[...]


def join(first, second, after):
    return pl.pallas_call(
        join_kernel,
        out_shape=jax.ShapeDtypeStruct((2 * first.shape[0], *first.shape[1:]), first.dtype),
        in_specs=[VMEM, VMEM, ANY],
        out_specs=VMEM,
        compiler_params=PARAMS,
        cost_estimate=COST,
        name="join",
    )(first, second, after)


def line_gather(value, place, homes, after):
    if homes == 4:
        beside = lax.ppermute(value, "batch", [(0, 1), (1, 0), (2, 3), (3, 2)])
        across = lax.ppermute(join(value, beside, after), "batch", [(1, 2), (2, 1)])
        beyond = lax.ppermute(across, "batch", [(1, 0), (2, 3)])
        far = jnp.where((place == 1) | (place == 2), across, beyond)
        near, next_to = far[: value.shape[0]], far[value.shape[0] :]
        even = place % 2 == 0
        low, high = jnp.where(even, value, beside), jnp.where(even, beside, value)
        left = place < 2
        return jnp.concatenate(
            [
                jnp.where(left, low, next_to),
                jnp.where(left, high, near),
                jnp.where(left, near, low),
                jnp.where(left, next_to, high),
            ],
            axis=0,
        )
    bit = 1
    while bit < homes:
        other = lax.ppermute(value, "batch", [(i, i ^ bit) for i in range(homes)])
        first = (place // bit) % 2 == 0
        value = jnp.concatenate([jnp.where(first, value, other), jnp.where(first, other, value)], axis=0)
        bit *= 2
    return value


def gather_up(adapter_up, place, homes, after):
    teams = lax.axis_size("groups")
    team = lax.axis_index("groups")
    share = adapter_up.shape[1] // teams
    ordered = line_gather(lax.dynamic_slice_in_dim(adapter_up, team * share, share, 1), place, homes, after)
    shares = [ordered] + [
        lax.ppermute(ordered, "groups", [(i, (i + s) % teams) for i in range(teams)])
        for s in range(1, teams)
    ]
    return jnp.concatenate(
        [
            functools.reduce(
                lambda kept, s: jnp.where(lax.rem(team + teams - s, teams) == part, shares[s], kept),
                range(1, teams),
                shares[0],
            )
            for part in range(teams)
        ],
        axis=1,
    )


def base_kernel(waited, block_ref, tokens_ref, weight_ref, *refs):
    refs[waited][...] = jnp.dot(tokens_ref[...], weight_ref[...], preferred_element_type=jnp.float32)


def base_part(tokens, weight, blocks, columns, slab, slabs, after):
    rows, width = tokens.shape[0] // slabs, tokens.shape[1]
    count = blocks.shape[0]
    return pl.pallas_call(
        functools.partial(base_kernel, len(after)),
        out_shape=jax.ShapeDtypeStruct((rows, count * columns), jnp.float32),
        grid_spec=pltpu.PrefetchScalarGridSpec(
            num_scalar_prefetch=1,
            grid=(count,),
            in_specs=[
                pl.BlockSpec((rows, width), lambda j, chosen: (slab, 0)),
                pl.BlockSpec((width, columns), lambda j, chosen: (0, chosen[j])),
            ]
            + [ANY] * len(after),
            out_specs=pl.BlockSpec((rows, columns), lambda j, chosen: (0, j)),
        ),
        compiler_params=PARAMS,
        cost_estimate=COST,
        name="base",
    )(blocks, tokens, weight, *after)


def reduce_base(tokens, weight, piece, pieces, columns, slab, slabs, after):
    keep = [0]
    bit = pieces // 2
    while bit > 1:
        keep = keep + [p + bit for p in keep]
        bit //= 2
    keep = jnp.array(keep, jnp.int32)
    sent = base_part(tokens, weight, piece ^ keep ^ 1, columns, slab, slabs, after)
    kept = base_part(tokens, weight, piece ^ keep, columns, slab, slabs, [sent])
    bit = 1
    while True:
        kept = kept + lax.ppermute(sent, "tensor", [(i, i ^ bit) for i in range(pieces)])
        bit *= 2
        if bit >= pieces:
            return kept
        half = kept.shape[1] // 2
        kept, sent = kept[:, :half], kept[:, half:]


def on_device(tokens, request_adapter, adapter_entry, key_value_weight, adapter_down, adapter_up):
    rows, width = tokens.shape
    adapters = adapter_entry.shape[0]
    held, rank, columns = adapter_up.shape
    value_side = key_value_weight.shape[1] // 2 // columns
    homes = lax.axis_size("batch")
    pieces = lax.axis_size("tensor")
    place = lax.axis_index("batch").astype(jnp.int32)
    piece = lax.axis_index("tensor").astype(jnp.int32)
    light = rows // adapters
    span = (held + 1) * light
    order = sorted(range(1, homes), key=lambda r: (-min(r, homes - r), r))
    block_shape = jax.ShapeDtypeStruct((span, width), jnp.bfloat16)

    index, heavy, first = pl.pallas_call(
        functools.partial(route_kernel, homes, held, light, order[0]),
        out_shape=[
            jax.ShapeDtypeStruct((1, rows), jnp.int32),
            jax.ShapeDtypeStruct((8, 128), jnp.int32),
            block_shape,
        ],
        in_specs=[SMEM, ANY, ANY, ANY],
        out_specs=[VMEM] * 3,
        scratch_shapes=[
            pltpu.SMEM(adapter_entry.shape, jnp.int32),
            pltpu.VMEM((rows,), jnp.int32),
            pltpu.VMEM(tokens.shape, jnp.bfloat16),
            pltpu.SemaphoreType.DMA((3,)),
        ],
        compiler_params=PARAMS,
        cost_estimate=COST,
        name="route",
    )(place.reshape(1), adapter_entry, request_adapter, tokens)
    up = gather_up(adapter_up, place, homes, index)

    def pack(shifts):
        return pl.pallas_call(
            functools.partial(pack_kernel, span, shifts),
            out_shape=[jax.ShapeDtypeStruct((8, 128), jnp.int32)] + [block_shape] * len(shifts),
            in_specs=[VMEM] * 2,
            out_specs=[VMEM] * (1 + len(shifts)),
            compiler_params=PARAMS,
            cost_estimate=COST,
            name="pack",
        )(index, tokens)

    def send(block, r):
        return lax.ppermute(block, "batch", [(i, (i + r) % homes) for i in range(homes)])

    arrived = {order[0]: send(first, order[0])}
    later = order[1:] + [0]
    packed, *blocks = pack(later)
    for r, block in zip(later, blocks):
        arrived[r] = send(block, r) if r else block

    heavy = heavy[0, 0]
    heavy_here = (heavy // held == place).astype(jnp.int32)
    scalars = jnp.stack([piece, lax.rem(heavy, held), heavy_here])
    height = entry_places(held) * light

    def shrink(block, after, passed):
        return pl.pallas_call(
            functools.partial(shrink_kernel, held, light, rank, value_side, len(after), len(passed)),
            out_shape=[jax.ShapeDtypeStruct((2 * height, 2 * rank), jnp.float32)]
            + [jax.ShapeDtypeStruct(p.shape, p.dtype) for p in passed],
            in_specs=[SMEM, VMEM, VMEM] + [ANY] * len(after) + [VMEM] * len(passed),
            out_specs=[VMEM] * (1 + len(passed)),
            compiler_params=PARAMS,
            cost_estimate=COST,
            name="shrink",
        )(scalars, block, adapter_down, *after, *passed)

    def combine(value):
        bit = 1
        while bit < pieces // 2:
            value = value + lax.ppermute(value, "tensor", [(i, i ^ bit) for i in range(pieces)])
            bit *= 2
        total = value[:height] + lax.ppermute(value[height:], "tensor", [(i, i ^ bit) for i in range(pieces)])
        return total

    early = order[:-1] + [0]
    totals = []
    after = [packed]
    for r in early:
        (value,) = shrink(arrived[r], after, [])
        totals.append(combine(value))
    slabs = 2
    base = jnp.concatenate(
        [
            reduce_base(tokens, key_value_weight, piece, pieces, columns, slab, slabs, [packed])
            for slab in range(slabs)
        ],
        axis=0,
    )
    value, *totals = shrink(arrived[order[-1]], [], totals)
    last = combine(value)

    def give_back(total, r):
        return lax.ppermute(total, "batch", [(i, (i - r) % homes) for i in range(homes)]) if r else total

    shrinks = [give_back(total, r) for total, r in zip(totals, early)]
    places = jnp.stack([place, heavy])
    column = index.reshape(rows, 1)
    running = finish(places, column, base, up, shrinks, [last], early, jnp.float32, homes, held, light)
    shrinks = [give_back(last, order[-1])]
    return finish(places, column, running, up, shrinks, [], order[-1:], jnp.bfloat16, homes, held, light)


def solution(mesh):
    in_specs = (
        P(("groups", "batch"), "tensor"),
        P(("groups", "batch")),
        P(),
        P("tensor", None),
        P("batch", "tensor", None),
        P("batch", None, "tensor"),
    )
    out_specs = P(("groups", "batch"), "tensor")
    return jax.shard_map(
        on_device, mesh=mesh, in_specs=in_specs, out_specs=out_specs, check_vma=False
    )
```

```python
import functools

import jax
import jax.numpy as jnp
from jax import lax
from jax.experimental import pallas as pl
from jax.experimental.pallas import tpu as pltpu
from jax.sharding import PartitionSpec as P

adapter_scale = 0.5
VMEM_BYTES = 24 * 1024 * 1024
WIDE = pltpu.CompilerParams(vmem_limit_bytes=60 * 1024 * 1024)
VMEM = pl.BlockSpec(memory_space=pltpu.VMEM)
ANY = pl.BlockSpec(memory_space=pl.ANY)
HBM = pl.BlockSpec(memory_space=pltpu.HBM)
SMEM = pl.BlockSpec(memory_space=pltpu.SMEM)
COST = pl.CostEstimate(flops=1, bytes_accessed=1, transcendentals=0)
PARAMS = pltpu.CompilerParams(vmem_limit_bytes=VMEM_BYTES)


def place_rows(index, start, tokens_ref, block_ref):
    local = lax.broadcasted_iota(jnp.int32, (block_ref.shape[0], index.shape[1]), 0)
    choose = (local + start == index).astype(jnp.bfloat16)
    block_ref[...] = jnp.dot(
        choose, tokens_ref[...], preferred_element_type=jnp.float32
    ).astype(jnp.bfloat16)


def route_kernel(
    homes, held, light, shift, place_ref, entry_hbm, request_hbm, tokens_hbm,
    index_ref, heavy_ref, block_ref, entry_ref, request_ref, tokens_ref, sems,
):
    loads = [
        pltpu.make_async_copy(source, target, sems.at[n])
        for n, (source, target) in enumerate(
            [(request_hbm, request_ref), (entry_hbm, entry_ref), (tokens_hbm, tokens_ref)]
        )
    ]
    for load in loads:
        load.start()
    rows = tokens_ref.shape[0]
    adapters = entry_ref.shape[0]
    span = (held + 1) * light
    earlier = (
        lax.broadcasted_iota(jnp.int32, (rows, rows), 0) < lax.broadcasted_iota(jnp.int32, (rows, rows), 1)
    ).astype(jnp.bfloat16)
    loads[0].wait()
    request = request_ref[...].reshape(1, rows)
    onehot = lax.broadcasted_iota(jnp.int32, (adapters, rows), 0) == request
    before = jnp.dot(onehot.astype(jnp.bfloat16), earlier, preferred_element_type=jnp.float32)
    position = jnp.sum(jnp.where(onehot, before, 0.0), axis=0, keepdims=True).astype(jnp.int32)
    loads[1].wait()
    slot = jnp.zeros_like(position)
    for a in range(adapters):
        slot = jnp.where(request == a, entry_ref[a], slot)
    home = slot // held
    relative = lax.rem(home - place_ref[0] + homes, homes)
    inside = jnp.where(
        position < light, (slot - home * held) * light + position, held * light + position - light
    )
    index = relative * span + inside
    index_ref[...] = index
    heavy = jnp.max(jnp.where(position >= light, slot, 0), axis=1, keepdims=True)
    heavy_ref[...] = jnp.broadcast_to(heavy, heavy_ref.shape)
    loads[2].wait()
    place_rows(index, shift * span, tokens_ref, block_ref)


def pack_kernel(span, shifts, index_ref, tokens_ref, mark_ref, *refs):
    count = len(shifts)
    block_refs, buffer, sems = refs[:count], refs[count], refs[count + 1]
    mark_ref[...] = jnp.zeros_like(mark_ref)
    stores = []
    for n, shift in enumerate(shifts):
        place_rows(index_ref[...], shift * span, tokens_ref, buffer.at[n])
        stores.append(pltpu.make_async_copy(buffer.at[n], block_refs[n], sems.at[n]))
        stores[-1].start()
    for store in stores:
        store.wait()


def entry_places(held):
    return (held + 2) // 2


def shrink_kernel(held, light, rank, value_side, waited, passed, scalar_ref, block_ref, down_ref, *refs):
    passed_refs, out_ref, left_refs = refs[waited : waited + passed], refs[waited + passed], refs[waited + passed + 1 :]
    groups = entry_places(held)

    def product(e):
        if e > held:
            return jnp.zeros((light, 2 * rank), jnp.float32)
        factor = down_ref[e] if e < held else down_ref[scalar_ref[1]]
        value = jnp.dot(
            block_ref[e * light : (e + 1) * light, :], factor, preferred_element_type=jnp.float32
        )
        return value if e < held else jnp.where(scalar_ref[2] == 1, value, 0.0)

    on_value_side = scalar_ref[0] >= value_side
    for g in range(groups):
        first, second = product(g), product(g + groups)
        key = jnp.concatenate([first[:, :rank], second[:, :rank]], axis=1)
        value = jnp.concatenate([first[:, rank:], second[:, rank:]], axis=1)
        out_ref[g * light : (g + 1) * light, :] = jnp.where(on_value_side, value, key)
        out_ref[(groups + g) * light : (groups + g + 1) * light, :] = jnp.where(on_value_side, key, value)
    for source, target in zip(passed_refs, left_refs):
        target[...] = source[...]


def split_pair(value):
    high = value.astype(jnp.bfloat16)
    low = (value - high.astype(jnp.float32)).astype(jnp.bfloat16)
    return high, low


def finish_kernel(homes, held, light, rank, shifts, waited, place_ref, index_ref, base_ref, up_ref, *refs):
    count = len(shifts)
    refs = refs[:count] + refs[count + waited :]
    shrink_refs, out_ref, high_ref, low_ref = refs[:count], refs[count], refs[count + 1], refs[count + 2]
    span = (held + 1) * light
    rows = base_ref.shape[0]
    groups = entry_places(held)
    local = []
    for n, r in enumerate(shifts):
        for e in range(held + 1):
            entry = r * held + e if e < held else place_ref[0]
            g, side = e % groups, e // groups
            high, low = split_pair(
                shrink_refs[n][g * light : (g + 1) * light, side * rank : (side + 1) * rank]
            )
            factor = up_ref[entry]
            delta = jnp.dot(high, factor, preferred_element_type=jnp.float32) + jnp.dot(
                low, factor, preferred_element_type=jnp.float32
            )
            high, low = split_pair(delta)
            start = n * span + e * light
            high_ref[start : start + light, :] = high
            low_ref[start : start + light, :] = low
        local.append(lax.broadcasted_iota(jnp.int32, (rows, span), 1) + r * span == index_ref[...])
    delta = base_ref[...]
    for n in range(count):
        choose = local[n].astype(jnp.bfloat16)
        delta = delta + adapter_scale * (
            jnp.dot(choose, high_ref[n * span : (n + 1) * span, :], preferred_element_type=jnp.float32)
            + jnp.dot(choose, low_ref[n * span : (n + 1) * span, :], preferred_element_type=jnp.float32)
        )
    out_ref[...] = delta.astype(out_ref.dtype)


def finish(scalars, index, base, up, shrinks, after, shifts, dtype, homes, held, light):
    rows, columns = base.shape
    span = (held + 1) * light
    return pl.pallas_call(
        functools.partial(finish_kernel, homes, held, light, up.shape[1], shifts, len(after)),
        out_shape=jax.ShapeDtypeStruct((rows, columns), dtype),
        in_specs=[SMEM] + [VMEM] * (3 + len(shifts)) + [ANY] * len(after),
        out_specs=VMEM,
        scratch_shapes=[pltpu.VMEM((len(shifts) * span, columns), jnp.bfloat16)] * 2,
        compiler_params=PARAMS,
        cost_estimate=COST,
        name="finish",
    )(scalars, index, base, up, *shrinks, *after)


def gather_up(adapter_up, homes):
    teams = lax.axis_size("groups")
    team = lax.axis_index("groups")
    share = adapter_up.shape[1] // teams
    own = lax.dynamic_slice_in_dim(adapter_up, team * share, share, 1)
    found = [
        lax.ppermute(own, "batch", [(i, (i - r) % homes) for i in range(homes)]) for r in range(1, homes)
    ]
    ordered = jnp.concatenate([own] + found, axis=0)
    shares = [ordered] + [
        lax.ppermute(ordered, "groups", [(i, (i + s) % teams) for i in range(teams)])
        for s in range(1, teams)
    ]
    return jnp.concatenate(
        [
            functools.reduce(
                lambda kept, s: jnp.where(lax.rem(team + teams - s, teams) == part, shares[s], kept),
                range(1, teams),
                shares[0],
            )
            for part in range(teams)
        ],
        axis=1,
    ), found


def base_kernel(waited, block_ref, tokens_ref, weight_ref, *refs):
    refs[waited][...] = jnp.dot(tokens_ref[...], weight_ref[...], preferred_element_type=jnp.float32)


def base_part(tokens, weight, blocks, columns, slab, slabs, after):
    rows, width = tokens.shape[0] // slabs, tokens.shape[1]
    count = blocks.shape[0]
    return pl.pallas_call(
        functools.partial(base_kernel, len(after)),
        out_shape=jax.ShapeDtypeStruct((rows, count * columns), jnp.float32),
        grid_spec=pltpu.PrefetchScalarGridSpec(
            num_scalar_prefetch=1,
            grid=(count,),
            in_specs=[
                pl.BlockSpec((rows, width), lambda j, chosen: (slab, 0)),
                pl.BlockSpec((width, columns), lambda j, chosen: (0, chosen[j])),
            ]
            + [ANY] * len(after),
            out_specs=pl.BlockSpec((rows, columns), lambda j, chosen: (0, j)),
        ),
        compiler_params=PARAMS,
        cost_estimate=COST,
        name="base",
    )(blocks, tokens, weight, *after)


def reduce_base(tokens, weight, piece, pieces, columns, slab, slabs, after):
    keep = [0]
    bit = pieces // 2
    while bit > 1:
        keep = keep + [p + bit for p in keep]
        bit //= 2
    keep = jnp.array(keep, jnp.int32)
    sent = base_part(tokens, weight, piece ^ keep ^ 1, columns, slab, slabs, after)
    kept = base_part(tokens, weight, piece ^ keep, columns, slab, slabs, [sent])
    bit = 1
    while True:
        kept = kept + lax.ppermute(sent, "tensor", [(i, i ^ bit) for i in range(pieces)])
        bit *= 2
        if bit >= pieces:
            return kept
        half = kept.shape[1] // 2
        kept, sent = kept[:, :half], kept[:, half:]


def on_device(tokens, request_adapter, adapter_entry, key_value_weight, adapter_down, adapter_up):
    rows, width = tokens.shape
    adapters = adapter_entry.shape[0]
    held, rank, columns = adapter_up.shape
    value_side = key_value_weight.shape[1] // 2 // columns
    homes = lax.axis_size("batch")
    pieces = lax.axis_size("tensor")
    place = lax.axis_index("batch").astype(jnp.int32)
    piece = lax.axis_index("tensor").astype(jnp.int32)
    light = rows // adapters
    span = (held + 1) * light
    order = sorted(range(1, homes), key=lambda r: (-min(r, homes - r), r))
    block_shape = jax.ShapeDtypeStruct((span, width), jnp.bfloat16)

    up, found = gather_up(adapter_up, homes)
    index, heavy, first = pl.pallas_call(
        functools.partial(route_kernel, homes, held, light, order[0]),
        out_shape=[
            jax.ShapeDtypeStruct((1, rows), jnp.int32),
            jax.ShapeDtypeStruct((8, 128), jnp.int32),
            block_shape,
        ],
        in_specs=[SMEM, HBM, HBM, HBM],
        out_specs=[VMEM] * 3,
        scratch_shapes=[
            pltpu.SMEM(adapter_entry.shape, jnp.int32),
            pltpu.VMEM((rows,), jnp.int32),
            pltpu.VMEM(tokens.shape, jnp.bfloat16),
            pltpu.SemaphoreType.DMA((3,)),
        ],
        compiler_params=WIDE,
        cost_estimate=COST,
        name="route",
    )(place.reshape(1), adapter_entry, request_adapter, tokens)
    def pack(shifts):
        return pl.pallas_call(
            functools.partial(pack_kernel, span, shifts),
            out_shape=[jax.ShapeDtypeStruct((8, 128), jnp.int32)] + [block_shape] * len(shifts),
            in_specs=[VMEM] * 2,
            out_specs=[VMEM] + [HBM] * len(shifts),
            scratch_shapes=[
                pltpu.VMEM((len(shifts), span, width), jnp.bfloat16),
                pltpu.SemaphoreType.DMA((len(shifts),)),
            ],
            compiler_params=WIDE,
            cost_estimate=COST,
            name="pack",
        )(index, tokens)

    def send(block, r):
        return lax.ppermute(block, "batch", [(i, (i + r) % homes) for i in range(homes)])

    arrived = {order[0]: send(first, order[0])}
    later = order[1:] + [0]
    packed, *blocks = pack(later)
    for r, block in zip(later, blocks):
        arrived[r] = send(block, r) if r else block

    heavy = heavy[0, 0]
    heavy_here = (heavy // held == place).astype(jnp.int32)
    scalars = jnp.stack([piece, lax.rem(heavy, held), heavy_here])
    height = entry_places(held) * light

    def shrink(block, after, passed):
        return pl.pallas_call(
            functools.partial(shrink_kernel, held, light, rank, value_side, len(after), len(passed)),
            out_shape=[jax.ShapeDtypeStruct((2 * height, 2 * rank), jnp.float32)]
            + [jax.ShapeDtypeStruct(p.shape, p.dtype) for p in passed],
            in_specs=[SMEM, VMEM, VMEM] + [ANY] * len(after) + [VMEM] * len(passed),
            out_specs=[VMEM] * (1 + len(passed)),
            compiler_params=PARAMS,
            cost_estimate=COST,
            name="shrink",
        )(scalars, block, adapter_down, *after, *passed)

    def combine(value):
        bit = 1
        while bit < pieces // 2:
            value = value + lax.ppermute(value, "tensor", [(i, i ^ bit) for i in range(pieces)])
            bit *= 2
        total = value[:height] + lax.ppermute(value[height:], "tensor", [(i, i ^ bit) for i in range(pieces)])
        return total

    early = order[:-1] + [0]
    totals = []
    after = [packed]
    for r in early:
        (value,) = shrink(arrived[r], after, [])
        totals.append(combine(value))
    slabs = 2
    base = jnp.concatenate(
        [
            reduce_base(tokens, key_value_weight, piece, pieces, columns, slab, slabs, [packed])
            for slab in range(slabs)
        ],
        axis=0,
    )
    value, *totals = shrink(arrived[order[-1]], [], totals)
    last = combine(value)

    def give_back(total, r):
        return lax.ppermute(total, "batch", [(i, (i - r) % homes) for i in range(homes)]) if r else total

    shrinks = [give_back(total, r) for total, r in zip(totals, early)]
    places = lax.rem(heavy - place * held + adapters, adapters).reshape(1)
    column = index.reshape(rows, 1)
    running = finish(places, column, base, up, shrinks, [last], early, jnp.float32, homes, held, light)
    shrinks = [give_back(last, order[-1])]
    return finish(places, column, running, up, shrinks, [], order[-1:], jnp.bfloat16, homes, held, light)


def solution(mesh):
    in_specs = (
        P(("groups", "batch"), "tensor"),
        P(("groups", "batch")),
        P(),
        P("tensor", None),
        P("batch", "tensor", None),
        P("batch", None, "tensor"),
    )
    out_specs = P(("groups", "batch"), "tensor")
    return jax.shard_map(
        on_device, mesh=mesh, in_specs=in_specs, out_specs=out_specs, check_vma=False
    )
```

```python
import functools

import jax
import jax.numpy as jnp
from jax import lax
from jax.experimental import pallas as pl
from jax.experimental.pallas import tpu as pltpu
from jax.sharding import PartitionSpec as P

adapter_scale = 0.5
VMEM_BYTES = 24 * 1024 * 1024
WIDE = pltpu.CompilerParams(vmem_limit_bytes=60 * 1024 * 1024)
VMEM = pl.BlockSpec(memory_space=pltpu.VMEM)
ANY = pl.BlockSpec(memory_space=pl.ANY)
HBM = pl.BlockSpec(memory_space=pltpu.HBM)
SMEM = pl.BlockSpec(memory_space=pltpu.SMEM)
COST = pl.CostEstimate(flops=1, bytes_accessed=1, transcendentals=0)
PARAMS = pltpu.CompilerParams(vmem_limit_bytes=VMEM_BYTES)


def place_rows(index, start, tokens_ref, block_ref):
    local = lax.broadcasted_iota(jnp.int32, (block_ref.shape[0], index.shape[1]), 0)
    choose = (local + start == index).astype(jnp.bfloat16)
    block_ref[...] = jnp.dot(
        choose, tokens_ref[...], preferred_element_type=jnp.float32
    ).astype(jnp.bfloat16)


def route_kernel(
    homes, held, light, place_ref, entry_hbm, request_hbm, index_ref, heavy_ref, entry_ref, request_ref, sems
):
    loads = [
        pltpu.make_async_copy(source, target, sems.at[n])
        for n, (source, target) in enumerate(
            [(request_hbm, request_ref), (entry_hbm, entry_ref)]
        )
    ]
    for load in loads:
        load.start()
    rows = request_ref.shape[0]
    adapters = entry_ref.shape[0]
    span = (held + 1) * light
    earlier = (
        lax.broadcasted_iota(jnp.int32, (rows, rows), 0) < lax.broadcasted_iota(jnp.int32, (rows, rows), 1)
    ).astype(jnp.bfloat16)
    loads[0].wait()
    request = request_ref[...].reshape(1, rows)
    onehot = lax.broadcasted_iota(jnp.int32, (adapters, rows), 0) == request
    before = jnp.dot(onehot.astype(jnp.bfloat16), earlier, preferred_element_type=jnp.float32)
    position = jnp.sum(jnp.where(onehot, before, 0.0), axis=0, keepdims=True).astype(jnp.int32)
    loads[1].wait()
    slot = jnp.zeros_like(position)
    for a in range(adapters):
        slot = jnp.where(request == a, entry_ref[a], slot)
    home = slot // held
    relative = lax.rem(home - place_ref[0] + homes, homes)
    inside = jnp.where(
        position < light, (slot - home * held) * light + position, held * light + position - light
    )
    index = relative * span + inside
    index_ref[...] = index
    heavy = jnp.max(jnp.where(position >= light, slot, 0), axis=1, keepdims=True)
    heavy_ref[...] = jnp.broadcast_to(heavy, heavy_ref.shape)


def pack_kernel(span, shifts, index_ref, tokens_ref, mark_ref, *refs):
    count = len(shifts)
    block_refs, buffer, sems = refs[:count], refs[count], refs[count + 1]
    mark_ref[...] = jnp.zeros_like(mark_ref)
    stores = []
    for n, shift in enumerate(shifts):
        place_rows(index_ref[...], shift * span, tokens_ref, buffer.at[n])
        stores.append(pltpu.make_async_copy(buffer.at[n], block_refs[n], sems.at[n]))
        stores[-1].start()
    for store in stores:
        store.wait()


def entry_places(held):
    return (held + 2) // 2


def shrink_kernel(held, light, rank, value_side, waited, passed, scalar_ref, block_ref, down_ref, *refs):
    passed_refs, out_ref, left_refs = refs[waited : waited + passed], refs[waited + passed], refs[waited + passed + 1 :]
    groups = entry_places(held)

    def product(e):
        if e > held:
            return jnp.zeros((light, 2 * rank), jnp.float32)
        factor = down_ref[e] if e < held else down_ref[scalar_ref[1]]
        value = jnp.dot(
            block_ref[e * light : (e + 1) * light, :], factor, preferred_element_type=jnp.float32
        )
        return value if e < held else jnp.where(scalar_ref[2] == 1, value, 0.0)

    on_value_side = scalar_ref[0] >= value_side
    for g in range(groups):
        first, second = product(g), product(g + groups)
        key = jnp.concatenate([first[:, :rank], second[:, :rank]], axis=1)
        value = jnp.concatenate([first[:, rank:], second[:, rank:]], axis=1)
        out_ref[g * light : (g + 1) * light, :] = jnp.where(on_value_side, value, key)
        out_ref[(groups + g) * light : (groups + g + 1) * light, :] = jnp.where(on_value_side, key, value)
    for source, target in zip(passed_refs, left_refs):
        target[...] = source[...]


def split_pair(value):
    high = value.astype(jnp.bfloat16)
    low = (value - high.astype(jnp.float32)).astype(jnp.bfloat16)
    return high, low


def finish_kernel(homes, held, light, rank, shifts, waited, place_ref, index_ref, base_ref, up_ref, *refs):
    count = len(shifts)
    refs = refs[:count] + refs[count + waited :]
    shrink_refs, out_ref, high_ref, low_ref = refs[:count], refs[count], refs[count + 1], refs[count + 2]
    span = (held + 1) * light
    rows = base_ref.shape[0]
    groups = entry_places(held)
    local = []
    for n, r in enumerate(shifts):
        for e in range(held + 1):
            entry = r * held + e if e < held else place_ref[0]
            g, side = e % groups, e // groups
            high, low = split_pair(
                shrink_refs[n][g * light : (g + 1) * light, side * rank : (side + 1) * rank]
            )
            factor = up_ref[entry]
            delta = jnp.dot(high, factor, preferred_element_type=jnp.float32) + jnp.dot(
                low, factor, preferred_element_type=jnp.float32
            )
            high, low = split_pair(delta)
            start = n * span + e * light
            high_ref[start : start + light, :] = high
            low_ref[start : start + light, :] = low
        local.append(lax.broadcasted_iota(jnp.int32, (rows, span), 1) + r * span == index_ref[...])
    delta = base_ref[...]
    for n in range(count):
        choose = local[n].astype(jnp.bfloat16)
        delta = delta + adapter_scale * (
            jnp.dot(choose, high_ref[n * span : (n + 1) * span, :], preferred_element_type=jnp.float32)
            + jnp.dot(choose, low_ref[n * span : (n + 1) * span, :], preferred_element_type=jnp.float32)
        )
    out_ref[...] = delta.astype(out_ref.dtype)


def finish(scalars, index, base, up, shrinks, after, shifts, dtype, homes, held, light):
    rows, columns = base.shape
    span = (held + 1) * light
    return pl.pallas_call(
        functools.partial(finish_kernel, homes, held, light, up.shape[1], shifts, len(after)),
        out_shape=jax.ShapeDtypeStruct((rows, columns), dtype),
        in_specs=[SMEM] + [VMEM] * (3 + len(shifts)) + [ANY] * len(after),
        out_specs=VMEM,
        scratch_shapes=[pltpu.VMEM((len(shifts) * span, columns), jnp.bfloat16)] * 2,
        compiler_params=PARAMS,
        cost_estimate=COST,
        name="finish",
    )(scalars, index, base, up, *shrinks, *after)


def gate_kernel(*refs):
    pass


def gate(blocks, after):
    return pl.pallas_call(
        gate_kernel,
        out_shape=[jax.ShapeDtypeStruct(b.shape, b.dtype) for b in blocks],
        in_specs=[HBM] * len(blocks) + [ANY] * len(after),
        out_specs=[HBM] * len(blocks),
        input_output_aliases={n: n for n in range(len(blocks))},
        compiler_params=WIDE,
        cost_estimate=COST,
        name="gate",
    )(*blocks, *after)


def gather_up(adapter_up, homes):
    teams = lax.axis_size("groups")
    team = lax.axis_index("groups")
    share = adapter_up.shape[1] // teams
    own = lax.dynamic_slice_in_dim(adapter_up, team * share, share, 1)
    found = [
        lax.ppermute(own, "batch", [(i, (i - r) % homes) for i in range(homes)]) for r in range(1, homes)
    ]
    ordered = jnp.concatenate([own] + found, axis=0)
    shares = [ordered] + [
        lax.ppermute(ordered, "groups", [(i, (i + s) % teams) for i in range(teams)])
        for s in range(1, teams)
    ]
    return jnp.concatenate(
        [
            functools.reduce(
                lambda kept, s: jnp.where(lax.rem(team + teams - s, teams) == part, shares[s], kept),
                range(1, teams),
                shares[0],
            )
            for part in range(teams)
        ],
        axis=1,
    ), found


def base_kernel(waited, block_ref, tokens_ref, weight_ref, *refs):
    refs[waited][...] = jnp.dot(tokens_ref[...], weight_ref[...], preferred_element_type=jnp.float32)


def base_part(tokens, weight, blocks, columns, slab, slabs, after):
    rows, width = tokens.shape[0] // slabs, tokens.shape[1]
    count = blocks.shape[0]
    return pl.pallas_call(
        functools.partial(base_kernel, len(after)),
        out_shape=jax.ShapeDtypeStruct((rows, count * columns), jnp.float32),
        grid_spec=pltpu.PrefetchScalarGridSpec(
            num_scalar_prefetch=1,
            grid=(count,),
            in_specs=[
                pl.BlockSpec((rows, width), lambda j, chosen: (slab, 0)),
                pl.BlockSpec((width, columns), lambda j, chosen: (0, chosen[j])),
            ]
            + [ANY] * len(after),
            out_specs=pl.BlockSpec((rows, columns), lambda j, chosen: (0, j)),
        ),
        compiler_params=PARAMS,
        cost_estimate=COST,
        name="base",
    )(blocks, tokens, weight, *after)


def reduce_base(tokens, weight, piece, pieces, columns, slab, slabs, after):
    keep = [0]
    bit = pieces // 2
    while bit > 1:
        keep = keep + [p + bit for p in keep]
        bit //= 2
    keep = jnp.array(keep, jnp.int32)
    sent = base_part(tokens, weight, piece ^ keep ^ 1, columns, slab, slabs, after)
    kept = base_part(tokens, weight, piece ^ keep, columns, slab, slabs, [sent])
    bit = 1
    while True:
        kept = kept + lax.ppermute(sent, "tensor", [(i, i ^ bit) for i in range(pieces)])
        bit *= 2
        if bit >= pieces:
            return kept
        half = kept.shape[1] // 2
        kept, sent = kept[:, :half], kept[:, half:]


def on_device(tokens, request_adapter, adapter_entry, key_value_weight, adapter_down, adapter_up):
    rows, width = tokens.shape
    adapters = adapter_entry.shape[0]
    held, rank, columns = adapter_up.shape
    value_side = key_value_weight.shape[1] // 2 // columns
    homes = lax.axis_size("batch")
    pieces = lax.axis_size("tensor")
    place = lax.axis_index("batch").astype(jnp.int32)
    piece = lax.axis_index("tensor").astype(jnp.int32)
    light = rows // adapters
    span = (held + 1) * light
    order = sorted(range(1, homes), key=lambda r: (-min(r, homes - r), r))
    block_shape = jax.ShapeDtypeStruct((span, width), jnp.bfloat16)

    up, found = gather_up(adapter_up, homes)
    index, heavy = pl.pallas_call(
        functools.partial(route_kernel, homes, held, light),
        out_shape=[
            jax.ShapeDtypeStruct((1, rows), jnp.int32),
            jax.ShapeDtypeStruct((8, 128), jnp.int32),
        ],
        in_specs=[SMEM, HBM, HBM],
        out_specs=[VMEM] * 2,
        scratch_shapes=[
            pltpu.SMEM(adapter_entry.shape, jnp.int32),
            pltpu.VMEM((rows,), jnp.int32),
            pltpu.SemaphoreType.DMA((2,)),
        ],
        compiler_params=WIDE,
        cost_estimate=COST,
        name="route",
    )(place.reshape(1), adapter_entry, request_adapter)
    def pack(shifts):
        return pl.pallas_call(
            functools.partial(pack_kernel, span, shifts),
            out_shape=[jax.ShapeDtypeStruct((8, 128), jnp.int32)] + [block_shape] * len(shifts),
            in_specs=[VMEM] * 2,
            out_specs=[VMEM] + [HBM] * len(shifts),
            scratch_shapes=[
                pltpu.VMEM((len(shifts), span, width), jnp.bfloat16),
                pltpu.SemaphoreType.DMA((len(shifts),)),
            ],
            compiler_params=WIDE,
            cost_estimate=COST,
            name="pack",
        )(index, tokens)

    def send(block, r):
        return lax.ppermute(block, "batch", [(i, (i + r) % homes) for i in range(homes)])

    packed, own_block, *blocks = pack([0] + order)
    arrived = {0: own_block}
    for r, block in zip(order, gate(blocks, found)):
        arrived[r] = send(block, r)

    heavy = heavy[0, 0]
    heavy_here = (heavy // held == place).astype(jnp.int32)
    scalars = jnp.stack([piece, lax.rem(heavy, held), heavy_here])
    height = entry_places(held) * light

    def shrink(block, after, passed):
        return pl.pallas_call(
            functools.partial(shrink_kernel, held, light, rank, value_side, len(after), len(passed)),
            out_shape=[jax.ShapeDtypeStruct((2 * height, 2 * rank), jnp.float32)]
            + [jax.ShapeDtypeStruct(p.shape, p.dtype) for p in passed],
            in_specs=[SMEM, VMEM, VMEM] + [ANY] * len(after) + [VMEM] * len(passed),
            out_specs=[VMEM] * (1 + len(passed)),
            compiler_params=PARAMS,
            cost_estimate=COST,
            name="shrink",
        )(scalars, block, adapter_down, *after, *passed)

    def combine(value):
        bit = 1
        while bit < pieces // 2:
            value = value + lax.ppermute(value, "tensor", [(i, i ^ bit) for i in range(pieces)])
            bit *= 2
        total = value[:height] + lax.ppermute(value[height:], "tensor", [(i, i ^ bit) for i in range(pieces)])
        return total

    early = order[:-1] + [0]
    totals = []
    after = [packed]
    for r in early:
        (value,) = shrink(arrived[r], after, [])
        totals.append(combine(value))
    slabs = 2
    base = jnp.concatenate(
        [
            reduce_base(tokens, key_value_weight, piece, pieces, columns, slab, slabs, [packed])
            for slab in range(slabs)
        ],
        axis=0,
    )
    value, *totals = shrink(arrived[order[-1]], [], totals)
    last = combine(value)

    def give_back(total, r):
        return lax.ppermute(total, "batch", [(i, (i - r) % homes) for i in range(homes)]) if r else total

    shrinks = [give_back(total, r) for total, r in zip(totals, early)]
    places = lax.rem(heavy - place * held + adapters, adapters).reshape(1)
    column = index.reshape(rows, 1)
    running = finish(places, column, base, up, shrinks, [last], early, jnp.float32, homes, held, light)
    shrinks = [give_back(last, order[-1])]
    return finish(places, column, running, up, shrinks, [], order[-1:], jnp.bfloat16, homes, held, light)


def solution(mesh):
    in_specs = (
        P(("groups", "batch"), "tensor"),
        P(("groups", "batch")),
        P(),
        P("tensor", None),
        P("batch", "tensor", None),
        P("batch", None, "tensor"),
    )
    out_specs = P(("groups", "batch"), "tensor")
    return jax.shard_map(
        on_device, mesh=mesh, in_specs=in_specs, out_specs=out_specs, check_vma=False
    )
```

```python
import functools

import jax
import jax.numpy as jnp
from jax import lax
from jax.experimental import pallas as pl
from jax.experimental.pallas import tpu as pltpu
from jax.sharding import PartitionSpec as P

adapter_scale = 0.5
VMEM_BYTES = 24 * 1024 * 1024
WIDE = pltpu.CompilerParams(vmem_limit_bytes=60 * 1024 * 1024)
VMEM = pl.BlockSpec(memory_space=pltpu.VMEM)
ANY = pl.BlockSpec(memory_space=pl.ANY)
HBM = pl.BlockSpec(memory_space=pltpu.HBM)
SMEM = pl.BlockSpec(memory_space=pltpu.SMEM)
COST = pl.CostEstimate(flops=1, bytes_accessed=1, transcendentals=0)
PARAMS = pltpu.CompilerParams(vmem_limit_bytes=VMEM_BYTES)


def place_rows(index, start, tokens_ref, block_ref):
    local = lax.broadcasted_iota(jnp.int32, (block_ref.shape[0], index.shape[1]), 0)
    choose = (local + start == index).astype(jnp.bfloat16)
    block_ref[...] = jnp.dot(
        choose, tokens_ref[...], preferred_element_type=jnp.float32
    ).astype(jnp.bfloat16)


def route_kernel(
    homes, held, light, place_ref, entry_hbm, request_hbm, index_ref, heavy_ref, entry_ref, request_ref, sems
):
    loads = [
        pltpu.make_async_copy(source, target, sems.at[n])
        for n, (source, target) in enumerate(
            [(request_hbm, request_ref), (entry_hbm, entry_ref)]
        )
    ]
    for load in loads:
        load.start()
    rows = request_ref.shape[0]
    adapters = entry_ref.shape[0]
    span = (held + 1) * light
    earlier = (
        lax.broadcasted_iota(jnp.int32, (rows, rows), 0) < lax.broadcasted_iota(jnp.int32, (rows, rows), 1)
    ).astype(jnp.bfloat16)
    loads[0].wait()
    request = request_ref[...].reshape(1, rows)
    onehot = lax.broadcasted_iota(jnp.int32, (adapters, rows), 0) == request
    before = jnp.dot(onehot.astype(jnp.bfloat16), earlier, preferred_element_type=jnp.float32)
    position = jnp.sum(jnp.where(onehot, before, 0.0), axis=0, keepdims=True).astype(jnp.int32)
    loads[1].wait()
    slot = jnp.zeros_like(position)
    for a in range(adapters):
        slot = jnp.where(request == a, entry_ref[a], slot)
    home = slot // held
    relative = lax.rem(home - place_ref[0] + homes, homes)
    inside = jnp.where(
        position < light, (slot - home * held) * light + position, held * light + position - light
    )
    index = relative * span + inside
    index_ref[...] = index
    heavy = jnp.max(jnp.where(position >= light, slot, 0), axis=1, keepdims=True)
    heavy_ref[...] = jnp.broadcast_to(heavy, heavy_ref.shape)


def pack_kernel(span, shifts, index_ref, tokens_ref, mark_ref, *refs):
    count = len(shifts)
    block_refs, buffer, sems = refs[:count], refs[count], refs[count + 1]
    mark_ref[...] = jnp.zeros_like(mark_ref)
    stores = []
    for n, shift in enumerate(shifts):
        place_rows(index_ref[...], shift * span, tokens_ref, buffer.at[n])
        stores.append(pltpu.make_async_copy(buffer.at[n], block_refs[n], sems.at[n]))
        stores[-1].start()
    for store in stores:
        store.wait()


def entry_places(held):
    return (held + 2) // 2


def shrink_kernel(held, light, rank, value_side, waited, passed, scalar_ref, block_ref, down_ref, *refs):
    passed_refs, out_ref, left_refs = refs[waited : waited + passed], refs[waited + passed], refs[waited + passed + 1 :]
    groups = entry_places(held)

    def product(e):
        if e > held:
            return jnp.zeros((light, 2 * rank), jnp.float32)
        factor = down_ref[e] if e < held else down_ref[scalar_ref[1]]
        value = jnp.dot(
            block_ref[e * light : (e + 1) * light, :], factor, preferred_element_type=jnp.float32
        )
        return value if e < held else jnp.where(scalar_ref[2] == 1, value, 0.0)

    on_value_side = scalar_ref[0] >= value_side
    for g in range(groups):
        first, second = product(g), product(g + groups)
        key = jnp.concatenate([first[:, :rank], second[:, :rank]], axis=1)
        value = jnp.concatenate([first[:, rank:], second[:, rank:]], axis=1)
        out_ref[g * light : (g + 1) * light, :] = jnp.where(on_value_side, value, key)
        out_ref[(groups + g) * light : (groups + g + 1) * light, :] = jnp.where(on_value_side, key, value)
    for source, target in zip(passed_refs, left_refs):
        target[...] = source[...]


def split_pair(value):
    high = value.astype(jnp.bfloat16)
    low = (value - high.astype(jnp.float32)).astype(jnp.bfloat16)
    return high, low


def finish_kernel(homes, held, light, rank, shifts, waited, place_ref, index_ref, base_ref, up_ref, *refs):
    count = len(shifts)
    refs = refs[:count] + refs[count + waited :]
    shrink_refs, out_ref, high_ref, low_ref = refs[:count], refs[count], refs[count + 1], refs[count + 2]
    span = (held + 1) * light
    rows = base_ref.shape[0]
    groups = entry_places(held)
    local = []
    for n, r in enumerate(shifts):
        for e in range(held + 1):
            entry = r * held + e if e < held else place_ref[0]
            g, side = e % groups, e // groups
            high, low = split_pair(
                shrink_refs[n][g * light : (g + 1) * light, side * rank : (side + 1) * rank]
            )
            factor = up_ref[entry]
            delta = jnp.dot(high, factor, preferred_element_type=jnp.float32) + jnp.dot(
                low, factor, preferred_element_type=jnp.float32
            )
            high, low = split_pair(delta)
            start = n * span + e * light
            high_ref[start : start + light, :] = high
            low_ref[start : start + light, :] = low
        local.append(lax.broadcasted_iota(jnp.int32, (rows, span), 1) + r * span == index_ref[...])
    delta = base_ref[...]
    for n in range(count):
        choose = local[n].astype(jnp.bfloat16)
        delta = delta + adapter_scale * (
            jnp.dot(choose, high_ref[n * span : (n + 1) * span, :], preferred_element_type=jnp.float32)
            + jnp.dot(choose, low_ref[n * span : (n + 1) * span, :], preferred_element_type=jnp.float32)
        )
    out_ref[...] = delta.astype(out_ref.dtype)


def finish(scalars, index, base, up, shrinks, after, shifts, dtype, homes, held, light):
    rows, columns = base.shape
    span = (held + 1) * light
    return pl.pallas_call(
        functools.partial(finish_kernel, homes, held, light, up.shape[1], shifts, len(after)),
        out_shape=jax.ShapeDtypeStruct((rows, columns), dtype),
        in_specs=[SMEM] + [VMEM] * (3 + len(shifts)) + [ANY] * len(after),
        out_specs=VMEM,
        scratch_shapes=[pltpu.VMEM((len(shifts) * span, columns), jnp.bfloat16)] * 2,
        compiler_params=PARAMS,
        cost_estimate=COST,
        name="finish",
    )(scalars, index, base, up, *shrinks, *after)


def gate_kernel(waiting, *refs):
    refs[waiting][...] = jnp.zeros_like(refs[waiting])


def gate(blocks, after):
    return pl.pallas_call(
        functools.partial(gate_kernel, len(blocks) + len(after)),
        out_shape=[jax.ShapeDtypeStruct((8, 128), jnp.int32)]
        + [jax.ShapeDtypeStruct(b.shape, b.dtype) for b in blocks],
        in_specs=[HBM] * len(blocks) + [ANY] * len(after),
        out_specs=[VMEM] + [HBM] * len(blocks),
        input_output_aliases={n: n + 1 for n in range(len(blocks))},
        compiler_params=WIDE,
        cost_estimate=COST,
        name="gate",
    )(*blocks, *after)


def gather_up(adapter_up, homes):
    teams = lax.axis_size("groups")
    team = lax.axis_index("groups")
    share = adapter_up.shape[1] // teams
    own = lax.dynamic_slice_in_dim(adapter_up, team * share, share, 1)
    found = [
        lax.ppermute(own, "batch", [(i, (i - r) % homes) for i in range(homes)]) for r in range(1, homes)
    ]
    ordered = jnp.concatenate([own] + found, axis=0)
    shares = [ordered] + [
        lax.ppermute(ordered, "groups", [(i, (i + s) % teams) for i in range(teams)])
        for s in range(1, teams)
    ]
    return jnp.concatenate(
        [
            functools.reduce(
                lambda kept, s: jnp.where(lax.rem(team + teams - s, teams) == part, shares[s], kept),
                range(1, teams),
                shares[0],
            )
            for part in range(teams)
        ],
        axis=1,
    ), found


def base_kernel(waited, block_ref, tokens_ref, weight_ref, *refs):
    refs[waited][...] = jnp.dot(tokens_ref[...], weight_ref[...], preferred_element_type=jnp.float32)


def base_part(tokens, weight, blocks, columns, slab, slabs, after):
    rows, width = tokens.shape[0] // slabs, tokens.shape[1]
    count = blocks.shape[0]
    return pl.pallas_call(
        functools.partial(base_kernel, len(after)),
        out_shape=jax.ShapeDtypeStruct((rows, count * columns), jnp.float32),
        grid_spec=pltpu.PrefetchScalarGridSpec(
            num_scalar_prefetch=1,
            grid=(count,),
            in_specs=[
                pl.BlockSpec((rows, width), lambda j, chosen: (slab, 0)),
                pl.BlockSpec((width, columns), lambda j, chosen: (0, chosen[j])),
            ]
            + [ANY] * len(after),
            out_specs=pl.BlockSpec((rows, columns), lambda j, chosen: (0, j)),
        ),
        compiler_params=PARAMS,
        cost_estimate=COST,
        name="base",
    )(blocks, tokens, weight, *after)


def reduce_base(tokens, weight, piece, pieces, columns, slab, slabs, after):
    keep = [0]
    bit = pieces // 2
    while bit > 1:
        keep = keep + [p + bit for p in keep]
        bit //= 2
    keep = jnp.array(keep, jnp.int32)
    sent = base_part(tokens, weight, piece ^ keep ^ 1, columns, slab, slabs, after)
    kept = base_part(tokens, weight, piece ^ keep, columns, slab, slabs, [sent])
    bit = 1
    while True:
        kept = kept + lax.ppermute(sent, "tensor", [(i, i ^ bit) for i in range(pieces)])
        bit *= 2
        if bit >= pieces:
            return kept
        half = kept.shape[1] // 2
        kept, sent = kept[:, :half], kept[:, half:]


def on_device(tokens, request_adapter, adapter_entry, key_value_weight, adapter_down, adapter_up):
    rows, width = tokens.shape
    adapters = adapter_entry.shape[0]
    held, rank, columns = adapter_up.shape
    value_side = key_value_weight.shape[1] // 2 // columns
    homes = lax.axis_size("batch")
    pieces = lax.axis_size("tensor")
    place = lax.axis_index("batch").astype(jnp.int32)
    piece = lax.axis_index("tensor").astype(jnp.int32)
    light = rows // adapters
    span = (held + 1) * light
    order = sorted(range(1, homes), key=lambda r: (-min(r, homes - r), r))
    block_shape = jax.ShapeDtypeStruct((span, width), jnp.bfloat16)

    up, found = gather_up(adapter_up, homes)
    index, heavy = pl.pallas_call(
        functools.partial(route_kernel, homes, held, light),
        out_shape=[
            jax.ShapeDtypeStruct((1, rows), jnp.int32),
            jax.ShapeDtypeStruct((8, 128), jnp.int32),
        ],
        in_specs=[SMEM, HBM, HBM],
        out_specs=[VMEM] * 2,
        scratch_shapes=[
            pltpu.SMEM(adapter_entry.shape, jnp.int32),
            pltpu.VMEM((rows,), jnp.int32),
            pltpu.SemaphoreType.DMA((2,)),
        ],
        compiler_params=WIDE,
        cost_estimate=COST,
        name="route",
    )(place.reshape(1), adapter_entry, request_adapter)
    def pack(shifts):
        return pl.pallas_call(
            functools.partial(pack_kernel, span, shifts),
            out_shape=[jax.ShapeDtypeStruct((8, 128), jnp.int32)] + [block_shape] * len(shifts),
            in_specs=[VMEM] * 2,
            out_specs=[VMEM] + [HBM] * len(shifts),
            scratch_shapes=[
                pltpu.VMEM((len(shifts), span, width), jnp.bfloat16),
                pltpu.SemaphoreType.DMA((len(shifts),)),
            ],
            compiler_params=WIDE,
            cost_estimate=COST,
            name="pack",
        )(index, tokens)

    def send(block, r):
        return lax.ppermute(block, "batch", [(i, (i + r) % homes) for i in range(homes)])

    packed, own_block, *blocks = pack([0] + order)
    arrived = {0: own_block}
    mark, *blocks = gate(blocks, found)
    for r, block in zip(order, blocks):
        arrived[r] = send(block, r)

    heavy = heavy[0, 0]
    heavy_here = (heavy // held == place).astype(jnp.int32)
    scalars = jnp.stack([piece, lax.rem(heavy, held), heavy_here])
    height = entry_places(held) * light

    def shrink(block, after, passed):
        return pl.pallas_call(
            functools.partial(shrink_kernel, held, light, rank, value_side, len(after), len(passed)),
            out_shape=[jax.ShapeDtypeStruct((2 * height, 2 * rank), jnp.float32)]
            + [jax.ShapeDtypeStruct(p.shape, p.dtype) for p in passed],
            in_specs=[SMEM, VMEM, VMEM] + [ANY] * len(after) + [VMEM] * len(passed),
            out_specs=[VMEM] * (1 + len(passed)),
            compiler_params=PARAMS,
            cost_estimate=COST,
            name="shrink",
        )(scalars, block, adapter_down, *after, *passed)

    def combine(value):
        bit = 1
        while bit < pieces // 2:
            value = value + lax.ppermute(value, "tensor", [(i, i ^ bit) for i in range(pieces)])
            bit *= 2
        total = value[:height] + lax.ppermute(value[height:], "tensor", [(i, i ^ bit) for i in range(pieces)])
        return total

    slabs = 2
    base = jnp.concatenate(
        [
            reduce_base(tokens, key_value_weight, piece, pieces, columns, slab, slabs, [mark])
            for slab in range(slabs)
        ],
        axis=0,
    )
    early = order[:-1] + [0]
    totals = []
    done = [base[:8], base[-8:]]
    for r in early:
        (value,) = shrink(arrived[r], done if r == order[0] else [packed], [])
        totals.append(combine(value))
    value, *totals = shrink(arrived[order[-1]], [], totals)
    last = combine(value)

    def give_back(total, r):
        return lax.ppermute(total, "batch", [(i, (i - r) % homes) for i in range(homes)]) if r else total

    shrinks = [give_back(total, r) for total, r in zip(totals, early)]
    places = lax.rem(heavy - place * held + adapters, adapters).reshape(1)
    column = index.reshape(rows, 1)
    running = finish(places, column, base, up, shrinks, [last], early, jnp.float32, homes, held, light)
    shrinks = [give_back(last, order[-1])]
    return finish(places, column, running, up, shrinks, [], order[-1:], jnp.bfloat16, homes, held, light)


def solution(mesh):
    in_specs = (
        P(("groups", "batch"), "tensor"),
        P(("groups", "batch")),
        P(),
        P("tensor", None),
        P("batch", "tensor", None),
        P("batch", None, "tensor"),
    )
    out_specs = P(("groups", "batch"), "tensor")
    return jax.shard_map(
        on_device, mesh=mesh, in_specs=in_specs, out_specs=out_specs, check_vma=False
    )
```

```python
import functools

import jax
import jax.numpy as jnp
from jax import lax
from jax.experimental import pallas as pl
from jax.experimental.pallas import tpu as pltpu
from jax.sharding import PartitionSpec as P

adapter_scale = 0.5
VMEM_BYTES = 24 * 1024 * 1024
WIDE = pltpu.CompilerParams(vmem_limit_bytes=60 * 1024 * 1024)
VMEM = pl.BlockSpec(memory_space=pltpu.VMEM)
ANY = pl.BlockSpec(memory_space=pl.ANY)
HBM = pl.BlockSpec(memory_space=pltpu.HBM)
SMEM = pl.BlockSpec(memory_space=pltpu.SMEM)
COST = pl.CostEstimate(flops=1, bytes_accessed=1, transcendentals=0)
PARAMS = pltpu.CompilerParams(vmem_limit_bytes=VMEM_BYTES)


def place_rows(index, start, tokens_ref, block_ref):
    local = lax.broadcasted_iota(jnp.int32, (block_ref.shape[0], index.shape[1]), 0)
    choose = (local + start == index).astype(jnp.bfloat16)
    block_ref[...] = jnp.dot(
        choose, tokens_ref[...], preferred_element_type=jnp.float32
    ).astype(jnp.bfloat16)


def route_kernel(
    homes, held, light, place_ref, entry_hbm, request_hbm, index_ref, heavy_ref, entry_ref, request_ref, sems
):
    loads = [
        pltpu.make_async_copy(source, target, sems.at[n])
        for n, (source, target) in enumerate(
            [(request_hbm, request_ref), (entry_hbm, entry_ref)]
        )
    ]
    for load in loads:
        load.start()
    rows = request_ref.shape[0]
    adapters = entry_ref.shape[0]
    span = (held + 1) * light
    earlier = (
        lax.broadcasted_iota(jnp.int32, (rows, rows), 0) < lax.broadcasted_iota(jnp.int32, (rows, rows), 1)
    ).astype(jnp.bfloat16)
    loads[0].wait()
    request = request_ref[...].reshape(1, rows)
    onehot = lax.broadcasted_iota(jnp.int32, (adapters, rows), 0) == request
    before = jnp.dot(onehot.astype(jnp.bfloat16), earlier, preferred_element_type=jnp.float32)
    position = jnp.sum(jnp.where(onehot, before, 0.0), axis=0, keepdims=True).astype(jnp.int32)
    loads[1].wait()
    slot = jnp.zeros_like(position)
    for a in range(adapters):
        slot = jnp.where(request == a, entry_ref[a], slot)
    home = slot // held
    relative = lax.rem(home - place_ref[0] + homes, homes)
    inside = jnp.where(
        position < light, (slot - home * held) * light + position, held * light + position - light
    )
    index = relative * span + inside
    index_ref[...] = index
    heavy = jnp.max(jnp.where(position >= light, slot, 0), axis=1, keepdims=True)
    heavy_ref[...] = jnp.broadcast_to(heavy, heavy_ref.shape)


def pack_kernel(span, shifts, index_ref, tokens_ref, mark_ref, *refs):
    count = len(shifts)
    block_refs, buffer, sems = refs[:count], refs[count], refs[count + 1]
    mark_ref[...] = jnp.zeros_like(mark_ref)
    stores = []
    for n, shift in enumerate(shifts):
        place_rows(index_ref[...], shift * span, tokens_ref, buffer.at[n])
        stores.append(pltpu.make_async_copy(buffer.at[n], block_refs[n], sems.at[n]))
        stores[-1].start()
    for store in stores:
        store.wait()


def entry_places(held):
    return (held + 2) // 2


def shrink_kernel(held, light, rank, value_side, count, waited, passed, scalar_ref, *refs):
    block_refs, down_ref, refs = refs[:count], refs[count], refs[count + 1 + waited :]
    passed_refs, out_ref, left_refs = refs[:passed], refs[passed], refs[passed + 1 :]
    groups = entry_places(held)
    height = groups * light

    def product(e):
        if e > held:
            return jnp.zeros((count * light, 2 * rank), jnp.float32)
        factor = down_ref[e] if e < held else down_ref[scalar_ref[1]]
        rows = [block_ref[e * light : (e + 1) * light, :] for block_ref in block_refs]
        value = jnp.dot(
            jnp.concatenate(rows, axis=0) if count > 1 else rows[0], factor, preferred_element_type=jnp.float32
        )
        return value if e < held else jnp.where(scalar_ref[2] == 1, value, 0.0)

    on_value_side = scalar_ref[0] >= value_side
    for g in range(groups):
        first, second = product(g), product(g + groups)
        key = jnp.concatenate([first[:, :rank], second[:, :rank]], axis=1)
        value = jnp.concatenate([first[:, rank:], second[:, rank:]], axis=1)
        mine, other = jnp.where(on_value_side, value, key), jnp.where(on_value_side, key, value)
        for n in range(count):
            here, start = slice(n * light, (n + 1) * light), n * height + g * light
            out_ref[start : start + light, :] = mine[here]
            out_ref[count * height + start : count * height + start + light, :] = other[here]
    for source, target in zip(passed_refs, left_refs):
        target[...] = source[...]


def split_pair(value):
    high = value.astype(jnp.bfloat16)
    low = (value - high.astype(jnp.float32)).astype(jnp.bfloat16)
    return high, low


def finish_kernel(homes, held, light, rank, shifts, waited, place_ref, index_ref, base_ref, up_ref, *refs):
    count = len(shifts)
    refs = refs[:count] + refs[count + waited :]
    shrink_refs, out_ref, high_ref, low_ref = refs[:count], refs[count], refs[count + 1], refs[count + 2]
    span = (held + 1) * light
    rows = base_ref.shape[0]
    groups = entry_places(held)
    local = []
    for n, r in enumerate(shifts):
        for e in range(held + 1):
            entry = r * held + e if e < held else place_ref[0]
            g, side = e % groups, e // groups
            high, low = split_pair(
                shrink_refs[n][g * light : (g + 1) * light, side * rank : (side + 1) * rank]
            )
            factor = up_ref[entry]
            delta = jnp.dot(high, factor, preferred_element_type=jnp.float32) + jnp.dot(
                low, factor, preferred_element_type=jnp.float32
            )
            high, low = split_pair(delta)
            start = n * span + e * light
            high_ref[start : start + light, :] = high
            low_ref[start : start + light, :] = low
        local.append(lax.broadcasted_iota(jnp.int32, (rows, span), 1) + r * span == index_ref[...])
    delta = base_ref[...]
    for n in range(count):
        choose = local[n].astype(jnp.bfloat16)
        delta = delta + adapter_scale * (
            jnp.dot(choose, high_ref[n * span : (n + 1) * span, :], preferred_element_type=jnp.float32)
            + jnp.dot(choose, low_ref[n * span : (n + 1) * span, :], preferred_element_type=jnp.float32)
        )
    out_ref[...] = delta.astype(out_ref.dtype)


def finish(scalars, index, base, up, shrinks, after, shifts, dtype, homes, held, light):
    rows, columns = base.shape
    span = (held + 1) * light
    return pl.pallas_call(
        functools.partial(finish_kernel, homes, held, light, up.shape[1], shifts, len(after)),
        out_shape=jax.ShapeDtypeStruct((rows, columns), dtype),
        in_specs=[SMEM] + [VMEM] * (3 + len(shifts)) + [ANY] * len(after),
        out_specs=VMEM,
        scratch_shapes=[pltpu.VMEM((len(shifts) * span, columns), jnp.bfloat16)] * 2,
        compiler_params=PARAMS,
        cost_estimate=COST,
        name="finish",
    )(scalars, index, base, up, *shrinks, *after)


def gate_kernel(waiting, *refs):
    refs[waiting][...] = jnp.zeros_like(refs[waiting])


def gate(blocks, after):
    return pl.pallas_call(
        functools.partial(gate_kernel, len(blocks) + len(after)),
        out_shape=[jax.ShapeDtypeStruct((8, 128), jnp.int32)]
        + [jax.ShapeDtypeStruct(b.shape, b.dtype) for b in blocks],
        in_specs=[HBM] * len(blocks) + [ANY] * len(after),
        out_specs=[VMEM] + [HBM] * len(blocks),
        input_output_aliases={n: n + 1 for n in range(len(blocks))},
        compiler_params=WIDE,
        cost_estimate=COST,
        name="gate",
    )(*blocks, *after)


def gather_up(adapter_up, homes):
    teams = lax.axis_size("groups")
    team = lax.axis_index("groups")
    share = adapter_up.shape[1] // teams
    own = lax.dynamic_slice_in_dim(adapter_up, team * share, share, 1)
    found = [
        lax.ppermute(own, "batch", [(i, (i - r) % homes) for i in range(homes)]) for r in range(1, homes)
    ]
    ordered = jnp.concatenate([own] + found, axis=0)
    shares = [ordered] + [
        lax.ppermute(ordered, "groups", [(i, (i + s) % teams) for i in range(teams)])
        for s in range(1, teams)
    ]
    return jnp.concatenate(
        [
            functools.reduce(
                lambda kept, s: jnp.where(lax.rem(team + teams - s, teams) == part, shares[s], kept),
                range(1, teams),
                shares[0],
            )
            for part in range(teams)
        ],
        axis=1,
    ), found


def base_kernel(waited, block_ref, tokens_ref, weight_ref, *refs):
    refs[waited][...] = jnp.dot(tokens_ref[...], weight_ref[...], preferred_element_type=jnp.float32)


def base_part(tokens, weight, blocks, columns, slab, slabs, after):
    rows, width = tokens.shape[0] // slabs, tokens.shape[1]
    count = blocks.shape[0]
    return pl.pallas_call(
        functools.partial(base_kernel, len(after)),
        out_shape=jax.ShapeDtypeStruct((rows, count * columns), jnp.float32),
        grid_spec=pltpu.PrefetchScalarGridSpec(
            num_scalar_prefetch=1,
            grid=(count,),
            in_specs=[
                pl.BlockSpec((rows, width), lambda j, chosen: (slab, 0)),
                pl.BlockSpec((width, columns), lambda j, chosen: (0, chosen[j])),
            ]
            + [ANY] * len(after),
            out_specs=pl.BlockSpec((rows, columns), lambda j, chosen: (0, j)),
        ),
        compiler_params=WIDE,
        cost_estimate=COST,
        name="base",
    )(blocks, tokens, weight, *after)


def reduce_base(tokens, weight, piece, pieces, columns, slab, slabs, after):
    keep = [0]
    bit = pieces // 2
    while bit > 1:
        keep = keep + [p + bit for p in keep]
        bit //= 2
    keep = jnp.array(keep, jnp.int32)
    sent = base_part(tokens, weight, piece ^ keep ^ 1, columns, slab, slabs, after)
    kept = base_part(tokens, weight, piece ^ keep, columns, slab, slabs, [sent])
    bit = 1
    while True:
        kept = kept + lax.ppermute(sent, "tensor", [(i, i ^ bit) for i in range(pieces)])
        bit *= 2
        if bit >= pieces:
            return kept
        half = kept.shape[1] // 2
        kept, sent = kept[:, :half], kept[:, half:]


def on_device(tokens, request_adapter, adapter_entry, key_value_weight, adapter_down, adapter_up):
    rows, width = tokens.shape
    adapters = adapter_entry.shape[0]
    held, rank, columns = adapter_up.shape
    value_side = key_value_weight.shape[1] // 2 // columns
    homes = lax.axis_size("batch")
    pieces = lax.axis_size("tensor")
    place = lax.axis_index("batch").astype(jnp.int32)
    piece = lax.axis_index("tensor").astype(jnp.int32)
    light = rows // adapters
    span = (held + 1) * light
    order = sorted(range(1, homes), key=lambda r: (-min(r, homes - r), r))
    block_shape = jax.ShapeDtypeStruct((span, width), jnp.bfloat16)

    up, found = gather_up(adapter_up, homes)
    index, heavy = pl.pallas_call(
        functools.partial(route_kernel, homes, held, light),
        out_shape=[
            jax.ShapeDtypeStruct((1, rows), jnp.int32),
            jax.ShapeDtypeStruct((8, 128), jnp.int32),
        ],
        in_specs=[SMEM, HBM, HBM],
        out_specs=[VMEM] * 2,
        scratch_shapes=[
            pltpu.SMEM(adapter_entry.shape, jnp.int32),
            pltpu.VMEM((rows,), jnp.int32),
            pltpu.SemaphoreType.DMA((2,)),
        ],
        compiler_params=WIDE,
        cost_estimate=COST,
        name="route",
    )(place.reshape(1), adapter_entry, request_adapter)
    def pack(shifts):
        return pl.pallas_call(
            functools.partial(pack_kernel, span, shifts),
            out_shape=[jax.ShapeDtypeStruct((8, 128), jnp.int32)] + [block_shape] * len(shifts),
            in_specs=[VMEM] * 2,
            out_specs=[VMEM] + [HBM] * len(shifts),
            scratch_shapes=[
                pltpu.VMEM((len(shifts), span, width), jnp.bfloat16),
                pltpu.SemaphoreType.DMA((len(shifts),)),
            ],
            compiler_params=WIDE,
            cost_estimate=COST,
            name="pack",
        )(index, tokens)

    def send(block, r):
        return lax.ppermute(block, "batch", [(i, (i + r) % homes) for i in range(homes)])

    packed, own_block, *blocks = pack([0] + order)
    arrived = {0: own_block}
    mark, *blocks = gate(blocks, found)
    for r, block in zip(order, blocks):
        arrived[r] = send(block, r)

    heavy = heavy[0, 0]
    heavy_here = (heavy // held == place).astype(jnp.int32)
    scalars = jnp.stack([piece, lax.rem(heavy, held), heavy_here])
    height = entry_places(held) * light

    def shrink(blocks, after, passed):
        return pl.pallas_call(
            functools.partial(
                shrink_kernel, held, light, rank, value_side, len(blocks), len(after), len(passed)
            ),
            out_shape=[jax.ShapeDtypeStruct((2 * len(blocks) * height, 2 * rank), jnp.float32)]
            + [jax.ShapeDtypeStruct(p.shape, p.dtype) for p in passed],
            in_specs=[SMEM] + [VMEM] * (len(blocks) + 1) + [ANY] * len(after) + [VMEM] * len(passed),
            out_specs=[VMEM] * (1 + len(passed)),
            compiler_params=PARAMS,
            cost_estimate=COST,
            name="shrink",
        )(scalars, *blocks, adapter_down, *after, *passed)

    def combine(value):
        bit, half = 1, value.shape[0] // 2
        while bit < pieces // 2:
            value = value + lax.ppermute(value, "tensor", [(i, i ^ bit) for i in range(pieces)])
            bit *= 2
        return value[:half] + lax.ppermute(value[half:], "tensor", [(i, i ^ bit) for i in range(pieces)])

    slabs = 2
    base = jnp.concatenate(
        [
            reduce_base(tokens, key_value_weight, piece, pieces, columns, slab, slabs, [mark])
            for slab in range(slabs)
        ],
        axis=0,
    )
    late = order[-2:]
    early = order[:-2] + [0]
    totals = []
    for r in early:
        (value,) = shrink([arrived[r]], [packed], [])
        totals.append(combine(value))
    value, *totals = shrink([arrived[r] for r in late], [base[:8], base[-8:]], totals)
    last = combine(value)

    def give_back(total, r):
        return lax.ppermute(total, "batch", [(i, (i - r) % homes) for i in range(homes)]) if r else total

    shrinks = [give_back(total, r) for total, r in zip(totals, early)]
    places = lax.rem(heavy - place * held + adapters, adapters).reshape(1)
    column = index.reshape(rows, 1)
    running = finish(places, column, base, up, shrinks, [last], early, jnp.float32, homes, held, light)
    shrinks = [give_back(last[n * height : (n + 1) * height], r) for n, r in enumerate(late)]
    return finish(places, column, running, up, shrinks, [], late, jnp.bfloat16, homes, held, light)


def solution(mesh):
    in_specs = (
        P(("groups", "batch"), "tensor"),
        P(("groups", "batch")),
        P(),
        P("tensor", None),
        P("batch", "tensor", None),
        P("batch", None, "tensor"),
    )
    out_specs = P(("groups", "batch"), "tensor")
    return jax.shard_map(
        on_device, mesh=mesh, in_specs=in_specs, out_specs=out_specs, check_vma=False
    )
```

```python
import functools

import jax
import jax.numpy as jnp
from jax import lax
from jax.experimental import pallas as pl
from jax.experimental.pallas import tpu as pltpu
from jax.sharding import PartitionSpec as P

adapter_scale = 0.5
VMEM_BYTES = 24 * 1024 * 1024
WIDE = pltpu.CompilerParams(vmem_limit_bytes=60 * 1024 * 1024)
VMEM = pl.BlockSpec(memory_space=pltpu.VMEM)
ANY = pl.BlockSpec(memory_space=pl.ANY)
HBM = pl.BlockSpec(memory_space=pltpu.HBM)
SMEM = pl.BlockSpec(memory_space=pltpu.SMEM)
COST = pl.CostEstimate(flops=1, bytes_accessed=1, transcendentals=0)
PARAMS = pltpu.CompilerParams(vmem_limit_bytes=VMEM_BYTES)


def place_rows(index, start, tokens_ref, block_ref):
    local = lax.broadcasted_iota(jnp.int32, (block_ref.shape[0], index.shape[1]), 0)
    choose = (local + start == index).astype(jnp.bfloat16)
    block_ref[...] = jnp.dot(
        choose, tokens_ref[...], preferred_element_type=jnp.float32
    ).astype(jnp.bfloat16)


def route_kernel(
    homes, held, light, place_ref, entry_hbm, request_hbm, index_ref, heavy_ref, entry_ref, request_ref, sems
):
    loads = [
        pltpu.make_async_copy(source, target, sems.at[n])
        for n, (source, target) in enumerate(
            [(request_hbm, request_ref), (entry_hbm, entry_ref)]
        )
    ]
    for load in loads:
        load.start()
    rows = request_ref.shape[0]
    adapters = entry_ref.shape[0]
    span = (held + 1) * light
    earlier = (
        lax.broadcasted_iota(jnp.int32, (rows, rows), 0) < lax.broadcasted_iota(jnp.int32, (rows, rows), 1)
    ).astype(jnp.bfloat16)
    loads[0].wait()
    request = request_ref[...].reshape(1, rows)
    onehot = lax.broadcasted_iota(jnp.int32, (adapters, rows), 0) == request
    before = jnp.dot(onehot.astype(jnp.bfloat16), earlier, preferred_element_type=jnp.float32)
    position = jnp.sum(jnp.where(onehot, before, 0.0), axis=0, keepdims=True).astype(jnp.int32)
    loads[1].wait()
    slot = jnp.zeros_like(position)
    for a in range(adapters):
        slot = jnp.where(request == a, entry_ref[a], slot)
    home = slot // held
    relative = lax.rem(home - place_ref[0] + homes, homes)
    inside = jnp.where(
        position < light, (slot - home * held) * light + position, held * light + position - light
    )
    index = relative * span + inside
    index_ref[...] = index
    heavy = jnp.max(jnp.where(position >= light, slot, 0), axis=1, keepdims=True)
    heavy_ref[...] = jnp.broadcast_to(heavy, heavy_ref.shape)


def pack_kernel(span, shifts, index_ref, tokens_ref, mark_ref, *refs):
    count = len(shifts)
    block_refs, buffer, sems = refs[:count], refs[count], refs[count + 1]
    mark_ref[...] = jnp.zeros_like(mark_ref)
    stores = []
    for n, shift in enumerate(shifts):
        place_rows(index_ref[...], shift * span, tokens_ref, buffer.at[n])
        stores.append(pltpu.make_async_copy(buffer.at[n], block_refs[n], sems.at[n]))
        stores[-1].start()
    for store in stores:
        store.wait()


def entry_places(held):
    return (held + 2) // 2


def shrink_kernel(held, light, rank, value_side, count, waited, passed, scalar_ref, *refs):
    block_refs, down_ref, refs = refs[:count], refs[count], refs[count + 1 + waited :]
    passed_refs, out_ref, left_refs = refs[:passed], refs[passed], refs[passed + 1 :]
    groups = entry_places(held)
    height = groups * light

    def product(e):
        if e > held:
            return jnp.zeros((count * light, 2 * rank), jnp.float32)
        factor = down_ref[e] if e < held else down_ref[scalar_ref[1]]
        rows = [block_ref[e * light : (e + 1) * light, :] for block_ref in block_refs]
        value = jnp.dot(
            jnp.concatenate(rows, axis=0) if count > 1 else rows[0], factor, preferred_element_type=jnp.float32
        )
        return value if e < held else jnp.where(scalar_ref[2] == 1, value, 0.0)

    on_value_side = scalar_ref[0] >= value_side
    for g in range(groups):
        first, second = product(g), product(g + groups)
        key = jnp.concatenate([first[:, :rank], second[:, :rank]], axis=1)
        value = jnp.concatenate([first[:, rank:], second[:, rank:]], axis=1)
        mine, other = jnp.where(on_value_side, value, key), jnp.where(on_value_side, key, value)
        for n in range(count):
            here, start = slice(n * light, (n + 1) * light), n * height + g * light
            out_ref[start : start + light, :] = mine[here]
            out_ref[count * height + start : count * height + start + light, :] = other[here]
    for source, target in zip(passed_refs, left_refs):
        target[...] = source[...]


def split_pair(value):
    high = value.astype(jnp.bfloat16)
    low = (value - high.astype(jnp.float32)).astype(jnp.bfloat16)
    return high, low


def finish_kernel(homes, held, light, rank, shifts, waited, place_ref, index_ref, base_ref, up_ref, *refs):
    count = len(shifts)
    refs = refs[:count] + refs[count + waited :]
    shrink_refs, out_ref, high_ref, low_ref = refs[:count], refs[count], refs[count + 1], refs[count + 2]
    span = (held + 1) * light
    rows = base_ref.shape[0]
    groups = entry_places(held)
    local = []
    for n, r in enumerate(shifts):
        for e in range(held + 1):
            entry = r * held + e if e < held else place_ref[0]
            g, side = e % groups, e // groups
            high, low = split_pair(
                shrink_refs[n][g * light : (g + 1) * light, side * rank : (side + 1) * rank]
            )
            factor = up_ref[entry]
            delta = jnp.dot(high, factor, preferred_element_type=jnp.float32) + jnp.dot(
                low, factor, preferred_element_type=jnp.float32
            )
            high, low = split_pair(delta)
            start = n * span + e * light
            high_ref[start : start + light, :] = high
            low_ref[start : start + light, :] = low
        local.append(lax.broadcasted_iota(jnp.int32, (rows, span), 1) + r * span == index_ref[...])
    delta = base_ref[...]
    for n in range(count):
        choose = local[n].astype(jnp.bfloat16)
        delta = delta + adapter_scale * (
            jnp.dot(choose, high_ref[n * span : (n + 1) * span, :], preferred_element_type=jnp.float32)
            + jnp.dot(choose, low_ref[n * span : (n + 1) * span, :], preferred_element_type=jnp.float32)
        )
    out_ref[...] = delta.astype(out_ref.dtype)


def finish(scalars, index, base, up, shrinks, after, shifts, dtype, homes, held, light):
    rows, columns = base.shape
    span = (held + 1) * light
    return pl.pallas_call(
        functools.partial(finish_kernel, homes, held, light, up.shape[1], shifts, len(after)),
        out_shape=jax.ShapeDtypeStruct((rows, columns), dtype),
        in_specs=[SMEM] + [VMEM] * (3 + len(shifts)) + [ANY] * len(after),
        out_specs=VMEM,
        scratch_shapes=[pltpu.VMEM((len(shifts) * span, columns), jnp.bfloat16)] * 2,
        compiler_params=PARAMS,
        cost_estimate=COST,
        name="finish",
    )(scalars, index, base, up, *shrinks, *after)


def gate_kernel(waiting, *refs):
    refs[waiting][...] = jnp.zeros_like(refs[waiting])


def gate(blocks, after):
    return pl.pallas_call(
        functools.partial(gate_kernel, len(blocks) + len(after)),
        out_shape=[jax.ShapeDtypeStruct((8, 128), jnp.int32)]
        + [jax.ShapeDtypeStruct(b.shape, b.dtype) for b in blocks],
        in_specs=[HBM] * len(blocks) + [ANY] * len(after),
        out_specs=[VMEM] + [HBM] * len(blocks),
        input_output_aliases={n: n + 1 for n in range(len(blocks))},
        compiler_params=WIDE,
        cost_estimate=COST,
        name="gate",
    )(*blocks, *after)


def gather_up(adapter_up, homes):
    teams = lax.axis_size("groups")
    team = lax.axis_index("groups")
    share = adapter_up.shape[1] // teams
    own = lax.dynamic_slice_in_dim(adapter_up, team * share, share, 1)
    found = [
        lax.ppermute(own, "batch", [(i, (i - r) % homes) for i in range(homes)]) for r in range(1, homes)
    ]
    ordered = jnp.concatenate([own] + found, axis=0)
    shares = [ordered] + [
        lax.ppermute(ordered, "groups", [(i, (i + s) % teams) for i in range(teams)])
        for s in range(1, teams)
    ]
    return jnp.concatenate(
        [
            functools.reduce(
                lambda kept, s: jnp.where(lax.rem(team + teams - s, teams) == part, shares[s], kept),
                range(1, teams),
                shares[0],
            )
            for part in range(teams)
        ],
        axis=1,
    ), found


def base_kernel(waited, block_ref, tokens_ref, weight_ref, *refs):
    refs[waited][...] = jnp.dot(tokens_ref[...], weight_ref[...], preferred_element_type=jnp.float32)


def base_part(tokens, weight, blocks, columns, slab, slabs, after):
    rows, width = tokens.shape[0] // slabs, tokens.shape[1]
    count = blocks.shape[0]
    return pl.pallas_call(
        functools.partial(base_kernel, len(after)),
        out_shape=jax.ShapeDtypeStruct((rows, count * columns), jnp.float32),
        grid_spec=pltpu.PrefetchScalarGridSpec(
            num_scalar_prefetch=1,
            grid=(count,),
            in_specs=[
                pl.BlockSpec((rows, width), lambda j, chosen: (slab, 0)),
                pl.BlockSpec((width, columns), lambda j, chosen: (0, chosen[j])),
            ]
            + [ANY] * len(after),
            out_specs=pl.BlockSpec((rows, columns), lambda j, chosen: (0, j)),
        ),
        compiler_params=PARAMS,
        cost_estimate=COST,
        name="base",
    )(blocks, tokens, weight, *after)


def reduce_base(tokens, weight, piece, pieces, columns, slab, slabs, after):
    keep = [0]
    bit = pieces // 2
    while bit > 1:
        keep = keep + [p + bit for p in keep]
        bit //= 2
    keep = jnp.array(keep, jnp.int32)
    sent = base_part(tokens, weight, piece ^ keep ^ 1, columns, slab, slabs, after)
    kept = base_part(tokens, weight, piece ^ keep, columns, slab, slabs, [sent])
    bit, first = 1, None
    while True:
        kept = kept + lax.ppermute(sent, "tensor", [(i, i ^ bit) for i in range(pieces)])
        first = kept[:8] if first is None else first
        bit *= 2
        if bit >= pieces:
            return kept, first
        half = kept.shape[1] // 2
        kept, sent = kept[:, :half], kept[:, half:]


def on_device(tokens, request_adapter, adapter_entry, key_value_weight, adapter_down, adapter_up):
    rows, width = tokens.shape
    adapters = adapter_entry.shape[0]
    held, rank, columns = adapter_up.shape
    value_side = key_value_weight.shape[1] // 2 // columns
    homes = lax.axis_size("batch")
    pieces = lax.axis_size("tensor")
    place = lax.axis_index("batch").astype(jnp.int32)
    piece = lax.axis_index("tensor").astype(jnp.int32)
    light = rows // adapters
    span = (held + 1) * light
    order = sorted(range(1, homes), key=lambda r: (-min(r, homes - r), r))
    block_shape = jax.ShapeDtypeStruct((span, width), jnp.bfloat16)

    up, found = gather_up(adapter_up, homes)
    index, heavy = pl.pallas_call(
        functools.partial(route_kernel, homes, held, light),
        out_shape=[
            jax.ShapeDtypeStruct((1, rows), jnp.int32),
            jax.ShapeDtypeStruct((8, 128), jnp.int32),
        ],
        in_specs=[SMEM, HBM, HBM],
        out_specs=[VMEM] * 2,
        scratch_shapes=[
            pltpu.SMEM(adapter_entry.shape, jnp.int32),
            pltpu.VMEM((rows,), jnp.int32),
            pltpu.SemaphoreType.DMA((2,)),
        ],
        compiler_params=WIDE,
        cost_estimate=COST,
        name="route",
    )(place.reshape(1), adapter_entry, request_adapter)
    def pack(shifts):
        return pl.pallas_call(
            functools.partial(pack_kernel, span, shifts),
            out_shape=[jax.ShapeDtypeStruct((8, 128), jnp.int32)] + [block_shape] * len(shifts),
            in_specs=[VMEM] * 2,
            out_specs=[VMEM] + [HBM] * len(shifts),
            scratch_shapes=[
                pltpu.VMEM((len(shifts), span, width), jnp.bfloat16),
                pltpu.SemaphoreType.DMA((len(shifts),)),
            ],
            compiler_params=WIDE,
            cost_estimate=COST,
            name="pack",
        )(index, tokens)

    def send(block, r):
        return lax.ppermute(block, "batch", [(i, (i + r) % homes) for i in range(homes)])

    packed, own_block, *blocks = pack([0] + order)
    arrived = {0: own_block}
    mark, *blocks = gate(blocks, found)
    for r, block in zip(order, blocks):
        arrived[r] = send(block, r)

    heavy = heavy[0, 0]
    heavy_here = (heavy // held == place).astype(jnp.int32)
    scalars = jnp.stack([piece, lax.rem(heavy, held), heavy_here])
    height = entry_places(held) * light

    def shrink(blocks, after, passed):
        return pl.pallas_call(
            functools.partial(
                shrink_kernel, held, light, rank, value_side, len(blocks), len(after), len(passed)
            ),
            out_shape=[jax.ShapeDtypeStruct((2 * len(blocks) * height, 2 * rank), jnp.float32)]
            + [jax.ShapeDtypeStruct(p.shape, p.dtype) for p in passed],
            in_specs=[SMEM] + [VMEM] * (len(blocks) + 1) + [ANY] * len(after) + [VMEM] * len(passed),
            out_specs=[VMEM] * (1 + len(passed)),
            compiler_params=PARAMS,
            cost_estimate=COST,
            name="shrink",
        )(scalars, *blocks, adapter_down, *after, *passed)

    def combine(value):
        bit, half = 1, value.shape[0] // 2
        while bit < pieces // 2:
            value = value + lax.ppermute(value, "tensor", [(i, i ^ bit) for i in range(pieces)])
            bit *= 2
        return value[:half] + lax.ppermute(value[half:], "tensor", [(i, i ^ bit) for i in range(pieces)])

    slabs = 2
    slab_sums = [
        reduce_base(tokens, key_value_weight, piece, pieces, columns, slab, slabs, [mark])
        for slab in range(slabs)
    ]
    base = jnp.concatenate([total for total, _ in slab_sums], axis=0)
    begun = [first for _, first in slab_sums]
    late = order[-2:]
    early = order[:-2] + [0]
    totals = []
    for r in early:
        (value,) = shrink([arrived[r]], begun if r else [packed], [])
        totals.append(combine(value))
    value, *totals = shrink([arrived[r] for r in late], [base[:8], base[-8:]], totals)
    last = combine(value)

    def give_back(total, r):
        return lax.ppermute(total, "batch", [(i, (i - r) % homes) for i in range(homes)]) if r else total

    shrinks = [give_back(total, r) for total, r in zip(totals, early)]
    places = lax.rem(heavy - place * held + adapters, adapters).reshape(1)
    column = index.reshape(rows, 1)
    running = finish(places, column, base, up, shrinks, [last], early, jnp.float32, homes, held, light)
    shrinks = [give_back(last[n * height : (n + 1) * height], r) for n, r in enumerate(late)]
    return finish(places, column, running, up, shrinks, [], late, jnp.bfloat16, homes, held, light)


def solution(mesh):
    in_specs = (
        P(("groups", "batch"), "tensor"),
        P(("groups", "batch")),
        P(),
        P("tensor", None),
        P("batch", "tensor", None),
        P("batch", None, "tensor"),
    )
    out_specs = P(("groups", "batch"), "tensor")
    return jax.shard_map(
        on_device, mesh=mesh, in_specs=in_specs, out_specs=out_specs, check_vma=False
    )
```

```python
import functools

import jax
import jax.numpy as jnp
from jax import lax
from jax.experimental import pallas as pl
from jax.experimental.pallas import tpu as pltpu
from jax.sharding import PartitionSpec as P

adapter_scale = 0.5
VMEM_BYTES = 24 * 1024 * 1024
WIDE = pltpu.CompilerParams(vmem_limit_bytes=60 * 1024 * 1024)
VMEM = pl.BlockSpec(memory_space=pltpu.VMEM)
ANY = pl.BlockSpec(memory_space=pl.ANY)
HBM = pl.BlockSpec(memory_space=pltpu.HBM)
SMEM = pl.BlockSpec(memory_space=pltpu.SMEM)
COST = pl.CostEstimate(flops=1, bytes_accessed=1, transcendentals=0)
PARAMS = pltpu.CompilerParams(vmem_limit_bytes=VMEM_BYTES)


def place_rows(index, start, tokens_ref, block_ref):
    local = lax.broadcasted_iota(jnp.int32, (block_ref.shape[0], index.shape[1]), 0)
    choose = (local + start == index).astype(jnp.bfloat16)
    block_ref[...] = jnp.dot(
        choose, tokens_ref[...], preferred_element_type=jnp.float32
    ).astype(jnp.bfloat16)


def route_kernel(
    homes, held, light, place_ref, entry_hbm, request_hbm, index_ref, heavy_ref, entry_ref, request_ref, sems
):
    loads = [
        pltpu.make_async_copy(source, target, sems.at[n])
        for n, (source, target) in enumerate(
            [(request_hbm, request_ref), (entry_hbm, entry_ref)]
        )
    ]
    for load in loads:
        load.start()
    rows = request_ref.shape[0]
    adapters = entry_ref.shape[0]
    span = (held + 1) * light
    earlier = (
        lax.broadcasted_iota(jnp.int32, (rows, rows), 0) < lax.broadcasted_iota(jnp.int32, (rows, rows), 1)
    ).astype(jnp.bfloat16)
    loads[0].wait()
    request = request_ref[...].reshape(1, rows)
    onehot = lax.broadcasted_iota(jnp.int32, (adapters, rows), 0) == request
    before = jnp.dot(onehot.astype(jnp.bfloat16), earlier, preferred_element_type=jnp.float32)
    position = jnp.sum(jnp.where(onehot, before, 0.0), axis=0, keepdims=True).astype(jnp.int32)
    loads[1].wait()
    slot = jnp.zeros_like(position)
    for a in range(adapters):
        slot = jnp.where(request == a, entry_ref[a], slot)
    home = slot // held
    relative = lax.rem(home - place_ref[0] + homes, homes)
    inside = jnp.where(
        position < light, (slot - home * held) * light + position, held * light + position - light
    )
    index = relative * span + inside
    index_ref[...] = index
    heavy = jnp.max(jnp.where(position >= light, slot, 0), axis=1, keepdims=True)
    heavy_ref[...] = jnp.broadcast_to(heavy, heavy_ref.shape)


def pack_kernel(span, shifts, index_ref, tokens_ref, mark_ref, *refs):
    count = len(shifts)
    block_refs, buffer, sems = refs[:count], refs[count], refs[count + 1]
    mark_ref[...] = jnp.zeros_like(mark_ref)
    stores = []
    for n, shift in enumerate(shifts):
        place_rows(index_ref[...], shift * span, tokens_ref, buffer.at[n])
        stores.append(pltpu.make_async_copy(buffer.at[n], block_refs[n], sems.at[n]))
        stores[-1].start()
    for store in stores:
        store.wait()


def entry_places(held):
    return (held + 2) // 2


def shrink_kernel(held, light, rank, value_side, count, waited, passed, scalar_ref, *refs):
    block_refs, down_ref, refs = refs[:count], refs[count], refs[count + 1 + waited :]
    passed_refs, out_ref, left_refs = refs[:passed], refs[passed], refs[passed + 1 :]
    groups = entry_places(held)
    height = groups * light

    def product(e):
        if e > held:
            return jnp.zeros((count * light, 2 * rank), jnp.float32)
        factor = down_ref[e] if e < held else down_ref[scalar_ref[1]]
        rows = [block_ref[e * light : (e + 1) * light, :] for block_ref in block_refs]
        value = jnp.dot(
            jnp.concatenate(rows, axis=0) if count > 1 else rows[0], factor, preferred_element_type=jnp.float32
        )
        return value if e < held else jnp.where(scalar_ref[2] == 1, value, 0.0)

    on_value_side = scalar_ref[0] >= value_side
    for g in range(groups):
        first, second = product(g), product(g + groups)
        key = jnp.concatenate([first[:, :rank], second[:, :rank]], axis=1)
        value = jnp.concatenate([first[:, rank:], second[:, rank:]], axis=1)
        mine, other = jnp.where(on_value_side, value, key), jnp.where(on_value_side, key, value)
        for n in range(count):
            here, start = slice(n * light, (n + 1) * light), n * height + g * light
            out_ref[start : start + light, :] = mine[here]
            out_ref[count * height + start : count * height + start + light, :] = other[here]
    for source, target in zip(passed_refs, left_refs):
        target[...] = source[...]


def split_pair(value):
    high = value.astype(jnp.bfloat16)
    low = (value - high.astype(jnp.float32)).astype(jnp.bfloat16)
    return high, low


def finish_kernel(homes, held, light, rank, shifts, waited, place_ref, index_ref, base_ref, up_ref, *refs):
    count = len(shifts)
    refs = refs[:count] + refs[count + waited :]
    shrink_refs, out_ref, high_ref, low_ref = refs[:count], refs[count], refs[count + 1], refs[count + 2]
    span = (held + 1) * light
    rows = base_ref.shape[0]
    groups = entry_places(held)
    local = []
    for n, r in enumerate(shifts):
        for e in range(held + 1):
            entry = r * held + e if e < held else place_ref[0]
            g, side = e % groups, e // groups
            high, low = split_pair(
                shrink_refs[n][g * light : (g + 1) * light, side * rank : (side + 1) * rank]
            )
            factor = up_ref[entry]
            delta = jnp.dot(high, factor, preferred_element_type=jnp.float32) + jnp.dot(
                low, factor, preferred_element_type=jnp.float32
            )
            high, low = split_pair(delta)
            start = n * span + e * light
            high_ref[start : start + light, :] = high
            low_ref[start : start + light, :] = low
        local.append(lax.broadcasted_iota(jnp.int32, (rows, span), 1) + r * span == index_ref[...])
    delta = base_ref[...]
    for n in range(count):
        choose = local[n].astype(jnp.bfloat16)
        delta = delta + adapter_scale * (
            jnp.dot(choose, high_ref[n * span : (n + 1) * span, :], preferred_element_type=jnp.float32)
            + jnp.dot(choose, low_ref[n * span : (n + 1) * span, :], preferred_element_type=jnp.float32)
        )
    out_ref[...] = delta.astype(out_ref.dtype)


def finish(scalars, index, base, up, shrinks, after, shifts, dtype, homes, held, light):
    rows, columns = base.shape
    span = (held + 1) * light
    return pl.pallas_call(
        functools.partial(finish_kernel, homes, held, light, up.shape[1], shifts, len(after)),
        out_shape=jax.ShapeDtypeStruct((rows, columns), dtype),
        in_specs=[SMEM] + [VMEM] * (3 + len(shifts)) + [ANY] * len(after),
        out_specs=VMEM,
        scratch_shapes=[pltpu.VMEM((len(shifts) * span, columns), jnp.bfloat16)] * 2,
        compiler_params=PARAMS,
        cost_estimate=COST,
        name="finish",
    )(scalars, index, base, up, *shrinks, *after)


def gate_kernel(waiting, *refs):
    refs[waiting][...] = jnp.zeros_like(refs[waiting])


def gate(blocks, after):
    return pl.pallas_call(
        functools.partial(gate_kernel, len(blocks) + len(after)),
        out_shape=[jax.ShapeDtypeStruct((8, 128), jnp.int32)]
        + [jax.ShapeDtypeStruct(b.shape, b.dtype) for b in blocks],
        in_specs=[HBM] * len(blocks) + [ANY] * len(after),
        out_specs=[VMEM] + [HBM] * len(blocks),
        input_output_aliases={n: n + 1 for n in range(len(blocks))},
        compiler_params=WIDE,
        cost_estimate=COST,
        name="gate",
    )(*blocks, *after)


def gather_up(adapter_up, homes):
    teams = lax.axis_size("groups")
    team = lax.axis_index("groups")
    share = adapter_up.shape[1] // teams
    own = lax.dynamic_slice_in_dim(adapter_up, team * share, share, 1)
    found = [
        lax.ppermute(own, "batch", [(i, (i - r) % homes) for i in range(homes)]) for r in range(1, homes)
    ]
    ordered = jnp.concatenate([own] + found, axis=0)
    shares = [ordered] + [
        lax.ppermute(ordered, "groups", [(i, (i + s) % teams) for i in range(teams)])
        for s in range(1, teams)
    ]
    return jnp.concatenate(
        [
            functools.reduce(
                lambda kept, s: jnp.where(lax.rem(team + teams - s, teams) == part, shares[s], kept),
                range(1, teams),
                shares[0],
            )
            for part in range(teams)
        ],
        axis=1,
    ), found


def base_kernel(waited, block_ref, tokens_ref, weight_ref, *refs):
    refs[waited][...] = jnp.dot(tokens_ref[...], weight_ref[...], preferred_element_type=jnp.float32)


def base_part(tokens, weight, blocks, columns, slab, slabs, after, params=PARAMS):
    rows, width = tokens.shape[0] // slabs, tokens.shape[1]
    count = blocks.shape[0]
    return pl.pallas_call(
        functools.partial(base_kernel, len(after)),
        out_shape=jax.ShapeDtypeStruct((rows, count * columns), jnp.float32),
        grid_spec=pltpu.PrefetchScalarGridSpec(
            num_scalar_prefetch=1,
            grid=(count,),
            in_specs=[
                pl.BlockSpec((rows, width), lambda j, chosen: (slab, 0)),
                pl.BlockSpec((width, columns), lambda j, chosen: (0, chosen[j])),
            ]
            + [ANY] * len(after),
            out_specs=pl.BlockSpec((rows, columns), lambda j, chosen: (0, j)),
        ),
        compiler_params=params,
        cost_estimate=COST,
        name="base",
    )(blocks, tokens, weight, *after)


def reduce_base(tokens, weight, piece, pieces, columns, slab, slabs, after):
    keep = [0]
    bit = pieces // 2
    while bit > 1:
        keep = keep + [p + bit for p in keep]
        bit //= 2
    keep = jnp.array(keep, jnp.int32)
    sent = base_part(
        tokens, weight, piece ^ keep ^ 1, columns, slab, slabs, after, PARAMS if slab else WIDE
    )
    kept = base_part(tokens, weight, piece ^ keep, columns, slab, slabs, [sent])
    bit, first = 1, None
    while True:
        kept = kept + lax.ppermute(sent, "tensor", [(i, i ^ bit) for i in range(pieces)])
        first = kept[:8] if first is None else first
        bit *= 2
        if bit >= pieces:
            return kept, first
        half = kept.shape[1] // 2
        kept, sent = kept[:, :half], kept[:, half:]


def on_device(tokens, request_adapter, adapter_entry, key_value_weight, adapter_down, adapter_up):
    rows, width = tokens.shape
    adapters = adapter_entry.shape[0]
    held, rank, columns = adapter_up.shape
    value_side = key_value_weight.shape[1] // 2 // columns
    homes = lax.axis_size("batch")
    pieces = lax.axis_size("tensor")
    place = lax.axis_index("batch").astype(jnp.int32)
    piece = lax.axis_index("tensor").astype(jnp.int32)
    light = rows // adapters
    span = (held + 1) * light
    order = sorted(range(1, homes), key=lambda r: (-min(r, homes - r), r))
    block_shape = jax.ShapeDtypeStruct((span, width), jnp.bfloat16)

    up, found = gather_up(adapter_up, homes)
    index, heavy = pl.pallas_call(
        functools.partial(route_kernel, homes, held, light),
        out_shape=[
            jax.ShapeDtypeStruct((1, rows), jnp.int32),
            jax.ShapeDtypeStruct((8, 128), jnp.int32),
        ],
        in_specs=[SMEM, HBM, HBM],
        out_specs=[VMEM] * 2,
        scratch_shapes=[
            pltpu.SMEM(adapter_entry.shape, jnp.int32),
            pltpu.VMEM((rows,), jnp.int32),
            pltpu.SemaphoreType.DMA((2,)),
        ],
        compiler_params=WIDE,
        cost_estimate=COST,
        name="route",
    )(place.reshape(1), adapter_entry, request_adapter)
    def pack(shifts):
        return pl.pallas_call(
            functools.partial(pack_kernel, span, shifts),
            out_shape=[jax.ShapeDtypeStruct((8, 128), jnp.int32)] + [block_shape] * len(shifts),
            in_specs=[VMEM] * 2,
            out_specs=[VMEM] + [HBM] * len(shifts),
            scratch_shapes=[
                pltpu.VMEM((len(shifts), span, width), jnp.bfloat16),
                pltpu.SemaphoreType.DMA((len(shifts),)),
            ],
            compiler_params=WIDE,
            cost_estimate=COST,
            name="pack",
        )(index, tokens)

    def send(block, r):
        return lax.ppermute(block, "batch", [(i, (i + r) % homes) for i in range(homes)])

    packed, own_block, *blocks = pack([0] + order)
    arrived = {0: own_block}
    mark, *blocks = gate(blocks, found)
    for r, block in zip(order, blocks):
        arrived[r] = send(block, r)

    heavy = heavy[0, 0]
    heavy_here = (heavy // held == place).astype(jnp.int32)
    scalars = jnp.stack([piece, lax.rem(heavy, held), heavy_here])
    height = entry_places(held) * light

    def shrink(blocks, after, passed):
        return pl.pallas_call(
            functools.partial(
                shrink_kernel, held, light, rank, value_side, len(blocks), len(after), len(passed)
            ),
            out_shape=[jax.ShapeDtypeStruct((2 * len(blocks) * height, 2 * rank), jnp.float32)]
            + [jax.ShapeDtypeStruct(p.shape, p.dtype) for p in passed],
            in_specs=[SMEM] + [VMEM] * (len(blocks) + 1) + [ANY] * len(after) + [VMEM] * len(passed),
            out_specs=[VMEM] * (1 + len(passed)),
            compiler_params=PARAMS,
            cost_estimate=COST,
            name="shrink",
        )(scalars, *blocks, adapter_down, *after, *passed)

    def combine(value):
        bit, half = 1, value.shape[0] // 2
        while bit < pieces // 2:
            value = value + lax.ppermute(value, "tensor", [(i, i ^ bit) for i in range(pieces)])
            bit *= 2
        return value[:half] + lax.ppermute(value[half:], "tensor", [(i, i ^ bit) for i in range(pieces)])

    slabs = 3
    slab_sums = [
        reduce_base(tokens, key_value_weight, piece, pieces, columns, slab, slabs, [mark])
        for slab in range(slabs)
    ]
    base = jnp.concatenate([total for total, _ in slab_sums], axis=0)
    begun = [first for _, first in slab_sums]
    late = order[-2:]
    early = order[:-2] + [0]
    totals = []
    for r in early:
        (value,) = shrink([arrived[r]], [total[:8] for total, _ in slab_sums[:1]] + begun[1:] if r else [packed], [])
        totals.append(combine(value))
    value, *totals = shrink([arrived[r] for r in late], [base[:8], base[-8:]], totals)
    last = combine(value)

    def give_back(total, r):
        return lax.ppermute(total, "batch", [(i, (i - r) % homes) for i in range(homes)]) if r else total

    shrinks = [give_back(total, r) for total, r in zip(totals, early)]
    places = lax.rem(heavy - place * held + adapters, adapters).reshape(1)
    column = index.reshape(rows, 1)
    running = finish(places, column, base, up, shrinks, [last], early, jnp.float32, homes, held, light)
    shrinks = [give_back(last[n * height : (n + 1) * height], r) for n, r in enumerate(late)]
    return finish(places, column, running, up, shrinks, [], late, jnp.bfloat16, homes, held, light)


def solution(mesh):
    in_specs = (
        P(("groups", "batch"), "tensor"),
        P(("groups", "batch")),
        P(),
        P("tensor", None),
        P("batch", "tensor", None),
        P("batch", None, "tensor"),
    )
    out_specs = P(("groups", "batch"), "tensor")
    return jax.shard_map(
        on_device, mesh=mesh, in_specs=in_specs, out_specs=out_specs, check_vma=False
    )
```

```python
import functools

import jax
import jax.numpy as jnp
from jax import lax
from jax.experimental import pallas as pl
from jax.experimental.pallas import tpu as pltpu
from jax.sharding import PartitionSpec as P

adapter_scale = 0.5
VMEM_BYTES = 24 * 1024 * 1024
WIDE = pltpu.CompilerParams(vmem_limit_bytes=60 * 1024 * 1024)
VMEM = pl.BlockSpec(memory_space=pltpu.VMEM)
ANY = pl.BlockSpec(memory_space=pl.ANY)
HBM = pl.BlockSpec(memory_space=pltpu.HBM)
SMEM = pl.BlockSpec(memory_space=pltpu.SMEM)
COST = pl.CostEstimate(flops=1, bytes_accessed=1, transcendentals=0)
PARAMS = pltpu.CompilerParams(vmem_limit_bytes=VMEM_BYTES)


def place_rows(index, start, tokens_ref, block_ref):
    local = lax.broadcasted_iota(jnp.int32, (block_ref.shape[0], index.shape[1]), 0)
    choose = (local + start == index).astype(jnp.bfloat16)
    block_ref[...] = jnp.dot(
        choose, tokens_ref[...], preferred_element_type=jnp.float32
    ).astype(jnp.bfloat16)


def route_kernel(
    homes, held, light, place_ref, entry_hbm, request_hbm, index_ref, heavy_ref, entry_ref, request_ref, sems
):
    loads = [
        pltpu.make_async_copy(source, target, sems.at[n])
        for n, (source, target) in enumerate(
            [(request_hbm, request_ref), (entry_hbm, entry_ref)]
        )
    ]
    for load in loads:
        load.start()
    rows = request_ref.shape[0]
    adapters = entry_ref.shape[0]
    span = (held + 1) * light
    earlier = (
        lax.broadcasted_iota(jnp.int32, (rows, rows), 0) < lax.broadcasted_iota(jnp.int32, (rows, rows), 1)
    ).astype(jnp.bfloat16)
    loads[0].wait()
    request = request_ref[...].reshape(1, rows)
    onehot = lax.broadcasted_iota(jnp.int32, (adapters, rows), 0) == request
    before = jnp.dot(onehot.astype(jnp.bfloat16), earlier, preferred_element_type=jnp.float32)
    position = jnp.sum(jnp.where(onehot, before, 0.0), axis=0, keepdims=True).astype(jnp.int32)
    loads[1].wait()
    slot = jnp.zeros_like(position)
    for a in range(adapters):
        slot = jnp.where(request == a, entry_ref[a], slot)
    home = slot // held
    relative = lax.rem(home - place_ref[0] + homes, homes)
    inside = jnp.where(
        position < light, (slot - home * held) * light + position, held * light + position - light
    )
    index = relative * span + inside
    index_ref[...] = index
    heavy = jnp.max(jnp.where(position >= light, slot, 0), axis=1, keepdims=True)
    heavy_ref[...] = jnp.broadcast_to(heavy, heavy_ref.shape)


def pack_kernel(span, shifts, index_ref, tokens_ref, mark_ref, *refs):
    count = len(shifts)
    block_refs, buffer, sems = refs[:count], refs[count], refs[count + 1]
    mark_ref[...] = jnp.zeros_like(mark_ref)
    stores = []
    for n, shift in enumerate(shifts):
        place_rows(index_ref[...], shift * span, tokens_ref, buffer.at[n])
        stores.append(pltpu.make_async_copy(buffer.at[n], block_refs[n], sems.at[n]))
        stores[-1].start()
    for store in stores:
        store.wait()


def entry_places(held):
    return (held + 2) // 2


def shrink_kernel(held, light, rank, value_side, count, waited, passed, scalar_ref, *refs):
    block_refs, down_ref, refs = refs[:count], refs[count], refs[count + 1 + waited :]
    passed_refs, out_ref, left_refs = refs[:passed], refs[passed], refs[passed + 1 :]
    groups = entry_places(held)
    height = groups * light

    def product(e):
        if e > held:
            return jnp.zeros((count * light, 2 * rank), jnp.float32)
        factor = down_ref[e] if e < held else down_ref[scalar_ref[1]]
        rows = [block_ref[e * light : (e + 1) * light, :] for block_ref in block_refs]
        value = jnp.dot(
            jnp.concatenate(rows, axis=0) if count > 1 else rows[0], factor, preferred_element_type=jnp.float32
        )
        return value if e < held else jnp.where(scalar_ref[2] == 1, value, 0.0)

    on_value_side = scalar_ref[0] >= value_side
    for g in range(groups):
        first, second = product(g), product(g + groups)
        key = jnp.concatenate([first[:, :rank], second[:, :rank]], axis=1)
        value = jnp.concatenate([first[:, rank:], second[:, rank:]], axis=1)
        mine, other = jnp.where(on_value_side, value, key), jnp.where(on_value_side, key, value)
        for n in range(count):
            here, start = slice(n * light, (n + 1) * light), n * height + g * light
            out_ref[start : start + light, :] = mine[here]
            out_ref[count * height + start : count * height + start + light, :] = other[here]
    for source, target in zip(passed_refs, left_refs):
        target[...] = source[...]


def hold_kernel(value_ref, *refs):
    refs[-1][...] = value_ref[...]


def split_pair(value):
    high = value.astype(jnp.bfloat16)
    low = (value - high.astype(jnp.float32)).astype(jnp.bfloat16)
    return high, low


def finish_kernel(homes, held, light, rank, shifts, waited, place_ref, index_ref, base_ref, up_ref, *refs):
    count = len(shifts)
    refs = refs[:count] + refs[count + waited :]
    shrink_refs, out_ref, high_ref, low_ref = refs[:count], refs[count], refs[count + 1], refs[count + 2]
    span = (held + 1) * light
    rows = base_ref.shape[0]
    groups = entry_places(held)
    local = []
    for n, r in enumerate(shifts):
        for e in range(held + 1):
            entry = r * held + e if e < held else place_ref[0]
            g, side = e % groups, e // groups
            high, low = split_pair(
                shrink_refs[n][g * light : (g + 1) * light, side * rank : (side + 1) * rank]
            )
            factor = up_ref[entry]
            delta = jnp.dot(high, factor, preferred_element_type=jnp.float32) + jnp.dot(
                low, factor, preferred_element_type=jnp.float32
            )
            high, low = split_pair(delta)
            start = n * span + e * light
            high_ref[start : start + light, :] = high
            low_ref[start : start + light, :] = low
        local.append(lax.broadcasted_iota(jnp.int32, (rows, span), 1) + r * span == index_ref[...])
    delta = base_ref[...]
    for n in range(count):
        choose = local[n].astype(jnp.bfloat16)
        delta = delta + adapter_scale * (
            jnp.dot(choose, high_ref[n * span : (n + 1) * span, :], preferred_element_type=jnp.float32)
            + jnp.dot(choose, low_ref[n * span : (n + 1) * span, :], preferred_element_type=jnp.float32)
        )
    out_ref[...] = delta.astype(out_ref.dtype)


def finish(scalars, index, base, up, shrinks, after, shifts, dtype, homes, held, light):
    rows, columns = base.shape
    span = (held + 1) * light
    return pl.pallas_call(
        functools.partial(finish_kernel, homes, held, light, up.shape[1], shifts, len(after)),
        out_shape=jax.ShapeDtypeStruct((rows, columns), dtype),
        in_specs=[SMEM] + [VMEM] * (3 + len(shifts)) + [ANY] * len(after),
        out_specs=VMEM,
        scratch_shapes=[pltpu.VMEM((len(shifts) * span, columns), jnp.bfloat16)] * 2,
        compiler_params=PARAMS,
        cost_estimate=COST,
        name="finish",
    )(scalars, index, base, up, *shrinks, *after)


def gate_kernel(waiting, *refs):
    refs[waiting][...] = jnp.zeros_like(refs[waiting])


def gate(blocks, after):
    return pl.pallas_call(
        functools.partial(gate_kernel, len(blocks) + len(after)),
        out_shape=[jax.ShapeDtypeStruct((8, 128), jnp.int32)]
        + [jax.ShapeDtypeStruct(b.shape, b.dtype) for b in blocks],
        in_specs=[HBM] * len(blocks) + [ANY] * len(after),
        out_specs=[VMEM] + [HBM] * len(blocks),
        input_output_aliases={n: n + 1 for n in range(len(blocks))},
        compiler_params=WIDE,
        cost_estimate=COST,
        name="gate",
    )(*blocks, *after)


def gather_up(adapter_up, homes):
    teams = lax.axis_size("groups")
    team = lax.axis_index("groups")
    share = adapter_up.shape[1] // teams
    own = lax.dynamic_slice_in_dim(adapter_up, team * share, share, 1)
    found = [
        lax.ppermute(own, "batch", [(i, (i - r) % homes) for i in range(homes)]) for r in range(1, homes)
    ]
    ordered = jnp.concatenate([own] + found, axis=0)
    shares = [ordered] + [
        lax.ppermute(ordered, "groups", [(i, (i + s) % teams) for i in range(teams)])
        for s in range(1, teams)
    ]
    return jnp.concatenate(
        [
            functools.reduce(
                lambda kept, s: jnp.where(lax.rem(team + teams - s, teams) == part, shares[s], kept),
                range(1, teams),
                shares[0],
            )
            for part in range(teams)
        ],
        axis=1,
    ), found


def base_kernel(waited, block_ref, tokens_ref, weight_ref, *refs):
    refs[waited][...] = jnp.dot(tokens_ref[...], weight_ref[...], preferred_element_type=jnp.float32)


def base_part(tokens, weight, blocks, columns, slab, slabs, after, params=PARAMS):
    rows, width = tokens.shape[0] // slabs, tokens.shape[1]
    count = blocks.shape[0]
    return pl.pallas_call(
        functools.partial(base_kernel, len(after)),
        out_shape=jax.ShapeDtypeStruct((rows, count * columns), jnp.float32),
        grid_spec=pltpu.PrefetchScalarGridSpec(
            num_scalar_prefetch=1,
            grid=(count,),
            in_specs=[
                pl.BlockSpec((rows, width), lambda j, chosen: (slab, 0)),
                pl.BlockSpec((width, columns), lambda j, chosen: (0, chosen[j])),
            ]
            + [ANY] * len(after),
            out_specs=pl.BlockSpec((rows, columns), lambda j, chosen: (0, j)),
        ),
        compiler_params=params,
        cost_estimate=COST,
        name="base",
    )(blocks, tokens, weight, *after)


def reduce_base(tokens, weight, piece, pieces, columns, slab, slabs, after):
    keep = [0]
    bit = pieces // 2
    while bit > 1:
        keep = keep + [p + bit for p in keep]
        bit //= 2
    keep = jnp.array(keep, jnp.int32)
    sent = base_part(
        tokens, weight, piece ^ keep ^ 1, columns, slab, slabs, after, PARAMS if slab else WIDE
    )
    kept = base_part(tokens, weight, piece ^ keep, columns, slab, slabs, [sent])
    bit, first = 1, None
    while True:
        kept = kept + lax.ppermute(sent, "tensor", [(i, i ^ bit) for i in range(pieces)])
        first = kept[:8] if first is None else first
        bit *= 2
        if bit >= pieces:
            return kept, first
        half = kept.shape[1] // 2
        kept, sent = kept[:, :half], kept[:, half:]


def on_device(tokens, request_adapter, adapter_entry, key_value_weight, adapter_down, adapter_up):
    rows, width = tokens.shape
    adapters = adapter_entry.shape[0]
    held, rank, columns = adapter_up.shape
    value_side = key_value_weight.shape[1] // 2 // columns
    homes = lax.axis_size("batch")
    pieces = lax.axis_size("tensor")
    place = lax.axis_index("batch").astype(jnp.int32)
    piece = lax.axis_index("tensor").astype(jnp.int32)
    light = rows // adapters
    span = (held + 1) * light
    order = sorted(range(1, homes), key=lambda r: (-min(r, homes - r), r))
    block_shape = jax.ShapeDtypeStruct((span, width), jnp.bfloat16)

    up, found = gather_up(adapter_up, homes)
    index, heavy = pl.pallas_call(
        functools.partial(route_kernel, homes, held, light),
        out_shape=[
            jax.ShapeDtypeStruct((1, rows), jnp.int32),
            jax.ShapeDtypeStruct((8, 128), jnp.int32),
        ],
        in_specs=[SMEM, HBM, HBM],
        out_specs=[VMEM] * 2,
        scratch_shapes=[
            pltpu.SMEM(adapter_entry.shape, jnp.int32),
            pltpu.VMEM((rows,), jnp.int32),
            pltpu.SemaphoreType.DMA((2,)),
        ],
        compiler_params=WIDE,
        cost_estimate=COST,
        name="route",
    )(place.reshape(1), adapter_entry, request_adapter)
    def pack(shifts):
        return pl.pallas_call(
            functools.partial(pack_kernel, span, shifts),
            out_shape=[jax.ShapeDtypeStruct((8, 128), jnp.int32)] + [block_shape] * len(shifts),
            in_specs=[VMEM] * 2,
            out_specs=[VMEM] + [HBM] * len(shifts),
            scratch_shapes=[
                pltpu.VMEM((len(shifts), span, width), jnp.bfloat16),
                pltpu.SemaphoreType.DMA((len(shifts),)),
            ],
            compiler_params=WIDE,
            cost_estimate=COST,
            name="pack",
        )(index, tokens)

    def send(block, r):
        return lax.ppermute(block, "batch", [(i, (i + r) % homes) for i in range(homes)])

    packed, own_block, *blocks = pack([0] + order)
    arrived = {0: own_block}
    mark, *blocks = gate(blocks, found)
    for r, block in zip(order, blocks):
        arrived[r] = send(block, r)

    heavy = heavy[0, 0]
    heavy_here = (heavy // held == place).astype(jnp.int32)
    scalars = jnp.stack([piece, lax.rem(heavy, held), heavy_here])
    height = entry_places(held) * light

    def shrink(blocks, after, passed):
        return pl.pallas_call(
            functools.partial(
                shrink_kernel, held, light, rank, value_side, len(blocks), len(after), len(passed)
            ),
            out_shape=[jax.ShapeDtypeStruct((2 * len(blocks) * height, 2 * rank), jnp.float32)]
            + [jax.ShapeDtypeStruct(p.shape, p.dtype) for p in passed],
            in_specs=[SMEM] + [VMEM] * (len(blocks) + 1) + [ANY] * len(after) + [VMEM] * len(passed),
            out_specs=[VMEM] * (1 + len(passed)),
            compiler_params=PARAMS,
            cost_estimate=COST,
            name="shrink",
        )(scalars, *blocks, adapter_down, *after, *passed)

    def hold(value, after):
        return pl.pallas_call(
            hold_kernel,
            out_shape=jax.ShapeDtypeStruct(value.shape, value.dtype),
            in_specs=[VMEM] + [ANY] * len(after),
            out_specs=VMEM,
            compiler_params=PARAMS,
            cost_estimate=COST,
            name="hold",
        )(value, *after)

    def combine(value, after=()):
        bit, half = 1, value.shape[0] // 2
        while bit < pieces // 2:
            value = value + lax.ppermute(value, "tensor", [(i, i ^ bit) for i in range(pieces)])
            bit *= 2
        if after:
            value = hold(value, after)
        return value[:half] + lax.ppermute(value[half:], "tensor", [(i, i ^ bit) for i in range(pieces)])

    slabs = 3
    slab_sums = [
        reduce_base(tokens, key_value_weight, piece, pieces, columns, slab, slabs, [mark])
        for slab in range(slabs)
    ]
    base = jnp.concatenate([total for total, _ in slab_sums], axis=0)
    begun = [first for _, first in slab_sums]
    whole = [total[:8] for total, _ in slab_sums[:1]]
    late = order[-2:]
    early = order[:-2] + [0]
    totals = []
    for r in early:
        (value,) = shrink([arrived[r]], begun if r else [packed], [])
        totals.append(combine(value, whole if r else ()))
    value, *totals = shrink([arrived[r] for r in late], [base[:8], base[-8:]], totals)
    last = combine(value)

    def give_back(total, r):
        return lax.ppermute(total, "batch", [(i, (i - r) % homes) for i in range(homes)]) if r else total

    shrinks = [give_back(total, r) for total, r in zip(totals, early)]
    places = lax.rem(heavy - place * held + adapters, adapters).reshape(1)
    column = index.reshape(rows, 1)
    running = finish(places, column, base, up, shrinks, [last], early, jnp.float32, homes, held, light)
    shrinks = [give_back(last[n * height : (n + 1) * height], r) for n, r in enumerate(late)]
    return finish(places, column, running, up, shrinks, [], late, jnp.bfloat16, homes, held, light)


def solution(mesh):
    in_specs = (
        P(("groups", "batch"), "tensor"),
        P(("groups", "batch")),
        P(),
        P("tensor", None),
        P("batch", "tensor", None),
        P("batch", None, "tensor"),
    )
    out_specs = P(("groups", "batch"), "tensor")
    return jax.shard_map(
        on_device, mesh=mesh, in_specs=in_specs, out_specs=out_specs, check_vma=False
    )
```

```python
import functools

import jax
import jax.numpy as jnp
from jax import lax
from jax.experimental import pallas as pl
from jax.experimental.pallas import tpu as pltpu
from jax.sharding import PartitionSpec as P

adapter_scale = 0.5
VMEM_BYTES = 24 * 1024 * 1024
WIDE = pltpu.CompilerParams(vmem_limit_bytes=60 * 1024 * 1024)
VMEM = pl.BlockSpec(memory_space=pltpu.VMEM)
ANY = pl.BlockSpec(memory_space=pl.ANY)
HBM = pl.BlockSpec(memory_space=pltpu.HBM)
SMEM = pl.BlockSpec(memory_space=pltpu.SMEM)
COST = pl.CostEstimate(flops=1, bytes_accessed=1, transcendentals=0)
PARAMS = pltpu.CompilerParams(vmem_limit_bytes=VMEM_BYTES)


def place_rows(index, start, tokens_ref, block_ref):
    local = lax.broadcasted_iota(jnp.int32, (block_ref.shape[0], index.shape[1]), 0)
    choose = (local + start == index).astype(jnp.bfloat16)
    block_ref[...] = jnp.dot(
        choose, tokens_ref[...], preferred_element_type=jnp.float32
    ).astype(jnp.bfloat16)


def route_kernel(
    homes, held, light, place_ref, entry_hbm, request_hbm, index_ref, heavy_ref, entry_ref, request_ref, sems
):
    loads = [
        pltpu.make_async_copy(source, target, sems.at[n])
        for n, (source, target) in enumerate(
            [(request_hbm, request_ref), (entry_hbm, entry_ref)]
        )
    ]
    for load in loads:
        load.start()
    rows = request_ref.shape[0]
    adapters = entry_ref.shape[0]
    span = (held + 1) * light
    earlier = (
        lax.broadcasted_iota(jnp.int32, (rows, rows), 0) < lax.broadcasted_iota(jnp.int32, (rows, rows), 1)
    ).astype(jnp.bfloat16)
    loads[0].wait()
    request = request_ref[...].reshape(1, rows)
    onehot = lax.broadcasted_iota(jnp.int32, (adapters, rows), 0) == request
    before = jnp.dot(onehot.astype(jnp.bfloat16), earlier, preferred_element_type=jnp.float32)
    position = jnp.sum(jnp.where(onehot, before, 0.0), axis=0, keepdims=True).astype(jnp.int32)
    loads[1].wait()
    slot = jnp.zeros_like(position)
    for a in range(adapters):
        slot = jnp.where(request == a, entry_ref[a], slot)
    home = slot // held
    relative = lax.rem(home - place_ref[0] + homes, homes)
    inside = jnp.where(
        position < light, (slot - home * held) * light + position, held * light + position - light
    )
    index = relative * span + inside
    index_ref[...] = index
    heavy = jnp.max(jnp.where(position >= light, slot, 0), axis=1, keepdims=True)
    heavy_ref[...] = jnp.broadcast_to(heavy, heavy_ref.shape)


def pack_kernel(span, shifts, index_ref, tokens_ref, mark_ref, *refs):
    count = len(shifts)
    block_refs, buffer, sems = refs[:count], refs[count], refs[count + 1]
    mark_ref[...] = jnp.zeros_like(mark_ref)
    stores = []
    for n, shift in enumerate(shifts):
        place_rows(index_ref[...], shift * span, tokens_ref, buffer.at[n])
        stores.append(pltpu.make_async_copy(buffer.at[n], block_refs[n], sems.at[n]))
        stores[-1].start()
    for store in stores:
        store.wait()


def entry_places(held):
    return (held + 2) // 2


def shrink_kernel(held, light, rank, value_side, count, waited, passed, scalar_ref, *refs):
    block_refs, down_ref, refs = refs[:count], refs[count], refs[count + 1 + waited :]
    passed_refs, out_ref, left_refs = refs[:passed], refs[passed], refs[passed + 1 :]
    groups = entry_places(held)
    height = groups * light

    def product(e):
        if e > held:
            return jnp.zeros((count * light, 2 * rank), jnp.float32)
        factor = down_ref[e] if e < held else down_ref[scalar_ref[1]]
        rows = [block_ref[e * light : (e + 1) * light, :] for block_ref in block_refs]
        value = jnp.dot(
            jnp.concatenate(rows, axis=0) if count > 1 else rows[0], factor, preferred_element_type=jnp.float32
        )
        return value if e < held else jnp.where(scalar_ref[2] == 1, value, 0.0)

    on_value_side = scalar_ref[0] >= value_side
    for g in range(groups):
        first, second = product(g), product(g + groups)
        key = jnp.concatenate([first[:, :rank], second[:, :rank]], axis=1)
        value = jnp.concatenate([first[:, rank:], second[:, rank:]], axis=1)
        mine, other = jnp.where(on_value_side, value, key), jnp.where(on_value_side, key, value)
        for n in range(count):
            here, start = slice(n * light, (n + 1) * light), n * height + g * light
            out_ref[start : start + light, :] = mine[here]
            out_ref[count * height + start : count * height + start + light, :] = other[here]
    for source, target in zip(passed_refs, left_refs):
        target[...] = source[...]


def hold_kernel(value_ref, *refs):
    refs[-1][...] = value_ref[...]


def split_pair(value):
    high = value.astype(jnp.bfloat16)
    low = (value - high.astype(jnp.float32)).astype(jnp.bfloat16)
    return high, low


def finish_kernel(homes, held, light, rank, shifts, waited, place_ref, index_ref, base_ref, up_ref, *refs):
    count = len(shifts)
    refs = refs[:count] + refs[count + waited :]
    shrink_refs, out_ref, high_ref, low_ref = refs[:count], refs[count], refs[count + 1], refs[count + 2]
    span = (held + 1) * light
    rows = base_ref.shape[0]
    groups = entry_places(held)
    local = []
    for n, r in enumerate(shifts):
        for e in range(held + 1):
            entry = r * held + e if e < held else place_ref[0]
            g, side = e % groups, e // groups
            high, low = split_pair(
                shrink_refs[n][g * light : (g + 1) * light, side * rank : (side + 1) * rank]
            )
            factor = up_ref[entry]
            delta = jnp.dot(high, factor, preferred_element_type=jnp.float32) + jnp.dot(
                low, factor, preferred_element_type=jnp.float32
            )
            high, low = split_pair(delta)
            start = n * span + e * light
            high_ref[start : start + light, :] = high
            low_ref[start : start + light, :] = low
        local.append(lax.broadcasted_iota(jnp.int32, (rows, span), 1) + r * span == index_ref[...])
    delta = base_ref[...]
    for n in range(count):
        choose = local[n].astype(jnp.bfloat16)
        delta = delta + adapter_scale * (
            jnp.dot(choose, high_ref[n * span : (n + 1) * span, :], preferred_element_type=jnp.float32)
            + jnp.dot(choose, low_ref[n * span : (n + 1) * span, :], preferred_element_type=jnp.float32)
        )
    out_ref[...] = delta.astype(out_ref.dtype)


def finish(scalars, index, base, up, shrinks, after, shifts, dtype, homes, held, light):
    rows, columns = base.shape
    span = (held + 1) * light
    return pl.pallas_call(
        functools.partial(finish_kernel, homes, held, light, up.shape[1], shifts, len(after)),
        out_shape=jax.ShapeDtypeStruct((rows, columns), dtype),
        in_specs=[SMEM] + [VMEM] * (3 + len(shifts)) + [ANY] * len(after),
        out_specs=VMEM,
        scratch_shapes=[pltpu.VMEM((len(shifts) * span, columns), jnp.bfloat16)] * 2,
        compiler_params=PARAMS,
        cost_estimate=COST,
        name="finish",
    )(scalars, index, base, up, *shrinks, *after)


def gate_kernel(waiting, *refs):
    refs[waiting][...] = jnp.zeros_like(refs[waiting])


def gate(blocks, after):
    return pl.pallas_call(
        functools.partial(gate_kernel, len(blocks) + len(after)),
        out_shape=[jax.ShapeDtypeStruct((8, 128), jnp.int32)]
        + [jax.ShapeDtypeStruct(b.shape, b.dtype) for b in blocks],
        in_specs=[HBM] * len(blocks) + [ANY] * len(after),
        out_specs=[VMEM] + [HBM] * len(blocks),
        input_output_aliases={n: n + 1 for n in range(len(blocks))},
        compiler_params=WIDE,
        cost_estimate=COST,
        name="gate",
    )(*blocks, *after)


def gather_up(adapter_up, homes):
    teams = lax.axis_size("groups")
    team = lax.axis_index("groups")
    share = adapter_up.shape[1] // teams
    own = lax.dynamic_slice_in_dim(adapter_up, team * share, share, 1)
    found = [
        lax.ppermute(own, "batch", [(i, (i - r) % homes) for i in range(homes)]) for r in range(1, homes)
    ]
    ordered = jnp.concatenate([own] + found, axis=0)
    shares = [ordered] + [
        lax.ppermute(ordered, "groups", [(i, (i + s) % teams) for i in range(teams)])
        for s in range(1, teams)
    ]
    return jnp.concatenate(
        [
            functools.reduce(
                lambda kept, s: jnp.where(lax.rem(team + teams - s, teams) == part, shares[s], kept),
                range(1, teams),
                shares[0],
            )
            for part in range(teams)
        ],
        axis=1,
    ), found


def base_kernel(waited, block_ref, tokens_ref, weight_ref, *refs):
    refs[waited][...] = jnp.dot(tokens_ref[...], weight_ref[...], preferred_element_type=jnp.float32)


def base_part(tokens, weight, blocks, columns, slab, slabs, after, params=PARAMS):
    rows, width = tokens.shape[0] // slabs, tokens.shape[1]
    count = blocks.shape[0]
    return pl.pallas_call(
        functools.partial(base_kernel, len(after)),
        out_shape=jax.ShapeDtypeStruct((rows, count * columns), jnp.float32),
        grid_spec=pltpu.PrefetchScalarGridSpec(
            num_scalar_prefetch=1,
            grid=(count,),
            in_specs=[
                pl.BlockSpec((rows, width), lambda j, chosen: (slab, 0)),
                pl.BlockSpec((width, columns), lambda j, chosen: (0, chosen[j])),
            ]
            + [ANY] * len(after),
            out_specs=pl.BlockSpec((rows, columns), lambda j, chosen: (0, j)),
        ),
        compiler_params=params,
        cost_estimate=COST,
        name="base",
    )(blocks, tokens, weight, *after)


def reduce_base(tokens, weight, piece, pieces, columns, slab, slabs, after):
    keep = [0]
    bit = pieces // 2
    while bit > 1:
        keep = keep + [p + bit for p in keep]
        bit //= 2
    keep = jnp.array(keep, jnp.int32)
    sent = base_part(
        tokens, weight, piece ^ keep ^ 1, columns, slab, slabs, after, PARAMS if slab else WIDE
    )
    kept = base_part(tokens, weight, piece ^ keep, columns, slab, slabs, [sent])
    bit, first = 1, None
    while True:
        kept = kept + lax.ppermute(sent, "tensor", [(i, i ^ bit) for i in range(pieces)])
        first = kept[:8] if first is None else first
        bit *= 2
        if bit >= pieces:
            return kept, first
        half = kept.shape[1] // 2
        kept, sent = kept[:, :half], kept[:, half:]


def on_device(tokens, request_adapter, adapter_entry, key_value_weight, adapter_down, adapter_up):
    rows, width = tokens.shape
    adapters = adapter_entry.shape[0]
    held, rank, columns = adapter_up.shape
    value_side = key_value_weight.shape[1] // 2 // columns
    homes = lax.axis_size("batch")
    pieces = lax.axis_size("tensor")
    place = lax.axis_index("batch").astype(jnp.int32)
    piece = lax.axis_index("tensor").astype(jnp.int32)
    light = rows // adapters
    span = (held + 1) * light
    order = sorted(range(1, homes), key=lambda r: (-min(r, homes - r), r))
    block_shape = jax.ShapeDtypeStruct((span, width), jnp.bfloat16)

    up, found = gather_up(adapter_up, homes)
    index, heavy = pl.pallas_call(
        functools.partial(route_kernel, homes, held, light),
        out_shape=[
            jax.ShapeDtypeStruct((1, rows), jnp.int32),
            jax.ShapeDtypeStruct((8, 128), jnp.int32),
        ],
        in_specs=[SMEM, HBM, HBM],
        out_specs=[VMEM] * 2,
        scratch_shapes=[
            pltpu.SMEM(adapter_entry.shape, jnp.int32),
            pltpu.VMEM((rows,), jnp.int32),
            pltpu.SemaphoreType.DMA((2,)),
        ],
        compiler_params=WIDE,
        cost_estimate=COST,
        name="route",
    )(place.reshape(1), adapter_entry, request_adapter)
    def pack(shifts):
        return pl.pallas_call(
            functools.partial(pack_kernel, span, shifts),
            out_shape=[jax.ShapeDtypeStruct((8, 128), jnp.int32)] + [block_shape] * len(shifts),
            in_specs=[VMEM] * 2,
            out_specs=[VMEM] + [HBM] * len(shifts),
            scratch_shapes=[
                pltpu.VMEM((len(shifts), span, width), jnp.bfloat16),
                pltpu.SemaphoreType.DMA((len(shifts),)),
            ],
            compiler_params=WIDE,
            cost_estimate=COST,
            name="pack",
        )(index, tokens)

    def send(block, r):
        return lax.ppermute(block, "batch", [(i, (i + r) % homes) for i in range(homes)])

    packed, own_block, *blocks = pack([0] + order)
    arrived = {0: own_block}
    mark, *blocks = gate(blocks, [packed])
    for r, block in zip(order, blocks):
        arrived[r] = send(block, r)

    heavy = heavy[0, 0]
    heavy_here = (heavy // held == place).astype(jnp.int32)
    scalars = jnp.stack([piece, lax.rem(heavy, held), heavy_here])
    height = entry_places(held) * light

    def shrink(blocks, after, passed):
        return pl.pallas_call(
            functools.partial(
                shrink_kernel, held, light, rank, value_side, len(blocks), len(after), len(passed)
            ),
            out_shape=[jax.ShapeDtypeStruct((2 * len(blocks) * height, 2 * rank), jnp.float32)]
            + [jax.ShapeDtypeStruct(p.shape, p.dtype) for p in passed],
            in_specs=[SMEM] + [VMEM] * (len(blocks) + 1) + [ANY] * len(after) + [VMEM] * len(passed),
            out_specs=[VMEM] * (1 + len(passed)),
            compiler_params=PARAMS,
            cost_estimate=COST,
            name="shrink",
        )(scalars, *blocks, adapter_down, *after, *passed)

    def hold(value, after):
        return pl.pallas_call(
            hold_kernel,
            out_shape=jax.ShapeDtypeStruct(value.shape, value.dtype),
            in_specs=[VMEM] + [ANY] * len(after),
            out_specs=VMEM,
            compiler_params=PARAMS,
            cost_estimate=COST,
            name="hold",
        )(value, *after)

    def combine(value, after=()):
        bit, half = 1, value.shape[0] // 2
        while bit < pieces // 2:
            value = value + lax.ppermute(value, "tensor", [(i, i ^ bit) for i in range(pieces)])
            bit *= 2
        if after:
            value = hold(value, after)
        return value[:half] + lax.ppermute(value[half:], "tensor", [(i, i ^ bit) for i in range(pieces)])

    slabs = 3
    slab_sums = [
        reduce_base(tokens, key_value_weight, piece, pieces, columns, slab, slabs, [mark] + found)
        for slab in range(slabs)
    ]
    base = jnp.concatenate([total for total, _ in slab_sums], axis=0)
    begun = [first for _, first in slab_sums]
    whole = [total[:8] for total, _ in slab_sums[:1]]
    late = order[-2:]
    early = order[:-2] + [0]
    totals = []
    for r in early:
        (value,) = shrink([arrived[r]], begun if r else [packed], [])
        totals.append(combine(value, whole if r else ()))
    value, *totals = shrink([arrived[r] for r in late], [base[:8], base[-8:]], totals)
    last = combine(value)

    def give_back(total, r):
        return lax.ppermute(total, "batch", [(i, (i - r) % homes) for i in range(homes)]) if r else total

    shrinks = [give_back(total, r) for total, r in zip(totals, early)]
    places = lax.rem(heavy - place * held + adapters, adapters).reshape(1)
    column = index.reshape(rows, 1)
    running = finish(places, column, base, up, shrinks, [last], early, jnp.float32, homes, held, light)
    shrinks = [give_back(last[n * height : (n + 1) * height], r) for n, r in enumerate(late)]
    return finish(places, column, running, up, shrinks, [], late, jnp.bfloat16, homes, held, light)


def solution(mesh):
    in_specs = (
        P(("groups", "batch"), "tensor"),
        P(("groups", "batch")),
        P(),
        P("tensor", None),
        P("batch", "tensor", None),
        P("batch", None, "tensor"),
    )
    out_specs = P(("groups", "batch"), "tensor")
    return jax.shard_map(
        on_device, mesh=mesh, in_specs=in_specs, out_specs=out_specs, check_vma=False
    )
```

```python
import functools

import jax
import jax.numpy as jnp
from jax import lax
from jax.experimental import pallas as pl
from jax.experimental.pallas import tpu as pltpu
from jax.sharding import PartitionSpec as P

adapter_scale = 0.5
VMEM_BYTES = 24 * 1024 * 1024
WIDE = pltpu.CompilerParams(vmem_limit_bytes=60 * 1024 * 1024)
VMEM = pl.BlockSpec(memory_space=pltpu.VMEM)
ANY = pl.BlockSpec(memory_space=pl.ANY)
HBM = pl.BlockSpec(memory_space=pltpu.HBM)
SMEM = pl.BlockSpec(memory_space=pltpu.SMEM)
COST = pl.CostEstimate(flops=1, bytes_accessed=1, transcendentals=0)
PARAMS = pltpu.CompilerParams(vmem_limit_bytes=VMEM_BYTES)


def place_rows(index, start, tokens_ref, block_ref):
    local = lax.broadcasted_iota(jnp.int32, (block_ref.shape[0], index.shape[1]), 0)
    choose = (local + start == index).astype(jnp.bfloat16)
    block_ref[...] = jnp.dot(
        choose, tokens_ref[...], preferred_element_type=jnp.float32
    ).astype(jnp.bfloat16)


def route_kernel(
    homes, held, light, place_ref, entry_hbm, request_hbm, index_ref, heavy_ref, entry_ref, request_ref, sems
):
    loads = [
        pltpu.make_async_copy(source, target, sems.at[n])
        for n, (source, target) in enumerate(
            [(request_hbm, request_ref), (entry_hbm, entry_ref)]
        )
    ]
    for load in loads:
        load.start()
    rows = request_ref.shape[0]
    adapters = entry_ref.shape[0]
    span = (held + 1) * light
    earlier = (
        lax.broadcasted_iota(jnp.int32, (rows, rows), 0) < lax.broadcasted_iota(jnp.int32, (rows, rows), 1)
    ).astype(jnp.bfloat16)
    loads[0].wait()
    request = request_ref[...].reshape(1, rows)
    onehot = lax.broadcasted_iota(jnp.int32, (adapters, rows), 0) == request
    before = jnp.dot(onehot.astype(jnp.bfloat16), earlier, preferred_element_type=jnp.float32)
    position = jnp.sum(jnp.where(onehot, before, 0.0), axis=0, keepdims=True).astype(jnp.int32)
    loads[1].wait()
    slot = jnp.zeros_like(position)
    for a in range(adapters):
        slot = jnp.where(request == a, entry_ref[a], slot)
    home = slot // held
    relative = lax.rem(home - place_ref[0] + homes, homes)
    inside = jnp.where(
        position < light, (slot - home * held) * light + position, held * light + position - light
    )
    index = relative * span + inside
    index_ref[...] = index
    heavy = jnp.max(jnp.where(position >= light, slot, 0), axis=1, keepdims=True)
    heavy_ref[...] = jnp.broadcast_to(heavy, heavy_ref.shape)


def pack_kernel(span, shifts, index_ref, tokens_ref, mark_ref, *refs):
    count = len(shifts)
    block_refs, buffer, sems = refs[:count], refs[count], refs[count + 1]
    mark_ref[...] = jnp.zeros_like(mark_ref)
    stores = []
    for n, shift in enumerate(shifts):
        place_rows(index_ref[...], shift * span, tokens_ref, buffer.at[n])
        stores.append(pltpu.make_async_copy(buffer.at[n], block_refs[n], sems.at[n]))
        stores[-1].start()
    for store in stores:
        store.wait()


def entry_places(held):
    return (held + 2) // 2


def shrink_kernel(held, light, rank, value_side, count, waited, passed, scalar_ref, *refs):
    block_refs, down_ref, refs = refs[:count], refs[count], refs[count + 1 + waited :]
    passed_refs, out_ref, left_refs = refs[:passed], refs[passed], refs[passed + 1 :]
    groups = entry_places(held)
    height = groups * light

    def product(e):
        if e > held:
            return jnp.zeros((count * light, 2 * rank), jnp.float32)
        factor = down_ref[e] if e < held else down_ref[scalar_ref[1]]
        rows = [block_ref[e * light : (e + 1) * light, :] for block_ref in block_refs]
        value = jnp.dot(
            jnp.concatenate(rows, axis=0) if count > 1 else rows[0], factor, preferred_element_type=jnp.float32
        )
        return value if e < held else jnp.where(scalar_ref[2] == 1, value, 0.0)

    on_value_side = scalar_ref[0] >= value_side
    for g in range(groups):
        first, second = product(g), product(g + groups)
        key = jnp.concatenate([first[:, :rank], second[:, :rank]], axis=1)
        value = jnp.concatenate([first[:, rank:], second[:, rank:]], axis=1)
        mine, other = jnp.where(on_value_side, value, key), jnp.where(on_value_side, key, value)
        for n in range(count):
            here, start = slice(n * light, (n + 1) * light), n * height + g * light
            out_ref[start : start + light, :] = mine[here]
            out_ref[count * height + start : count * height + start + light, :] = other[here]
    for source, target in zip(passed_refs, left_refs):
        target[...] = source[...]


def hold_kernel(value_ref, *refs):
    refs[-1][...] = value_ref[...]


def split_pair(value):
    high = value.astype(jnp.bfloat16)
    low = (value - high.astype(jnp.float32)).astype(jnp.bfloat16)
    return high, low


def finish_kernel(homes, held, light, rank, shifts, waited, place_ref, index_ref, base_ref, up_ref, *refs):
    count = len(shifts)
    refs = refs[:count] + refs[count + waited :]
    shrink_refs, out_ref, high_ref, low_ref = refs[:count], refs[count], refs[count + 1], refs[count + 2]
    span = (held + 1) * light
    rows = base_ref.shape[0]
    groups = entry_places(held)
    local = []
    for n, r in enumerate(shifts):
        for e in range(held + 1):
            entry = r * held + e if e < held else place_ref[0]
            g, side = e % groups, e // groups
            high, low = split_pair(
                shrink_refs[n][g * light : (g + 1) * light, side * rank : (side + 1) * rank]
            )
            factor = up_ref[entry]
            delta = jnp.dot(high, factor, preferred_element_type=jnp.float32) + jnp.dot(
                low, factor, preferred_element_type=jnp.float32
            )
            high, low = split_pair(delta)
            start = n * span + e * light
            high_ref[start : start + light, :] = high
            low_ref[start : start + light, :] = low
        local.append(lax.broadcasted_iota(jnp.int32, (rows, span), 1) + r * span == index_ref[...])
    delta = base_ref[...]
    for n in range(count):
        choose = local[n].astype(jnp.bfloat16)
        delta = delta + adapter_scale * (
            jnp.dot(choose, high_ref[n * span : (n + 1) * span, :], preferred_element_type=jnp.float32)
            + jnp.dot(choose, low_ref[n * span : (n + 1) * span, :], preferred_element_type=jnp.float32)
        )
    out_ref[...] = delta.astype(out_ref.dtype)


def finish(scalars, index, base, up, shrinks, after, shifts, dtype, homes, held, light):
    rows, columns = base.shape
    span = (held + 1) * light
    return pl.pallas_call(
        functools.partial(finish_kernel, homes, held, light, up.shape[1], shifts, len(after)),
        out_shape=jax.ShapeDtypeStruct((rows, columns), dtype),
        in_specs=[SMEM] + [VMEM] * (3 + len(shifts)) + [ANY] * len(after),
        out_specs=VMEM,
        scratch_shapes=[pltpu.VMEM((len(shifts) * span, columns), jnp.bfloat16)] * 2,
        compiler_params=PARAMS,
        cost_estimate=COST,
        name="finish",
    )(scalars, index, base, up, *shrinks, *after)


def gate_kernel(waiting, *refs):
    refs[waiting][...] = jnp.zeros_like(refs[waiting])


def gate(blocks, after):
    return pl.pallas_call(
        functools.partial(gate_kernel, len(blocks) + len(after)),
        out_shape=[jax.ShapeDtypeStruct((8, 128), jnp.int32)]
        + [jax.ShapeDtypeStruct(b.shape, b.dtype) for b in blocks],
        in_specs=[HBM] * len(blocks) + [ANY] * len(after),
        out_specs=[VMEM] + [HBM] * len(blocks),
        input_output_aliases={n: n + 1 for n in range(len(blocks))},
        compiler_params=WIDE,
        cost_estimate=COST,
        name="gate",
    )(*blocks, *after)


def gather_up(adapter_up, homes):
    teams = lax.axis_size("groups")
    team = lax.axis_index("groups")
    share = adapter_up.shape[1] // teams
    own = lax.dynamic_slice_in_dim(adapter_up, team * share, share, 1)
    found = [
        lax.ppermute(own, "batch", [(i, (i - r) % homes) for i in range(homes)]) for r in range(1, homes)
    ]
    ordered = jnp.concatenate([own] + found, axis=0)
    shares = [ordered] + [
        lax.ppermute(ordered, "groups", [(i, (i + s) % teams) for i in range(teams)])
        for s in range(1, teams)
    ]
    return jnp.concatenate(
        [
            functools.reduce(
                lambda kept, s: jnp.where(lax.rem(team + teams - s, teams) == part, shares[s], kept),
                range(1, teams),
                shares[0],
            )
            for part in range(teams)
        ],
        axis=1,
    ), found


def base_kernel(waited, block_ref, tokens_ref, weight_ref, *refs):
    refs[waited][...] = jnp.dot(tokens_ref[...], weight_ref[...], preferred_element_type=jnp.float32)


def base_part(tokens, weight, blocks, columns, slab, slabs, after, params=PARAMS):
    rows, width = tokens.shape[0] // slabs, tokens.shape[1]
    count = blocks.shape[0]
    return pl.pallas_call(
        functools.partial(base_kernel, len(after)),
        out_shape=jax.ShapeDtypeStruct((rows, count * columns), jnp.float32),
        grid_spec=pltpu.PrefetchScalarGridSpec(
            num_scalar_prefetch=1,
            grid=(count,),
            in_specs=[
                pl.BlockSpec((rows, width), lambda j, chosen: (slab, 0)),
                pl.BlockSpec((width, columns), lambda j, chosen: (0, chosen[j])),
            ]
            + [ANY] * len(after),
            out_specs=pl.BlockSpec((rows, columns), lambda j, chosen: (0, j)),
        ),
        compiler_params=params,
        cost_estimate=COST,
        name="base",
    )(blocks, tokens, weight, *after)


def reduce_base(tokens, weight, piece, pieces, columns, slab, slabs, after):
    keep = [0]
    bit = pieces // 2
    while bit > 1:
        keep = keep + [p + bit for p in keep]
        bit //= 2
    keep = jnp.array(keep, jnp.int32)
    sent = base_part(
        tokens, weight, piece ^ keep ^ 1, columns, slab, slabs, after, PARAMS if slab else WIDE
    )
    kept = base_part(tokens, weight, piece ^ keep, columns, slab, slabs, [sent])
    bit, first = 1, None
    while True:
        kept = kept + lax.ppermute(sent, "tensor", [(i, i ^ bit) for i in range(pieces)])
        first = kept[:8] if first is None else first
        bit *= 2
        if bit >= pieces:
            return kept, first
        half = kept.shape[1] // 2
        kept, sent = kept[:, :half], kept[:, half:]


def on_device(tokens, request_adapter, adapter_entry, key_value_weight, adapter_down, adapter_up):
    rows, width = tokens.shape
    adapters = adapter_entry.shape[0]
    held, rank, columns = adapter_up.shape
    value_side = key_value_weight.shape[1] // 2 // columns
    homes = lax.axis_size("batch")
    pieces = lax.axis_size("tensor")
    place = lax.axis_index("batch").astype(jnp.int32)
    piece = lax.axis_index("tensor").astype(jnp.int32)
    light = rows // adapters
    span = (held + 1) * light
    order = sorted(range(1, homes), key=lambda r: (-min(r, homes - r), r))
    block_shape = jax.ShapeDtypeStruct((span, width), jnp.bfloat16)

    up, found = gather_up(adapter_up, homes)
    index, heavy = pl.pallas_call(
        functools.partial(route_kernel, homes, held, light),
        out_shape=[
            jax.ShapeDtypeStruct((1, rows), jnp.int32),
            jax.ShapeDtypeStruct((8, 128), jnp.int32),
        ],
        in_specs=[SMEM, HBM, HBM],
        out_specs=[VMEM] * 2,
        scratch_shapes=[
            pltpu.SMEM(adapter_entry.shape, jnp.int32),
            pltpu.VMEM((rows,), jnp.int32),
            pltpu.SemaphoreType.DMA((2,)),
        ],
        compiler_params=WIDE,
        cost_estimate=COST,
        name="route",
    )(place.reshape(1), adapter_entry, request_adapter)
    def pack(shifts):
        return pl.pallas_call(
            functools.partial(pack_kernel, span, shifts),
            out_shape=[jax.ShapeDtypeStruct((8, 128), jnp.int32)] + [block_shape] * len(shifts),
            in_specs=[VMEM] * 2,
            out_specs=[VMEM] + [HBM] * len(shifts),
            scratch_shapes=[
                pltpu.VMEM((len(shifts), span, width), jnp.bfloat16),
                pltpu.SemaphoreType.DMA((len(shifts),)),
            ],
            compiler_params=WIDE,
            cost_estimate=COST,
            name="pack",
        )(index, tokens)

    def send(block, r):
        return lax.ppermute(block, "batch", [(i, (i + r) % homes) for i in range(homes)])

    packed, own_block, *blocks = pack([0] + order)
    arrived = {0: own_block}
    mark, *blocks = gate(blocks, [packed])
    for r, block in zip(order, blocks):
        arrived[r] = send(block, r)

    heavy = heavy[0, 0]
    heavy_here = (heavy // held == place).astype(jnp.int32)
    scalars = jnp.stack([piece, lax.rem(heavy, held), heavy_here])
    height = entry_places(held) * light

    def shrink(blocks, after, passed):
        return pl.pallas_call(
            functools.partial(
                shrink_kernel, held, light, rank, value_side, len(blocks), len(after), len(passed)
            ),
            out_shape=[jax.ShapeDtypeStruct((2 * len(blocks) * height, 2 * rank), jnp.float32)]
            + [jax.ShapeDtypeStruct(p.shape, p.dtype) for p in passed],
            in_specs=[SMEM] + [VMEM] * (len(blocks) + 1) + [ANY] * len(after) + [VMEM] * len(passed),
            out_specs=[VMEM] * (1 + len(passed)),
            compiler_params=PARAMS,
            cost_estimate=COST,
            name="shrink",
        )(scalars, *blocks, adapter_down, *after, *passed)

    def hold(value, after):
        return pl.pallas_call(
            hold_kernel,
            out_shape=jax.ShapeDtypeStruct(value.shape, value.dtype),
            in_specs=[VMEM] + [ANY] * len(after),
            out_specs=VMEM,
            compiler_params=PARAMS,
            cost_estimate=COST,
            name="hold",
        )(value, *after)

    def combine(value, after=()):
        bit, half = 1, value.shape[0] // 2
        while bit < pieces // 2:
            value = value + lax.ppermute(value, "tensor", [(i, i ^ bit) for i in range(pieces)])
            bit *= 2
        if after:
            value = hold(value, after)
        return value[:half] + lax.ppermute(value[half:], "tensor", [(i, i ^ bit) for i in range(pieces)])

    slabs = 3
    slab_sums = [
        reduce_base(tokens, key_value_weight, piece, pieces, columns, slab, slabs, [mark] + found)
        for slab in range(slabs)
    ]
    base = jnp.concatenate([total for total, _ in slab_sums], axis=0)
    begun = [first for _, first in slab_sums]
    whole = [total[:8] for total, _ in slab_sums[:1]]
    late = order[-2:]
    early = order[:-2] + [0]
    totals, far = [], [packed]
    for r in early:
        (value,) = shrink([arrived[r]], begun if r else far, [])
        far = [value]
        totals.append(combine(value, whole if r else ()))
    value, *totals = shrink([arrived[r] for r in late], [base[:8], base[-8:]], totals)
    last = combine(value)

    def give_back(total, r):
        return lax.ppermute(total, "batch", [(i, (i - r) % homes) for i in range(homes)]) if r else total

    shrinks = [give_back(total, r) for total, r in zip(totals, early)]
    places = lax.rem(heavy - place * held + adapters, adapters).reshape(1)
    column = index.reshape(rows, 1)
    running = finish(places, column, base, up, shrinks, [last], early, jnp.float32, homes, held, light)
    shrinks = [give_back(last[n * height : (n + 1) * height], r) for n, r in enumerate(late)]
    return finish(places, column, running, up, shrinks, [], late, jnp.bfloat16, homes, held, light)


def solution(mesh):
    in_specs = (
        P(("groups", "batch"), "tensor"),
        P(("groups", "batch")),
        P(),
        P("tensor", None),
        P("batch", "tensor", None),
        P("batch", None, "tensor"),
    )
    out_specs = P(("groups", "batch"), "tensor")
    return jax.shard_map(
        on_device, mesh=mesh, in_specs=in_specs, out_specs=out_specs, check_vma=False
    )
```

```python
import functools

import jax
import jax.numpy as jnp
from jax import lax
from jax.experimental import pallas as pl
from jax.experimental.pallas import tpu as pltpu
from jax.sharding import PartitionSpec as P

adapter_scale = 0.5
VMEM_BYTES = 24 * 1024 * 1024
WIDE = pltpu.CompilerParams(vmem_limit_bytes=60 * 1024 * 1024)
VMEM = pl.BlockSpec(memory_space=pltpu.VMEM)
ANY = pl.BlockSpec(memory_space=pl.ANY)
HBM = pl.BlockSpec(memory_space=pltpu.HBM)
SMEM = pl.BlockSpec(memory_space=pltpu.SMEM)
COST = pl.CostEstimate(flops=1, bytes_accessed=1, transcendentals=0)
PARAMS = pltpu.CompilerParams(vmem_limit_bytes=VMEM_BYTES)


def place_rows(index, start, tokens_ref, block_ref):
    local = lax.broadcasted_iota(jnp.int32, (block_ref.shape[0], index.shape[1]), 0)
    choose = (local + start == index).astype(jnp.bfloat16)
    block_ref[...] = jnp.dot(
        choose, tokens_ref[...], preferred_element_type=jnp.float32
    ).astype(jnp.bfloat16)


def route_kernel(
    homes, held, light, place_ref, entry_hbm, request_hbm, index_ref, heavy_ref, entry_ref, request_ref, sems
):
    loads = [
        pltpu.make_async_copy(source, target, sems.at[n])
        for n, (source, target) in enumerate(
            [(request_hbm, request_ref), (entry_hbm, entry_ref)]
        )
    ]
    for load in loads:
        load.start()
    rows = request_ref.shape[0]
    adapters = entry_ref.shape[0]
    span = (held + 1) * light
    earlier = (
        lax.broadcasted_iota(jnp.int32, (rows, rows), 0) < lax.broadcasted_iota(jnp.int32, (rows, rows), 1)
    ).astype(jnp.bfloat16)
    loads[0].wait()
    request = request_ref[...].reshape(1, rows)
    onehot = lax.broadcasted_iota(jnp.int32, (adapters, rows), 0) == request
    before = jnp.dot(onehot.astype(jnp.bfloat16), earlier, preferred_element_type=jnp.float32)
    position = jnp.sum(jnp.where(onehot, before, 0.0), axis=0, keepdims=True).astype(jnp.int32)
    loads[1].wait()
    slot = jnp.zeros_like(position)
    for a in range(adapters):
        slot = jnp.where(request == a, entry_ref[a], slot)
    home = slot // held
    relative = lax.rem(home - place_ref[0] + homes, homes)
    inside = jnp.where(
        position < light, (slot - home * held) * light + position, held * light + position - light
    )
    index = relative * span + inside
    index_ref[...] = index
    heavy = jnp.max(jnp.where(position >= light, slot, 0), axis=1, keepdims=True)
    heavy_ref[...] = jnp.broadcast_to(heavy, heavy_ref.shape)


def pack_kernel(span, shifts, index_ref, tokens_ref, mark_ref, *refs):
    count = len(shifts)
    block_refs, buffer, sems = refs[:count], refs[count], refs[count + 1]
    mark_ref[...] = jnp.zeros_like(mark_ref)
    stores = []
    for n, shift in enumerate(shifts):
        place_rows(index_ref[...], shift * span, tokens_ref, buffer.at[n])
        stores.append(pltpu.make_async_copy(buffer.at[n], block_refs[n], sems.at[n]))
        stores[-1].start()
    for store in stores:
        store.wait()


def entry_places(held):
    return (held + 2) // 2


def shrink_kernel(held, light, rank, value_side, count, waited, passed, scalar_ref, *refs):
    block_refs, down_ref, refs = refs[:count], refs[count], refs[count + 1 + waited :]
    passed_refs, out_ref, left_refs = refs[:passed], refs[passed], refs[passed + 1 :]
    groups = entry_places(held)
    height = groups * light

    def product(e):
        if e > held:
            return jnp.zeros((count * light, 2 * rank), jnp.float32)
        factor = down_ref[e] if e < held else down_ref[scalar_ref[1]]
        rows = [block_ref[e * light : (e + 1) * light, :] for block_ref in block_refs]
        value = jnp.dot(
            jnp.concatenate(rows, axis=0) if count > 1 else rows[0], factor, preferred_element_type=jnp.float32
        )
        return value if e < held else jnp.where(scalar_ref[2] == 1, value, 0.0)

    on_value_side = scalar_ref[0] >= value_side
    for g in range(groups):
        first, second = product(g), product(g + groups)
        key = jnp.concatenate([first[:, :rank], second[:, :rank]], axis=1)
        value = jnp.concatenate([first[:, rank:], second[:, rank:]], axis=1)
        mine, other = jnp.where(on_value_side, value, key), jnp.where(on_value_side, key, value)
        for n in range(count):
            here, start = slice(n * light, (n + 1) * light), n * height + g * light
            out_ref[start : start + light, :] = mine[here]
            out_ref[count * height + start : count * height + start + light, :] = other[here]
    for source, target in zip(passed_refs, left_refs):
        target[...] = source[...]


def hold_kernel(value_ref, *refs):
    refs[-1][...] = value_ref[...]


def split_pair(value):
    high = value.astype(jnp.bfloat16)
    low = (value - high.astype(jnp.float32)).astype(jnp.bfloat16)
    return high, low


def finish_kernel(homes, held, light, rank, shifts, waited, place_ref, index_ref, base_ref, up_ref, *refs):
    count = len(shifts)
    refs = refs[:count] + refs[count + waited :]
    shrink_refs, out_ref, high_ref, low_ref = refs[:count], refs[count], refs[count + 1], refs[count + 2]
    span = (held + 1) * light
    rows = base_ref.shape[0]
    groups = entry_places(held)
    local = []
    for n, r in enumerate(shifts):
        for e in range(held + 1):
            entry = r * held + e if e < held else place_ref[0]
            g, side = e % groups, e // groups
            high, low = split_pair(
                shrink_refs[n][g * light : (g + 1) * light, side * rank : (side + 1) * rank]
            )
            factor = up_ref[entry]
            delta = jnp.dot(high, factor, preferred_element_type=jnp.float32) + jnp.dot(
                low, factor, preferred_element_type=jnp.float32
            )
            high, low = split_pair(delta)
            start = n * span + e * light
            high_ref[start : start + light, :] = high
            low_ref[start : start + light, :] = low
        local.append(lax.broadcasted_iota(jnp.int32, (rows, span), 1) + r * span == index_ref[...])
    delta = base_ref[...]
    for n in range(count):
        choose = local[n].astype(jnp.bfloat16)
        delta = delta + adapter_scale * (
            jnp.dot(choose, high_ref[n * span : (n + 1) * span, :], preferred_element_type=jnp.float32)
            + jnp.dot(choose, low_ref[n * span : (n + 1) * span, :], preferred_element_type=jnp.float32)
        )
    out_ref[...] = delta.astype(out_ref.dtype)


def finish(scalars, index, base, up, shrinks, after, shifts, dtype, homes, held, light):
    rows, columns = base.shape
    span = (held + 1) * light
    return pl.pallas_call(
        functools.partial(finish_kernel, homes, held, light, up.shape[1], shifts, len(after)),
        out_shape=jax.ShapeDtypeStruct((rows, columns), dtype),
        in_specs=[SMEM] + [VMEM] * (3 + len(shifts)) + [ANY] * len(after),
        out_specs=VMEM,
        scratch_shapes=[pltpu.VMEM((len(shifts) * span, columns), jnp.bfloat16)] * 2,
        compiler_params=PARAMS,
        cost_estimate=COST,
        name="finish",
    )(scalars, index, base, up, *shrinks, *after)


def gate_kernel(waiting, *refs):
    refs[waiting][...] = jnp.zeros_like(refs[waiting])


def gate(blocks, after):
    return pl.pallas_call(
        functools.partial(gate_kernel, len(blocks) + len(after)),
        out_shape=[jax.ShapeDtypeStruct((8, 128), jnp.int32)]
        + [jax.ShapeDtypeStruct(b.shape, b.dtype) for b in blocks],
        in_specs=[HBM] * len(blocks) + [ANY] * len(after),
        out_specs=[VMEM] + [HBM] * len(blocks),
        input_output_aliases={n: n + 1 for n in range(len(blocks))},
        compiler_params=WIDE,
        cost_estimate=COST,
        name="gate",
    )(*blocks, *after)


def gather_up(adapter_up, homes):
    teams = lax.axis_size("groups")
    team = lax.axis_index("groups")
    share = adapter_up.shape[1] // teams
    own = lax.dynamic_slice_in_dim(adapter_up, team * share, share, 1)
    found = [
        lax.ppermute(own, "batch", [(i, (i - r) % homes) for i in range(homes)]) for r in range(1, homes)
    ]
    ordered = jnp.concatenate([own] + found, axis=0)
    shares = [ordered] + [
        lax.ppermute(ordered, "groups", [(i, (i + s) % teams) for i in range(teams)])
        for s in range(1, teams)
    ]
    return jnp.concatenate(
        [
            functools.reduce(
                lambda kept, s: jnp.where(lax.rem(team + teams - s, teams) == part, shares[s], kept),
                range(1, teams),
                shares[0],
            )
            for part in range(teams)
        ],
        axis=1,
    ), found


def base_kernel(waited, block_ref, tokens_ref, weight_ref, *refs):
    refs[waited][...] = jnp.dot(tokens_ref[...], weight_ref[...], preferred_element_type=jnp.float32)


def base_part(tokens, weight, blocks, columns, slab, slabs, after, params=PARAMS):
    rows, width = tokens.shape[0] // slabs, tokens.shape[1]
    count = blocks.shape[0]
    return pl.pallas_call(
        functools.partial(base_kernel, len(after)),
        out_shape=jax.ShapeDtypeStruct((rows, count * columns), jnp.float32),
        grid_spec=pltpu.PrefetchScalarGridSpec(
            num_scalar_prefetch=1,
            grid=(count,),
            in_specs=[
                pl.BlockSpec((rows, width), lambda j, chosen: (slab, 0)),
                pl.BlockSpec((width, columns), lambda j, chosen: (0, chosen[j])),
            ]
            + [ANY] * len(after),
            out_specs=pl.BlockSpec((rows, columns), lambda j, chosen: (0, j)),
        ),
        compiler_params=params,
        cost_estimate=COST,
        name="base",
    )(blocks, tokens, weight, *after)


def reduce_base(tokens, weight, piece, pieces, columns, slab, slabs, after):
    keep = [0]
    bit = pieces // 2
    while bit > 1:
        keep = keep + [p + bit for p in keep]
        bit //= 2
    keep = jnp.array(keep, jnp.int32)
    sent = base_part(
        tokens, weight, piece ^ keep ^ 1, columns, slab, slabs, after, PARAMS if slab else WIDE
    )
    kept = base_part(tokens, weight, piece ^ keep, columns, slab, slabs, [sent])
    bit, first = 1, None
    while True:
        kept = kept + lax.ppermute(sent, "tensor", [(i, i ^ bit) for i in range(pieces)])
        first = kept[:8] if first is None else first
        bit *= 2
        if bit >= pieces:
            return kept, first
        half = kept.shape[1] // 2
        kept, sent = kept[:, :half], kept[:, half:]


def on_device(tokens, request_adapter, adapter_entry, key_value_weight, adapter_down, adapter_up):
    rows, width = tokens.shape
    adapters = adapter_entry.shape[0]
    held, rank, columns = adapter_up.shape
    value_side = key_value_weight.shape[1] // 2 // columns
    homes = lax.axis_size("batch")
    pieces = lax.axis_size("tensor")
    place = lax.axis_index("batch").astype(jnp.int32)
    piece = lax.axis_index("tensor").astype(jnp.int32)
    light = rows // adapters
    span = (held + 1) * light
    order = sorted(range(1, homes), key=lambda r: (-min(r, homes - r), r))
    block_shape = jax.ShapeDtypeStruct((span, width), jnp.bfloat16)

    up, found = gather_up(adapter_up, homes)
    index, heavy = pl.pallas_call(
        functools.partial(route_kernel, homes, held, light),
        out_shape=[
            jax.ShapeDtypeStruct((1, rows), jnp.int32),
            jax.ShapeDtypeStruct((8, 128), jnp.int32),
        ],
        in_specs=[SMEM, HBM, HBM],
        out_specs=[VMEM] * 2,
        scratch_shapes=[
            pltpu.SMEM(adapter_entry.shape, jnp.int32),
            pltpu.VMEM((rows,), jnp.int32),
            pltpu.SemaphoreType.DMA((2,)),
        ],
        compiler_params=WIDE,
        cost_estimate=COST,
        name="route",
    )(place.reshape(1), adapter_entry, request_adapter)
    def pack(shifts):
        return pl.pallas_call(
            functools.partial(pack_kernel, span, shifts),
            out_shape=[jax.ShapeDtypeStruct((8, 128), jnp.int32)] + [block_shape] * len(shifts),
            in_specs=[VMEM] * 2,
            out_specs=[VMEM] + [HBM] * len(shifts),
            scratch_shapes=[
                pltpu.VMEM((len(shifts), span, width), jnp.bfloat16),
                pltpu.SemaphoreType.DMA((len(shifts),)),
            ],
            compiler_params=WIDE,
            cost_estimate=COST,
            name="pack",
        )(index, tokens)

    def send(block, r):
        return lax.ppermute(block, "batch", [(i, (i + r) % homes) for i in range(homes)])

    packed, own_block, *blocks = pack([0] + order)
    arrived = {0: own_block}
    mark, *blocks = gate(blocks, found)
    for r, block in zip(order, blocks):
        arrived[r] = send(block, r)

    heavy = heavy[0, 0]
    heavy_here = (heavy // held == place).astype(jnp.int32)
    scalars = jnp.stack([piece, lax.rem(heavy, held), heavy_here])
    height = entry_places(held) * light

    def shrink(blocks, after, passed):
        return pl.pallas_call(
            functools.partial(
                shrink_kernel, held, light, rank, value_side, len(blocks), len(after), len(passed)
            ),
            out_shape=[jax.ShapeDtypeStruct((2 * len(blocks) * height, 2 * rank), jnp.float32)]
            + [jax.ShapeDtypeStruct(p.shape, p.dtype) for p in passed],
            in_specs=[SMEM] + [VMEM] * (len(blocks) + 1) + [ANY] * len(after) + [VMEM] * len(passed),
            out_specs=[VMEM] * (1 + len(passed)),
            compiler_params=PARAMS,
            cost_estimate=COST,
            name="shrink",
        )(scalars, *blocks, adapter_down, *after, *passed)

    def hold(value, after):
        return pl.pallas_call(
            hold_kernel,
            out_shape=jax.ShapeDtypeStruct(value.shape, value.dtype),
            in_specs=[VMEM] + [ANY] * len(after),
            out_specs=VMEM,
            compiler_params=PARAMS,
            cost_estimate=COST,
            name="hold",
        )(value, *after)

    def combine(value, after=()):
        bit, half = 1, value.shape[0] // 2
        while bit < pieces // 2:
            value = value + lax.ppermute(value, "tensor", [(i, i ^ bit) for i in range(pieces)])
            bit *= 2
        if after:
            value = hold(value, after)
        return value[:half] + lax.ppermute(value[half:], "tensor", [(i, i ^ bit) for i in range(pieces)])

    slabs = 3
    slab_sums = [
        reduce_base(tokens, key_value_weight, piece, pieces, columns, slab, slabs, [mark])
        for slab in range(slabs)
    ]
    base = jnp.concatenate([total for total, _ in slab_sums], axis=0)
    begun = [first for _, first in slab_sums]
    whole = [total[:8] for total, _ in slab_sums[:1]]
    late = order[-2:]
    early = order[:-2] + [0]
    totals, far = [], [packed]
    for r in early:
        (value,) = shrink([arrived[r]], begun if r else far, [])
        far = [value]
        totals.append(combine(value, whole if r else ()))
    value, *totals = shrink([arrived[r] for r in late], [base[:8], base[-8:]], totals)
    last = combine(value)

    def give_back(total, r):
        return lax.ppermute(total, "batch", [(i, (i - r) % homes) for i in range(homes)]) if r else total

    shrinks = [give_back(total, r) for total, r in zip(totals, early)]
    places = lax.rem(heavy - place * held + adapters, adapters).reshape(1)
    column = index.reshape(rows, 1)
    running = finish(places, column, base, up, shrinks, [last], early, jnp.float32, homes, held, light)
    shrinks = [give_back(last[n * height : (n + 1) * height], r) for n, r in enumerate(late)]
    return finish(places, column, running, up, shrinks, [], late, jnp.bfloat16, homes, held, light)


def solution(mesh):
    in_specs = (
        P(("groups", "batch"), "tensor"),
        P(("groups", "batch")),
        P(),
        P("tensor", None),
        P("batch", "tensor", None),
        P("batch", None, "tensor"),
    )
    out_specs = P(("groups", "batch"), "tensor")
    return jax.shard_map(
        on_device, mesh=mesh, in_specs=in_specs, out_specs=out_specs, check_vma=False
    )
```

```python
import functools

import jax
import jax.numpy as jnp
from jax import lax
from jax.experimental import pallas as pl
from jax.experimental.pallas import tpu as pltpu
from jax.sharding import PartitionSpec as P

adapter_scale = 0.5
VMEM_BYTES = 24 * 1024 * 1024
WIDE = pltpu.CompilerParams(vmem_limit_bytes=60 * 1024 * 1024)
VMEM = pl.BlockSpec(memory_space=pltpu.VMEM)
ANY = pl.BlockSpec(memory_space=pl.ANY)
HBM = pl.BlockSpec(memory_space=pltpu.HBM)
SMEM = pl.BlockSpec(memory_space=pltpu.SMEM)
COST = pl.CostEstimate(flops=1, bytes_accessed=1, transcendentals=0)
PARAMS = pltpu.CompilerParams(vmem_limit_bytes=VMEM_BYTES)


def place_rows(index, start, tokens_ref, block_ref):
    local = lax.broadcasted_iota(jnp.int32, (block_ref.shape[0], index.shape[1]), 0)
    choose = (local + start == index).astype(jnp.bfloat16)
    block_ref[...] = jnp.dot(
        choose, tokens_ref[...], preferred_element_type=jnp.float32
    ).astype(jnp.bfloat16)


def route_kernel(
    homes, held, light, place_ref, entry_hbm, request_hbm, index_ref, heavy_ref, entry_ref, request_ref, sems
):
    loads = [
        pltpu.make_async_copy(source, target, sems.at[n])
        for n, (source, target) in enumerate(
            [(request_hbm, request_ref), (entry_hbm, entry_ref)]
        )
    ]
    for load in loads:
        load.start()
    rows = request_ref.shape[0]
    adapters = entry_ref.shape[0]
    span = (held + 1) * light
    earlier = (
        lax.broadcasted_iota(jnp.int32, (rows, rows), 0) < lax.broadcasted_iota(jnp.int32, (rows, rows), 1)
    ).astype(jnp.bfloat16)
    loads[0].wait()
    request = request_ref[...].reshape(1, rows)
    onehot = lax.broadcasted_iota(jnp.int32, (adapters, rows), 0) == request
    before = jnp.dot(onehot.astype(jnp.bfloat16), earlier, preferred_element_type=jnp.float32)
    position = jnp.sum(jnp.where(onehot, before, 0.0), axis=0, keepdims=True).astype(jnp.int32)
    loads[1].wait()
    slot = jnp.zeros_like(position)
    for a in range(adapters):
        slot = jnp.where(request == a, entry_ref[a], slot)
    home = slot // held
    relative = lax.rem(home - place_ref[0] + homes, homes)
    inside = jnp.where(
        position < light, (slot - home * held) * light + position, held * light + position - light
    )
    index = relative * span + inside
    index_ref[...] = index
    heavy = jnp.max(jnp.where(position >= light, slot, 0), axis=1, keepdims=True)
    heavy_ref[...] = jnp.broadcast_to(heavy, heavy_ref.shape)


def pack_kernel(span, shifts, waited, index_ref, tokens_ref, *refs):
    mark_ref, *refs = refs[waited:]
    count = len(shifts)
    block_refs, buffer, sems = refs[:count], refs[count], refs[count + 1]
    mark_ref[...] = jnp.zeros_like(mark_ref)
    stores = []
    for n, shift in enumerate(shifts):
        place_rows(index_ref[...], shift * span, tokens_ref, buffer.at[n])
        stores.append(pltpu.make_async_copy(buffer.at[n], block_refs[n], sems.at[n]))
        stores[-1].start()
    for store in stores:
        store.wait()


def entry_places(held):
    return (held + 2) // 2


def shrink_kernel(held, light, rank, value_side, count, waited, passed, scalar_ref, *refs):
    block_refs, down_ref, refs = refs[:count], refs[count], refs[count + 1 + waited :]
    passed_refs, out_ref, left_refs = refs[:passed], refs[passed], refs[passed + 1 :]
    groups = entry_places(held)
    height = groups * light

    def product(e):
        if e > held:
            return jnp.zeros((count * light, 2 * rank), jnp.float32)
        factor = down_ref[e] if e < held else down_ref[scalar_ref[1]]
        rows = [block_ref[e * light : (e + 1) * light, :] for block_ref in block_refs]
        value = jnp.dot(
            jnp.concatenate(rows, axis=0) if count > 1 else rows[0], factor, preferred_element_type=jnp.float32
        )
        return value if e < held else jnp.where(scalar_ref[2] == 1, value, 0.0)

    on_value_side = scalar_ref[0] >= value_side
    for g in range(groups):
        first, second = product(g), product(g + groups)
        key = jnp.concatenate([first[:, :rank], second[:, :rank]], axis=1)
        value = jnp.concatenate([first[:, rank:], second[:, rank:]], axis=1)
        mine, other = jnp.where(on_value_side, value, key), jnp.where(on_value_side, key, value)
        for n in range(count):
            here, start = slice(n * light, (n + 1) * light), n * height + g * light
            out_ref[start : start + light, :] = mine[here]
            out_ref[count * height + start : count * height + start + light, :] = other[here]
    for source, target in zip(passed_refs, left_refs):
        target[...] = source[...]


def hold_kernel(value_ref, *refs):
    refs[-1][...] = value_ref[...]


def split_pair(value):
    high = value.astype(jnp.bfloat16)
    low = (value - high.astype(jnp.float32)).astype(jnp.bfloat16)
    return high, low


def finish_kernel(homes, held, light, rank, shifts, waited, place_ref, index_ref, base_ref, up_ref, *refs):
    count = len(shifts)
    refs = refs[:count] + refs[count + waited :]
    shrink_refs, out_ref, high_ref, low_ref = refs[:count], refs[count], refs[count + 1], refs[count + 2]
    span = (held + 1) * light
    rows = base_ref.shape[0]
    groups = entry_places(held)
    local = []
    for n, r in enumerate(shifts):
        for e in range(held + 1):
            entry = r * held + e if e < held else place_ref[0]
            g, side = e % groups, e // groups
            high, low = split_pair(
                shrink_refs[n][g * light : (g + 1) * light, side * rank : (side + 1) * rank]
            )
            factor = up_ref[entry]
            delta = jnp.dot(high, factor, preferred_element_type=jnp.float32) + jnp.dot(
                low, factor, preferred_element_type=jnp.float32
            )
            high, low = split_pair(delta)
            start = n * span + e * light
            high_ref[start : start + light, :] = high
            low_ref[start : start + light, :] = low
        local.append(lax.broadcasted_iota(jnp.int32, (rows, span), 1) + r * span == index_ref[...])
    delta = base_ref[...]
    for n in range(count):
        choose = local[n].astype(jnp.bfloat16)
        delta = delta + adapter_scale * (
            jnp.dot(choose, high_ref[n * span : (n + 1) * span, :], preferred_element_type=jnp.float32)
            + jnp.dot(choose, low_ref[n * span : (n + 1) * span, :], preferred_element_type=jnp.float32)
        )
    out_ref[...] = delta.astype(out_ref.dtype)


def finish(scalars, index, base, up, shrinks, after, shifts, dtype, homes, held, light):
    rows, columns = base.shape
    span = (held + 1) * light
    return pl.pallas_call(
        functools.partial(finish_kernel, homes, held, light, up.shape[1], shifts, len(after)),
        out_shape=jax.ShapeDtypeStruct((rows, columns), dtype),
        in_specs=[SMEM] + [VMEM] * (3 + len(shifts)) + [ANY] * len(after),
        out_specs=VMEM,
        scratch_shapes=[pltpu.VMEM((len(shifts) * span, columns), jnp.bfloat16)] * 2,
        compiler_params=PARAMS,
        cost_estimate=COST,
        name="finish",
    )(scalars, index, base, up, *shrinks, *after)


def gate_kernel(waiting, *refs):
    refs[waiting][...] = jnp.zeros_like(refs[waiting])


def gate(blocks, after):
    return pl.pallas_call(
        functools.partial(gate_kernel, len(blocks) + len(after)),
        out_shape=[jax.ShapeDtypeStruct((8, 128), jnp.int32)]
        + [jax.ShapeDtypeStruct(b.shape, b.dtype) for b in blocks],
        in_specs=[HBM] * len(blocks) + [ANY] * len(after),
        out_specs=[VMEM] + [HBM] * len(blocks),
        input_output_aliases={n: n + 1 for n in range(len(blocks))},
        compiler_params=WIDE,
        cost_estimate=COST,
        name="gate",
    )(*blocks, *after)


def gather_up(adapter_up, homes):
    teams = lax.axis_size("groups")
    team = lax.axis_index("groups")
    share = adapter_up.shape[1] // teams
    own = lax.dynamic_slice_in_dim(adapter_up, team * share, share, 1)
    found = [
        lax.ppermute(own, "batch", [(i, (i - r) % homes) for i in range(homes)]) for r in range(1, homes)
    ]
    ordered = jnp.concatenate([own] + found, axis=0)
    shares = [ordered] + [
        lax.ppermute(ordered, "groups", [(i, (i + s) % teams) for i in range(teams)])
        for s in range(1, teams)
    ]
    return jnp.concatenate(
        [
            functools.reduce(
                lambda kept, s: jnp.where(lax.rem(team + teams - s, teams) == part, shares[s], kept),
                range(1, teams),
                shares[0],
            )
            for part in range(teams)
        ],
        axis=1,
    ), found


def base_kernel(waited, block_ref, tokens_ref, weight_ref, *refs):
    refs[waited][...] = jnp.dot(tokens_ref[...], weight_ref[...], preferred_element_type=jnp.float32)


def base_part(tokens, weight, blocks, columns, slab, slabs, after, params=PARAMS):
    rows, width = tokens.shape[0] // slabs, tokens.shape[1]
    count = blocks.shape[0]
    return pl.pallas_call(
        functools.partial(base_kernel, len(after)),
        out_shape=jax.ShapeDtypeStruct((rows, count * columns), jnp.float32),
        grid_spec=pltpu.PrefetchScalarGridSpec(
            num_scalar_prefetch=1,
            grid=(count,),
            in_specs=[
                pl.BlockSpec((rows, width), lambda j, chosen: (slab, 0)),
                pl.BlockSpec((width, columns), lambda j, chosen: (0, chosen[j])),
            ]
            + [ANY] * len(after),
            out_specs=pl.BlockSpec((rows, columns), lambda j, chosen: (0, j)),
        ),
        compiler_params=params,
        cost_estimate=COST,
        name="base",
    )(blocks, tokens, weight, *after)


def reduce_base(tokens, weight, piece, pieces, columns, slab, slabs, after):
    keep = [0]
    bit = pieces // 2
    while bit > 1:
        keep = keep + [p + bit for p in keep]
        bit //= 2
    keep = jnp.array(keep, jnp.int32)
    sent = base_part(
        tokens, weight, piece ^ keep ^ 1, columns, slab, slabs, after, PARAMS if slab else WIDE
    )
    kept = base_part(tokens, weight, piece ^ keep, columns, slab, slabs, [sent])
    bit, first = 1, None
    while True:
        kept = kept + lax.ppermute(sent, "tensor", [(i, i ^ bit) for i in range(pieces)])
        first = kept[:8] if first is None else first
        bit *= 2
        if bit >= pieces:
            return kept, first
        half = kept.shape[1] // 2
        kept, sent = kept[:, :half], kept[:, half:]


def on_device(tokens, request_adapter, adapter_entry, key_value_weight, adapter_down, adapter_up):
    rows, width = tokens.shape
    adapters = adapter_entry.shape[0]
    held, rank, columns = adapter_up.shape
    value_side = key_value_weight.shape[1] // 2 // columns
    homes = lax.axis_size("batch")
    pieces = lax.axis_size("tensor")
    place = lax.axis_index("batch").astype(jnp.int32)
    piece = lax.axis_index("tensor").astype(jnp.int32)
    light = rows // adapters
    span = (held + 1) * light
    order = sorted(range(1, homes), key=lambda r: (-min(r, homes - r), r))
    block_shape = jax.ShapeDtypeStruct((span, width), jnp.bfloat16)

    up, found = gather_up(adapter_up, homes)
    index, heavy = pl.pallas_call(
        functools.partial(route_kernel, homes, held, light),
        out_shape=[
            jax.ShapeDtypeStruct((1, rows), jnp.int32),
            jax.ShapeDtypeStruct((8, 128), jnp.int32),
        ],
        in_specs=[SMEM, HBM, HBM],
        out_specs=[VMEM] * 2,
        scratch_shapes=[
            pltpu.SMEM(adapter_entry.shape, jnp.int32),
            pltpu.VMEM((rows,), jnp.int32),
            pltpu.SemaphoreType.DMA((2,)),
        ],
        compiler_params=WIDE,
        cost_estimate=COST,
        name="route",
    )(place.reshape(1), adapter_entry, request_adapter)
    def pack(shifts, after):
        return pl.pallas_call(
            functools.partial(pack_kernel, span, shifts, len(after)),
            out_shape=[jax.ShapeDtypeStruct((8, 128), jnp.int32)] + [block_shape] * len(shifts),
            in_specs=[VMEM] * 2 + [ANY] * len(after),
            out_specs=[VMEM] + [HBM] * len(shifts),
            scratch_shapes=[
                pltpu.VMEM((len(shifts), span, width), jnp.bfloat16),
                pltpu.SemaphoreType.DMA((len(shifts),)),
            ],
            compiler_params=WIDE,
            cost_estimate=COST,
            name="pack",
        )(index, tokens, *after)

    def send(block, r):
        return lax.ppermute(block, "batch", [(i, (i + r) % homes) for i in range(homes)])

    packed, *blocks = pack(order, [])
    mark, *blocks = gate(blocks, [packed])
    _, own_block = pack([0], [mark])
    arrived = {0: own_block}
    for r, block in zip(order, blocks):
        arrived[r] = send(block, r)

    heavy = heavy[0, 0]
    heavy_here = (heavy // held == place).astype(jnp.int32)
    scalars = jnp.stack([piece, lax.rem(heavy, held), heavy_here])
    height = entry_places(held) * light

    def shrink(blocks, after, passed):
        return pl.pallas_call(
            functools.partial(
                shrink_kernel, held, light, rank, value_side, len(blocks), len(after), len(passed)
            ),
            out_shape=[jax.ShapeDtypeStruct((2 * len(blocks) * height, 2 * rank), jnp.float32)]
            + [jax.ShapeDtypeStruct(p.shape, p.dtype) for p in passed],
            in_specs=[SMEM] + [VMEM] * (len(blocks) + 1) + [ANY] * len(after) + [VMEM] * len(passed),
            out_specs=[VMEM] * (1 + len(passed)),
            compiler_params=PARAMS,
            cost_estimate=COST,
            name="shrink",
        )(scalars, *blocks, adapter_down, *after, *passed)

    def hold(value, after):
        return pl.pallas_call(
            hold_kernel,
            out_shape=jax.ShapeDtypeStruct(value.shape, value.dtype),
            in_specs=[VMEM] + [ANY] * len(after),
            out_specs=VMEM,
            compiler_params=PARAMS,
            cost_estimate=COST,
            name="hold",
        )(value, *after)

    def combine(value, after=()):
        bit, half = 1, value.shape[0] // 2
        while bit < pieces // 2:
            value = value + lax.ppermute(value, "tensor", [(i, i ^ bit) for i in range(pieces)])
            bit *= 2
        if after:
            value = hold(value, after)
        return value[:half] + lax.ppermute(value[half:], "tensor", [(i, i ^ bit) for i in range(pieces)])

    slabs = 3
    slab_sums = [
        reduce_base(tokens, key_value_weight, piece, pieces, columns, slab, slabs, [mark] + found)
        for slab in range(slabs)
    ]
    base = jnp.concatenate([total for total, _ in slab_sums], axis=0)
    begun = [first for _, first in slab_sums]
    whole = [total[:8] for total, _ in slab_sums[:1]]
    late = order[-2:]
    early = order[:-2] + [0]
    totals, far = [], [packed]
    for r in early:
        (value,) = shrink([arrived[r]], begun if r else far, [])
        far = [value]
        totals.append(combine(value, whole if r else ()))
    value, *totals = shrink([arrived[r] for r in late], [base[:8], base[-8:]], totals)
    last = combine(value)

    def give_back(total, r):
        return lax.ppermute(total, "batch", [(i, (i - r) % homes) for i in range(homes)]) if r else total

    shrinks = [give_back(total, r) for total, r in zip(totals, early)]
    places = lax.rem(heavy - place * held + adapters, adapters).reshape(1)
    column = index.reshape(rows, 1)
    running = finish(places, column, base, up, shrinks, [last], early, jnp.float32, homes, held, light)
    shrinks = [give_back(last[n * height : (n + 1) * height], r) for n, r in enumerate(late)]
    return finish(places, column, running, up, shrinks, [], late, jnp.bfloat16, homes, held, light)


def solution(mesh):
    in_specs = (
        P(("groups", "batch"), "tensor"),
        P(("groups", "batch")),
        P(),
        P("tensor", None),
        P("batch", "tensor", None),
        P("batch", None, "tensor"),
    )
    out_specs = P(("groups", "batch"), "tensor")
    return jax.shard_map(
        on_device, mesh=mesh, in_specs=in_specs, out_specs=out_specs, check_vma=False
    )
```

```python
import functools

import jax
import jax.numpy as jnp
from jax import lax
from jax.experimental import pallas as pl
from jax.experimental.pallas import tpu as pltpu
from jax.sharding import PartitionSpec as P

adapter_scale = 0.5
VMEM_BYTES = 24 * 1024 * 1024
WIDE = pltpu.CompilerParams(vmem_limit_bytes=60 * 1024 * 1024)
VMEM = pl.BlockSpec(memory_space=pltpu.VMEM)
ANY = pl.BlockSpec(memory_space=pl.ANY)
HBM = pl.BlockSpec(memory_space=pltpu.HBM)
SMEM = pl.BlockSpec(memory_space=pltpu.SMEM)
COST = pl.CostEstimate(flops=1, bytes_accessed=1, transcendentals=0)
PARAMS = pltpu.CompilerParams(vmem_limit_bytes=VMEM_BYTES)


def place_rows(index, start, tokens_ref, block_ref):
    local = lax.broadcasted_iota(jnp.int32, (block_ref.shape[0], index.shape[1]), 0)
    choose = (local + start == index).astype(jnp.bfloat16)
    block_ref[...] = jnp.dot(
        choose, tokens_ref[...], preferred_element_type=jnp.float32
    ).astype(jnp.bfloat16)


def route_kernel(
    homes, held, light, place_ref, entry_hbm, request_hbm, index_ref, heavy_ref, entry_ref, request_ref, sems
):
    loads = [
        pltpu.make_async_copy(source, target, sems.at[n])
        for n, (source, target) in enumerate(
            [(request_hbm, request_ref), (entry_hbm, entry_ref)]
        )
    ]
    for load in loads:
        load.start()
    rows = request_ref.shape[0]
    adapters = entry_ref.shape[0]
    span = (held + 1) * light
    earlier = (
        lax.broadcasted_iota(jnp.int32, (rows, rows), 0) < lax.broadcasted_iota(jnp.int32, (rows, rows), 1)
    ).astype(jnp.bfloat16)
    loads[0].wait()
    request = request_ref[...].reshape(1, rows)
    onehot = lax.broadcasted_iota(jnp.int32, (adapters, rows), 0) == request
    before = jnp.dot(onehot.astype(jnp.bfloat16), earlier, preferred_element_type=jnp.float32)
    position = jnp.sum(jnp.where(onehot, before, 0.0), axis=0, keepdims=True).astype(jnp.int32)
    loads[1].wait()
    slot = jnp.zeros_like(position)
    for a in range(adapters):
        slot = jnp.where(request == a, entry_ref[a], slot)
    home = slot // held
    relative = lax.rem(home - place_ref[0] + homes, homes)
    inside = jnp.where(
        position < light, (slot - home * held) * light + position, held * light + position - light
    )
    index = relative * span + inside
    index_ref[...] = index
    heavy = jnp.max(jnp.where(position >= light, slot, 0), axis=1, keepdims=True)
    heavy_ref[...] = jnp.broadcast_to(heavy, heavy_ref.shape)


def pack_kernel(span, shifts, waited, index_ref, tokens_ref, *refs):
    mark_ref, *refs = refs[waited:]
    count = len(shifts)
    block_refs, buffer, sems = refs[:count], refs[count], refs[count + 1]
    mark_ref[...] = jnp.zeros_like(mark_ref)
    stores = []
    for n, shift in enumerate(shifts):
        place_rows(index_ref[...], shift * span, tokens_ref, buffer.at[n])
        stores.append(pltpu.make_async_copy(buffer.at[n], block_refs[n], sems.at[n]))
        stores[-1].start()
    for store in stores:
        store.wait()


def entry_places(held):
    return (held + 2) // 2


def shrink_kernel(held, light, rank, value_side, count, waited, passed, scalar_ref, *refs):
    block_refs, down_ref, refs = refs[:count], refs[count], refs[count + 1 + waited :]
    passed_refs, out_ref, left_refs = refs[:passed], refs[passed], refs[passed + 1 :]
    groups = entry_places(held)
    height = groups * light

    def product(e):
        if e > held:
            return jnp.zeros((count * light, 2 * rank), jnp.float32)
        factor = down_ref[e] if e < held else down_ref[scalar_ref[1]]
        rows = [block_ref[e * light : (e + 1) * light, :] for block_ref in block_refs]
        value = jnp.dot(
            jnp.concatenate(rows, axis=0) if count > 1 else rows[0], factor, preferred_element_type=jnp.float32
        )
        return value if e < held else jnp.where(scalar_ref[2] == 1, value, 0.0)

    on_value_side = scalar_ref[0] >= value_side
    for g in range(groups):
        first, second = product(g), product(g + groups)
        key = jnp.concatenate([first[:, :rank], second[:, :rank]], axis=1)
        value = jnp.concatenate([first[:, rank:], second[:, rank:]], axis=1)
        mine, other = jnp.where(on_value_side, value, key), jnp.where(on_value_side, key, value)
        for n in range(count):
            here, start = slice(n * light, (n + 1) * light), n * height + g * light
            out_ref[start : start + light, :] = mine[here]
            out_ref[count * height + start : count * height + start + light, :] = other[here]
    for source, target in zip(passed_refs, left_refs):
        target[...] = source[...]


def hold_kernel(value_ref, *refs):
    refs[-1][...] = value_ref[...]


def split_pair(value):
    high = value.astype(jnp.bfloat16)
    low = (value - high.astype(jnp.float32)).astype(jnp.bfloat16)
    return high, low


def finish_kernel(homes, held, light, rank, shifts, waited, place_ref, index_ref, base_ref, up_ref, *refs):
    count = len(shifts)
    refs = refs[:count] + refs[count + waited :]
    shrink_refs, out_ref, high_ref, low_ref = refs[:count], refs[count], refs[count + 1], refs[count + 2]
    span = (held + 1) * light
    rows = base_ref.shape[0]
    groups = entry_places(held)
    local = []
    for n, r in enumerate(shifts):
        for e in range(held + 1):
            entry = r * held + e if e < held else place_ref[0]
            g, side = e % groups, e // groups
            high, low = split_pair(
                shrink_refs[n][g * light : (g + 1) * light, side * rank : (side + 1) * rank]
            )
            factor = up_ref[entry]
            delta = jnp.dot(high, factor, preferred_element_type=jnp.float32) + jnp.dot(
                low, factor, preferred_element_type=jnp.float32
            )
            high, low = split_pair(delta)
            start = n * span + e * light
            high_ref[start : start + light, :] = high
            low_ref[start : start + light, :] = low
        local.append(lax.broadcasted_iota(jnp.int32, (rows, span), 1) + r * span == index_ref[...])
    delta = base_ref[...]
    for n in range(count):
        choose = local[n].astype(jnp.bfloat16)
        delta = delta + adapter_scale * (
            jnp.dot(choose, high_ref[n * span : (n + 1) * span, :], preferred_element_type=jnp.float32)
            + jnp.dot(choose, low_ref[n * span : (n + 1) * span, :], preferred_element_type=jnp.float32)
        )
    out_ref[...] = delta.astype(out_ref.dtype)


def finish(scalars, index, base, up, shrinks, after, shifts, dtype, homes, held, light):
    rows, columns = base.shape
    span = (held + 1) * light
    return pl.pallas_call(
        functools.partial(finish_kernel, homes, held, light, up.shape[1], shifts, len(after)),
        out_shape=jax.ShapeDtypeStruct((rows, columns), dtype),
        in_specs=[SMEM] + [VMEM] * (3 + len(shifts)) + [ANY] * len(after),
        out_specs=VMEM,
        scratch_shapes=[pltpu.VMEM((len(shifts) * span, columns), jnp.bfloat16)] * 2,
        compiler_params=PARAMS,
        cost_estimate=COST,
        name="finish",
    )(scalars, index, base, up, *shrinks, *after)


def gate_kernel(waiting, *refs):
    refs[waiting][...] = jnp.zeros_like(refs[waiting])


def gate(blocks, after):
    return pl.pallas_call(
        functools.partial(gate_kernel, len(blocks) + len(after)),
        out_shape=[jax.ShapeDtypeStruct((8, 128), jnp.int32)]
        + [jax.ShapeDtypeStruct(b.shape, b.dtype) for b in blocks],
        in_specs=[HBM] * len(blocks) + [ANY] * len(after),
        out_specs=[VMEM] + [HBM] * len(blocks),
        input_output_aliases={n: n + 1 for n in range(len(blocks))},
        compiler_params=WIDE,
        cost_estimate=COST,
        name="gate",
    )(*blocks, *after)


def gather_up(adapter_up, homes):
    teams = lax.axis_size("groups")
    team = lax.axis_index("groups")
    share = adapter_up.shape[1] // teams
    own = lax.dynamic_slice_in_dim(adapter_up, team * share, share, 1)
    found = [
        lax.ppermute(own, "batch", [(i, (i - r) % homes) for i in range(homes)]) for r in range(1, homes)
    ]
    ordered = jnp.concatenate([own] + found, axis=0)
    shares = [ordered] + [
        lax.ppermute(ordered, "groups", [(i, (i + s) % teams) for i in range(teams)])
        for s in range(1, teams)
    ]
    return jnp.concatenate(
        [
            functools.reduce(
                lambda kept, s: jnp.where(lax.rem(team + teams - s, teams) == part, shares[s], kept),
                range(1, teams),
                shares[0],
            )
            for part in range(teams)
        ],
        axis=1,
    ), found


def base_kernel(waited, block_ref, tokens_ref, weight_ref, *refs):
    refs[waited][...] = jnp.dot(tokens_ref[...], weight_ref[...], preferred_element_type=jnp.float32)


def base_part(tokens, weight, blocks, columns, slab, slabs, after, params=PARAMS):
    rows, width = tokens.shape[0] // slabs, tokens.shape[1]
    count = blocks.shape[0]
    return pl.pallas_call(
        functools.partial(base_kernel, len(after)),
        out_shape=jax.ShapeDtypeStruct((rows, count * columns), jnp.float32),
        grid_spec=pltpu.PrefetchScalarGridSpec(
            num_scalar_prefetch=1,
            grid=(count,),
            in_specs=[
                pl.BlockSpec((rows, width), lambda j, chosen: (slab, 0)),
                pl.BlockSpec((width, columns), lambda j, chosen: (0, chosen[j])),
            ]
            + [ANY] * len(after),
            out_specs=pl.BlockSpec((rows, columns), lambda j, chosen: (0, j)),
        ),
        compiler_params=params,
        cost_estimate=COST,
        name="base",
    )(blocks, tokens, weight, *after)


def reduce_base(tokens, weight, piece, pieces, columns, slab, slabs, after):
    keep = [0]
    bit = pieces // 2
    while bit > 1:
        keep = keep + [p + bit for p in keep]
        bit //= 2
    keep = jnp.array(keep, jnp.int32)
    sent = base_part(
        tokens, weight, piece ^ keep ^ 1, columns, slab, slabs, after, PARAMS if slab else WIDE
    )
    kept = base_part(tokens, weight, piece ^ keep, columns, slab, slabs, [sent])
    bit, first = 1, None
    while True:
        kept = kept + lax.ppermute(sent, "tensor", [(i, i ^ bit) for i in range(pieces)])
        first = kept[:8] if first is None else first
        bit *= 2
        if bit >= pieces:
            return kept, first
        half = kept.shape[1] // 2
        kept, sent = kept[:, :half], kept[:, half:]


def on_device(tokens, request_adapter, adapter_entry, key_value_weight, adapter_down, adapter_up):
    rows, width = tokens.shape
    adapters = adapter_entry.shape[0]
    held, rank, columns = adapter_up.shape
    value_side = key_value_weight.shape[1] // 2 // columns
    homes = lax.axis_size("batch")
    pieces = lax.axis_size("tensor")
    place = lax.axis_index("batch").astype(jnp.int32)
    piece = lax.axis_index("tensor").astype(jnp.int32)
    light = rows // adapters
    span = (held + 1) * light
    order = sorted(range(1, homes), key=lambda r: (-min(r, homes - r), r))
    block_shape = jax.ShapeDtypeStruct((span, width), jnp.bfloat16)

    up, found = gather_up(adapter_up, homes)
    index, heavy = pl.pallas_call(
        functools.partial(route_kernel, homes, held, light),
        out_shape=[
            jax.ShapeDtypeStruct((1, rows), jnp.int32),
            jax.ShapeDtypeStruct((8, 128), jnp.int32),
        ],
        in_specs=[SMEM, HBM, HBM],
        out_specs=[VMEM] * 2,
        scratch_shapes=[
            pltpu.SMEM(adapter_entry.shape, jnp.int32),
            pltpu.VMEM((rows,), jnp.int32),
            pltpu.SemaphoreType.DMA((2,)),
        ],
        compiler_params=WIDE,
        cost_estimate=COST,
        name="route",
    )(place.reshape(1), adapter_entry, request_adapter)
    def pack(shifts, after):
        return pl.pallas_call(
            functools.partial(pack_kernel, span, shifts, len(after)),
            out_shape=[jax.ShapeDtypeStruct((8, 128), jnp.int32)] + [block_shape] * len(shifts),
            in_specs=[VMEM] * 2 + [ANY] * len(after),
            out_specs=[VMEM] + [HBM] * len(shifts),
            scratch_shapes=[
                pltpu.VMEM((len(shifts), span, width), jnp.bfloat16),
                pltpu.SemaphoreType.DMA((len(shifts),)),
            ],
            compiler_params=WIDE,
            cost_estimate=COST,
            name="pack",
        )(index, tokens, *after)

    def send(block, r):
        return lax.ppermute(block, "batch", [(i, (i + r) % homes) for i in range(homes)])

    packed, *blocks = pack(order, [])
    mark, *blocks = gate(blocks, found)
    _, own_block = pack([0], [mark])
    arrived = {0: own_block}
    for r, block in zip(order, blocks):
        arrived[r] = send(block, r)

    heavy = heavy[0, 0]
    heavy_here = (heavy // held == place).astype(jnp.int32)
    scalars = jnp.stack([piece, lax.rem(heavy, held), heavy_here])
    height = entry_places(held) * light

    def shrink(blocks, after, passed):
        return pl.pallas_call(
            functools.partial(
                shrink_kernel, held, light, rank, value_side, len(blocks), len(after), len(passed)
            ),
            out_shape=[jax.ShapeDtypeStruct((2 * len(blocks) * height, 2 * rank), jnp.float32)]
            + [jax.ShapeDtypeStruct(p.shape, p.dtype) for p in passed],
            in_specs=[SMEM] + [VMEM] * (len(blocks) + 1) + [ANY] * len(after) + [VMEM] * len(passed),
            out_specs=[VMEM] * (1 + len(passed)),
            compiler_params=PARAMS,
            cost_estimate=COST,
            name="shrink",
        )(scalars, *blocks, adapter_down, *after, *passed)

    def hold(value, after):
        return pl.pallas_call(
            hold_kernel,
            out_shape=jax.ShapeDtypeStruct(value.shape, value.dtype),
            in_specs=[VMEM] + [ANY] * len(after),
            out_specs=VMEM,
            compiler_params=PARAMS,
            cost_estimate=COST,
            name="hold",
        )(value, *after)

    def combine(value, after=()):
        bit, half = 1, value.shape[0] // 2
        while bit < pieces // 2:
            value = value + lax.ppermute(value, "tensor", [(i, i ^ bit) for i in range(pieces)])
            bit *= 2
        if after:
            value = hold(value, after)
        return value[:half] + lax.ppermute(value[half:], "tensor", [(i, i ^ bit) for i in range(pieces)])

    slabs = 3
    slab_sums = [
        reduce_base(tokens, key_value_weight, piece, pieces, columns, slab, slabs, [mark])
        for slab in range(slabs)
    ]
    base = jnp.concatenate([total for total, _ in slab_sums], axis=0)
    begun = [first for _, first in slab_sums]
    whole = [total[:8] for total, _ in slab_sums[:1]]
    late = order[-2:]
    early = order[:-2] + [0]
    totals, far = [], [packed]
    for r in early:
        (value,) = shrink([arrived[r]], begun if r else far, [])
        far = [value]
        totals.append(combine(value, whole if r else ()))
    value, *totals = shrink([arrived[r] for r in late], [base[:8], base[-8:]], totals)
    last = combine(value)

    def give_back(total, r):
        return lax.ppermute(total, "batch", [(i, (i - r) % homes) for i in range(homes)]) if r else total

    shrinks = [give_back(total, r) for total, r in zip(totals, early)]
    places = lax.rem(heavy - place * held + adapters, adapters).reshape(1)
    column = index.reshape(rows, 1)
    running = finish(places, column, base, up, shrinks, [last], early, jnp.float32, homes, held, light)
    shrinks = [give_back(last[n * height : (n + 1) * height], r) for n, r in enumerate(late)]
    return finish(places, column, running, up, shrinks, [], late, jnp.bfloat16, homes, held, light)


def solution(mesh):
    in_specs = (
        P(("groups", "batch"), "tensor"),
        P(("groups", "batch")),
        P(),
        P("tensor", None),
        P("batch", "tensor", None),
        P("batch", None, "tensor"),
    )
    out_specs = P(("groups", "batch"), "tensor")
    return jax.shard_map(
        on_device, mesh=mesh, in_specs=in_specs, out_specs=out_specs, check_vma=False
    )
```
